256 devices in a mesh: section: 2 (over y_hi), seq: 32 (over y_lo, z, core), tensor: 4 (over x).
Axes of the slice: x: 4, y: 4 (y_hi: 2, y_lo: 2; y = y_hi * 2 + y_lo), z: 8, core: 2. Of those that a mesh axis runs over, the one named last changes fastest.
Arguments:
- token_ids: int32 [2, 4352], P(None, 'seq'), may hold values from 0 to 511
- embed_table: bfloat16 [512, 4096], P(None, 'tensor')
- norm_gain: float32 [2, 4096], P('section'), may hold values from 0.1 to 1.9
- in_weight: bfloat16 [2, 4096, 3, 4096], P('section', 'seq', None, 'tensor'), may hold values from -0.09375 to 0.09375
- se_filter: float32 [2, 3, 7, 4096], P('section', None, None, 'tensor'), may hold values from -2.4 to 2.4
- mr_filter: float32 [2, 128, 4096], P('section', None, 'tensor'), may hold values from -0.54 to 0.54
- out_weight: bfloat16 [2, 4096, 4096], P('section', 'tensor')
Outputs:
- section_out: bfloat16 [2, 2, 4352, 4096], P('section', None, 'seq', 'tensor')
The draws below stay inside these ranges and needn't reach their ends.
All inputs are finite; a program needn't handle non-finite values.
Results may differ from the reference program's by a relative error of at most 0.025.
Values may be sent and summed in bfloat16 or wider, within the bound.
A program may use at most 192 MiB of HBM per device.

```python
import math
import jax
import jax.numpy as jnp
import numpy as np
from jax import lax

D = 4096
VOCAB = 512
SE_TAPS = 7
MR_TAPS = 128
MICRO = 2
TOKENS = 4352
N_SECTION = 2
N_TENSOR = 4


def spread_scale(key, shape, low, high):
    return jnp.exp(jax.random.uniform(key, shape, jnp.float32, math.log(low), math.log(high)))


def rising(count):
    return jnp.exp(math.log(3.0) * jnp.arange(count).astype(jnp.float32) / count)


def draw_embed_table(key, part):
    key = jax.random.fold_in(key, 11)
    first, second, third = jax.random.split(key, 3)
    row_scale = spread_scale(first, (VOCAB, 1), 0.3, 3.0)
    col_scale = spread_scale(second, (1, D), 0.3, 3.0) * rising(D)[None, :]
    entries = jax.random.normal(third, (VOCAB, D), jnp.float32)
    return (entries * row_scale * col_scale).astype(jnp.bfloat16)


def draw_out_weight(key, part):
    key = jax.random.fold_in(key, 23)
    first, second = jax.random.split(key, 2)
    col_scale = spread_scale(first, (N_SECTION, 1, D), 0.3, 3.0) * rising(D)[None, None, :]
    entries = jax.random.normal(second, (N_SECTION, D, D), jnp.float32)
    return (entries * col_scale / math.sqrt(D)).astype(jnp.bfloat16)


def with_ends(result, stream_key, low, largest):
    longest = result.shape.index(max(result.shape))
    spots = []
    for shift in (0, 1):
        where = [jax.random.randint(jax.random.fold_in(stream_key, axis), (), 0, length) for axis, length in enumerate(result.shape)]
        where[longest] = (where[longest] + shift) % result.shape[longest]
        spots.append(tuple(where))
    return result.at[spots[0]].set(low).at[spots[1]].set(largest)


def levels(rng, dims, shards, least, top_value):
    level, own = 1.0, jax.random.fold_in(rng, 6)
    for axis_at, shards_of in shards:
        heights = jnp.exp(jax.random.uniform(jax.random.fold_in(own, axis_at), (shards_of,), jnp.float32, least / len(shards), top_value / len(shards)))
        level = level * jnp.repeat(heights, dims[axis_at] // shards_of).reshape([-1 if axis == axis_at else 1 for axis in range(len(dims))])
    return level


def cumulative_ranks(number_of, slope):
    loads = [(1 << 20) // math.isqrt(standing ** slope) + 1 for standing in range(1, number_of + 1)]
    width = 1 + sum(loads) // (1 << 30)
    return np.cumsum(np.array([max(1, weight // width) for weight in loads]))


def ranked(rng, extent, amount, slope):
    listing = cumulative_ranks(amount, slope)
    pick = jax.random.randint(jax.random.fold_in(rng, 1), extent, 0, int(listing[amount - 1]))
    rank = jnp.searchsorted(jnp.asarray(listing, jnp.int32), pick, side="right")
    return jax.random.permutation(jax.random.fold_in(rng, 2), amount)[rank].astype(jnp.int32)


def scatter_about(key, shape, spread, limit, shards=(), held_as=jnp.bfloat16):
    result = spread * jax.random.normal(key, shape, jnp.float32)
    if shards:
        result = result * levels(key, shape, shards, -0.22, 0.18)
    return jnp.clip(result, -limit, limit).astype(held_as)


def setup_inputs(seed: int = 0) -> dict:
    streams_of = jax.random.split(jax.random.key(seed), 8)
    return {
        "token_ids": with_ends(ranked(streams_of[0], (MICRO, TOKENS), VOCAB, 2), jax.random.fold_in(streams_of[0], 3), 0, VOCAB - 1).astype(jnp.int32),
        "embed_table": draw_embed_table(jax.random.fold_in(streams_of[7], 71), 0),
        "norm_gain": jnp.clip(1.0 + 0.18 * jax.random.normal(streams_of[2], (N_SECTION, D), jnp.float32), 0.1, 1.9),
        "in_weight": scatter_about(streams_of[3], (N_SECTION, D, 3, D), D ** -0.5, 0.09375, ((0, 2), (1, 32), (3, 4))),
        "se_filter": scatter_about(streams_of[4], (N_SECTION, 3, SE_TAPS, D), 0.4, 2.4, ((0, 2), (3, 4)), jnp.float32),
        "mr_filter": scatter_about(streams_of[5], (N_SECTION, MR_TAPS, D), 0.09, 0.54, ((0, 2), (2, 4)), jnp.float32),
        "out_weight": draw_out_weight(jax.random.fold_in(streams_of[7], 71), 0),
    }


EPS = 1e-06

def causal_sum(values, filt):
    taps = filt.shape[0]
    padded = jnp.concatenate([jnp.zeros((taps - 1, values.shape[1]), values.dtype), values], axis=0)
    length = values.shape[0]

    def add_tap(j, total):
        begin = (taps - 1 - j).astype(jnp.int32)
        piece = lax.dynamic_slice_in_dim(padded, begin, length, 0)
        coeff = lax.dynamic_index_in_dim(filt, j.astype(jnp.int32), 0, keepdims=False)
        return total + coeff[None, :] * piece
    return lax.fori_loop(0, taps, add_tap, jnp.zeros_like(values))

def mixer_layer(stream, gain, in_proj, se_taps, mr_taps, weight):
    values = stream.astype(jnp.float32)
    scale = lax.rsqrt(lax.optimization_barrier(jnp.mean(values * values, axis=1)) + EPS)
    normed = (values * scale[:, None] * gain[None, :]).astype(jnp.bfloat16)
    length = normed.shape[0]
    streams = jnp.dot(normed, in_proj.reshape(D, 3 * D), preferred_element_type=jnp.float32)
    streams = streams.astype(jnp.bfloat16).reshape(length, 3, D).astype(jnp.float32)
    query = causal_sum(streams[:, 0, :], se_taps[0])
    keys = causal_sum(streams[:, 1, :], se_taps[1])
    vals = causal_sum(streams[:, 2, :], se_taps[2])
    gated = (keys * vals).astype(jnp.bfloat16)
    medium = causal_sum(gated.astype(jnp.float32), mr_taps)
    mixed = (query * medium).astype(jnp.bfloat16)
    share = D // N_TENSOR
    projected = jnp.zeros((length, D), jnp.float32)
    for group in range(N_TENSOR):
        term = jnp.dot(mixed[:, group * share:(group + 1) * share], weight[group * share:(group + 1) * share], preferred_element_type=jnp.float32)
        projected = projected + term.astype(jnp.bfloat16).astype(jnp.float32)
    return (values + projected).astype(jnp.bfloat16)

def reference(token_ids, embed_table, norm_gain, in_weight, se_filter, mr_filter, out_weight):
    per_section = [[] for _ in range(N_SECTION)]
    for turn in range(MICRO):
        ids = token_ids[turn]
        stream = jnp.take(embed_table, ids, axis=0)
        for section in range(N_SECTION):
            stream = mixer_layer(stream, norm_gain[section], in_weight[section], se_filter[section], mr_filter[section], out_weight[section])
            per_section[section].append(stream)
    return jnp.stack([jnp.stack(items) for items in per_section])
```

```python
import functools

import jax
import jax.numpy as jnp
from jax import lax
from jax.experimental import pallas as pl
from jax.experimental.pallas import tpu as pltpu
from jax.sharding import PartitionSpec as P

EPS = 1e-06
MESH = pl.DeviceIdType.MESH
RING = 8
VMEM = pl.BlockSpec(memory_space=pltpu.VMEM)
HBM = pl.BlockSpec(memory_space=pltpu.HBM)


def place():
    seq = lax.axis_index("seq")
    return seq // (2 * RING), (seq // 2) % RING, seq % 2


def seq_of(y, z, core):
    return (y * RING + z) * 2 + core


class Gather:
    MOVES = (
        ("a1", "up", True, 0, None),
        ("b1", "down", True, 0, None),
        ("c1", "y", True, 0, None),
        ("a2", "up", True, -1, None),
        ("b2", "down", True, 1, None),
        ("a3", "up", True, -2, None),
        ("b3", "down", True, 2, None),
        ("c2", "y", True, -2, 1),
        ("c3", "y", True, 2, 0),
        ("a4", "up", True, -3, 0),
        ("b4", "down", True, 3, 1),
        ("a5", "up", False, 0, None),
        ("b5", "down", False, 0, None),
        ("c4", "y", True, -3, None),
        ("c5", "y", True, 3, None),
        ("a6", "up", False, -1, 0),
        ("b6", "down", False, 1, 1),
        ("c6", "y", True, 4, 0),
        ("c7", "y", True, 4, 1),
    )
    COUNT = len(MOVES)

    def __init__(self, slot, own, send, recv, side_send, side_recv):
        self.y, self.z, self.core = place()
        self.slot, self.own = slot, own
        self.send, self.recv = send, recv
        self.side_send, self.side_recv = side_send, side_recv
        self.index = {move[0]: at for at, move in enumerate(self.MOVES)}
        self.pending = []

    def target(self, direction):
        if direction == "up":
            return seq_of(self.y, (self.z + 1) % RING, self.core)
        if direction == "down":
            return seq_of(self.y, (self.z + RING - 1) % RING, self.core)
        return seq_of(1 - self.y, self.z, self.core)

    def block(self, same, dz, core=None):
        y = self.y if same else 1 - self.y
        return seq_of(y, (self.z + dz + RING) % RING, self.core if core is None else core)

    def copy(self, name):
        at = self.index[name]
        _, direction, same, dz, half = self.MOVES[at]
        block = self.block(same, dz)
        dst = self.slot(block, half)
        src = self.own if same and dz == 0 else dst
        return pltpu.make_async_remote_copy(
            src_ref=src,
            dst_ref=dst,
            send_sem=self.send.at[at],
            recv_sem=self.recv.at[at],
            device_id={"seq": self.target(direction)},
            device_id_type=MESH,
        )

    def start(self, *names):
        for name in names:
            self.copy(name).start()

    def landed(self, name):
        at = self.index[name]
        _, direction, same, dz, half = self.MOVES[at]
        if direction == "y":
            block = self.block(not same, dz)
        else:
            block = self.block(same, dz + (-1 if direction == "up" else 1))
        got = self.slot(block, half)
        pltpu.make_async_copy(got, got, self.recv.at[at]).wait()
        side = pltpu.make_async_remote_copy(
            src_ref=got,
            dst_ref=got,
            send_sem=self.side_send.at[at],
            recv_sem=self.side_recv.at[at],
            device_id={"seq": seq_of(self.y, self.z, 1 - self.core)},
            device_id_type=MESH,
        )
        side.start()

    def side_own(self):
        return pltpu.make_async_remote_copy(
            src_ref=self.own,
            dst_ref=self.slot(self.block(True, 0), None),
            send_sem=self.side_send.at[self.COUNT],
            recv_sem=self.side_recv.at[self.COUNT],
            device_id={"seq": seq_of(self.y, self.z, 1 - self.core)},
            device_id_type=MESH,
        )

    def run(self, local_sem):
        keep = pltpu.make_async_copy(self.own, self.slot(self.block(True, 0), None), local_sem)
        self.start("a1", "b1", "c1")
        self.side_own().start()
        keep.start()
        self.landed("a1")
        self.start("a2")
        self.landed("b1")
        self.start("b2")
        self.landed("c1")
        self.landed("a2")
        self.start("a3", "c2")
        self.landed("b2")
        self.start("b3", "c3")
        self.start("a5", "b5")
        self.landed("a3")
        self.start("a4", "c4")
        self.landed("b3")
        self.start("b4", "c5")
        self.landed("a5")
        self.start("a6")
        self.landed("b5")
        self.start("b6")
        self.landed("a4")
        self.start("c6")
        self.landed("b4")
        self.start("c7")
        for name in ("c2", "c3", "a6", "b6", "c4", "c5", "c6", "c7"):
            self.landed(name)
        keep.wait()
        for at, (name, direction, same, dz, half) in enumerate(self.MOVES):
            self.copy(name).wait_send()
            if direction == "y":
                block = (not same, dz)
            else:
                block = (same, dz + (-1 if direction == "up" else 1))
            mine = self.slot(self.block(*block), half)
            pltpu.make_async_copy(mine, mine, self.side_send.at[at]).wait()
            other = self.slot(self.block(*block, 1 - self.core), half)
            pltpu.make_async_copy(other, other, self.side_recv.at[at]).wait()
        side = self.side_own()
        side.wait_send()
        other = self.slot(self.block(True, 0, 1 - self.core), None)
        pltpu.make_async_copy(other, other, self.side_recv.at[self.COUNT]).wait()


def first_kernel(
    tail, shard, table, gain, t_full, w_full, tail_all, part, tables,
    send, recv, side_send, side_recv, a2a_send, a2a_recv, x_send, x_recv, local,
):
    section = lax.axis_index("section")
    tensor = lax.axis_index("tensor")
    seq = lax.axis_index("seq")
    y, z, core = place()
    count = tail.shape[0]
    share, depth = tail.shape[1], tail.shape[2]
    vocab, width = table.shape
    half = vocab // 2
    ways = tables.shape[0]
    barrier = pltpu.get_barrier_semaphore()

    def greet(**axes):
        pl.semaphore_signal(barrier, inc=1, device_id=axes, device_id_type=MESH)

    @pl.when(section == 1)
    def _():
        greet(seq=seq_of(y, (z + 1) % RING, core))
        greet(seq=seq_of(y, (z + RING - 1) % RING, core))
        greet(seq=seq_of(1 - y, z, core))
        greet(seq=seq_of(y, z, 1 - core))
        pl.semaphore_wait(barrier, 4)

        def slot(block, part_of):
            if part_of is None:
                return w_full.at[pl.ds(pl.multiple_of(block * depth, depth), depth)]
            rows = depth // 2
            return w_full.at[pl.ds(pl.multiple_of(block * depth + part_of * rows, rows), rows)]

        Gather(slot, shard, send, recv, side_send, side_recv).run(local.at[0])

    @pl.when(section == 0)
    def _():
        right, left = (tensor + 1) % ways, (tensor + ways - 1) % ways
        greet(tensor=right)
        greet(tensor=left)

        def greet_seq(step, carry):
            greet(seq=(seq + step) % count)
            return carry

        lax.fori_loop(1, count, greet_seq, 0)
        pl.semaphore_wait(barrier, count + 1)

        rows = pl.ds(pl.multiple_of(core * half, half), half)

        def along(at, src, owner, to):
            return pltpu.make_async_remote_copy(
                src_ref=src,
                dst_ref=tables.at[owner, rows],
                send_sem=x_send.at[at],
                recv_sem=x_recv.at[at],
                device_id={"tensor": to},
                device_id_type=MESH,
            )

        def across(at, owner):
            return pltpu.make_async_remote_copy(
                src_ref=tables.at[owner, rows],
                dst_ref=tables.at[owner, rows],
                send_sem=x_send.at[at],
                recv_sem=x_recv.at[at],
                device_id={"seq": seq_of(y, z, 1 - core)},
                device_id_type=MESH,
            )

        mine = table.at[rows]
        along(0, mine, tensor, right).start()
        along(1, mine, tensor, left).start()
        keep = pltpu.make_async_copy(table, tables.at[tensor], local.at[0])
        keep.start()

        def spread(step):
            to = (seq + step) % count
            return pltpu.make_async_remote_copy(
                src_ref=tail.at[to],
                dst_ref=tail_all.at[:, pl.ds(pl.multiple_of(seq * depth, depth), depth)],
                send_sem=a2a_send.at[step],
                recv_sem=a2a_recv.at[step],
                device_id={"seq": to},
                device_id_type=MESH,
            )

        def spread_start(step, carry):
            spread(step).start()
            return carry

        lax.fori_loop(1, count, spread_start, 0)
        keep_tail = pltpu.make_async_copy(
            tail.at[seq],
            tail_all.at[:, pl.ds(pl.multiple_of(seq * depth, depth), depth)],
            local.at[1],
        )
        keep_tail.start()

        far = (tensor + 2) % ways
        along(0, mine, tensor, right).wait_recv()
        across(3, left).start()
        along(1, mine, tensor, left).wait_recv()
        across(4, right).start()

        @pl.when(core == 0)
        def _():
            along(2, tables.at[left, rows], left, right).start()

        @pl.when(core == 1)
        def _():
            along(2, tables.at[right, rows], right, left).start()

        got = tables.at[far, rows]
        pltpu.make_async_copy(got, got, x_recv.at[2]).wait()
        across(5, far).start()
        keep.wait()
        for at, owner in ((3, left), (4, right), (5, far)):
            across(at, owner).wait_recv()
        along(0, mine, tensor, right).wait_send()
        along(1, mine, tensor, left).wait_send()
        pltpu.make_async_copy(got, got, x_send.at[2]).wait()
        for at, owner in ((3, left), (4, right), (5, far)):
            across(at, owner).wait_send()

        lines = 32

        def normalise(at, carry):
            window = pl.ds(pl.multiple_of(at * lines, lines), lines)
            total = jnp.zeros((lines, 1), jnp.float32)
            for way in range(ways):
                values = tables[way, window, :].astype(jnp.float32)
                total += jnp.sum(values * values, axis=1, keepdims=True)
            scale = lax.rsqrt(total / (ways * width) + EPS)
            for way in range(ways):
                values = tables[way, window, :].astype(jnp.float32)
                values = values * scale * gain[:, way * width : (way + 1) * width]
                tables[way, window, :] = values.astype(jnp.bfloat16)
            return carry

        lax.fori_loop(0, vocab // lines, normalise, 0)

        def spread_wait(step, carry):
            spread(step).wait_send()
            piece = tail_all.at[:, pl.ds(0, depth)]
            pltpu.make_async_copy(piece, piece, a2a_recv.at[step]).wait()
            return carry

        lax.fori_loop(1, count, spread_wait, 0)
        keep_tail.wait()
        total = jnp.zeros((share, vocab), jnp.float32)
        for way in range(ways):
            total += lax.dot_general(
                tail_all[:, way * width : (way + 1) * width],
                tables[way],
                (((1,), (1,)), ((), ())),
                preferred_element_type=jnp.float32,
            )
        wide = part.shape[1]
        for stream in range(3):
            part[stream] = total[stream * wide : (stream + 1) * wide].astype(jnp.bfloat16)

        def slot(block, part_of):
            if part_of is None:
                return t_full.at[:, pl.ds(pl.multiple_of(block * wide, wide), wide)]
            rows_of = wide // 2
            at = pl.multiple_of(block * wide + part_of * rows_of, rows_of)
            return t_full.at[:, pl.ds(at, rows_of)]

        Gather(slot, part, send, recv, side_send, side_recv).run(local.at[0])


def prepare(tail, shard, table, gain):
    count, share, depth = tail.shape
    vocab, width = table.shape
    full = gain.shape[1]
    moves = Gather.COUNT
    dma = pltpu.SemaphoreType.DMA
    return pl.pallas_call(
        first_kernel,
        out_shape=(
            jax.ShapeDtypeStruct((3, width, vocab), jnp.bfloat16),
            jax.ShapeDtypeStruct((full, 3 * width), jnp.bfloat16),
        ),
        in_specs=[VMEM, HBM, VMEM, VMEM],
        out_specs=(HBM, HBM),
        scratch_shapes=[
            pltpu.VMEM((share, full), jnp.bfloat16),
            pltpu.VMEM((3, share // 3, vocab), jnp.bfloat16),
            pltpu.VMEM((full // width, vocab, width), jnp.bfloat16),
            dma((moves,)),
            dma((moves,)),
            dma((moves + 1,)),
            dma((moves + 1,)),
            dma((count,)),
            dma((count,)),
            dma((6,)),
            dma((6,)),
            dma((2,)),
        ],
        compiler_params=pltpu.CompilerParams(
            collective_id=0, has_side_effects=True, vmem_limit_bytes=24 << 20
        ),
        name="prepare",
    )(tail, shard, table, gain)


def passed_along(value, axis, steps):
    count = lax.axis_size(axis)
    initial, last = (max(0, -steps), min(count, count - steps))
    return lax.ppermute(value, axis, [(source, source + steps) for source in range(initial, last)])


def causal_sum(extended, coeffs, length):
    taps = coeffs.shape[0]
    total = jnp.zeros((extended.shape[0], length) + extended.shape[2:], jnp.float32)
    for tap in range(taps):
        begin = taps - 1 - tap
        total = total + coeffs[tap][None, None] * extended[:, begin : begin + length]
    return total


def body(token_ids, embed_table, norm_gain, in_weight, se_filter, mr_filter, out_weight):
    micro, length = token_ids.shape
    vocab, width = embed_table.shape
    full = norm_gain.shape[1]
    section = lax.axis_index("section")
    seq = lax.axis_index("seq")
    gain = norm_gain[0]
    short_coeffs = jnp.transpose(se_filter[0], (1, 0, 2))
    medium_taps = mr_filter[0]
    weight = out_weight[0]
    se = short_coeffs.shape[0] - 1
    mr = medium_taps.shape[0] - 1
    count = lax.axis_size("seq")
    shard = in_weight[0].reshape(-1, 3 * width)
    tail = in_weight[0].reshape(-1, 3, count, width // count).transpose(2, 1, 3, 0)
    tail = tail.reshape(count, 3 * width // count, -1)
    projected_table, in_full = prepare(tail, shard, embed_table, norm_gain)
    projected_table = projected_table.reshape(3 * width, vocab)

    def normalised(rows):
        values = rows.astype(jnp.float32)
        scale = lax.rsqrt(jnp.mean(values * values, axis=1) + EPS)
        return (values * scale[:, None] * gain[None, :]).astype(jnp.bfloat16)

    def finish(values, query, gated_ext):
        medium = causal_sum(gated_ext.astype(jnp.float32), medium_taps, length)
        mixed = (query * medium).astype(jnp.bfloat16).reshape(micro * length, width)
        terms = jnp.dot(mixed, weight, preferred_element_type=jnp.float32)
        projected = lax.psum_scatter(
            terms.astype(jnp.bfloat16), "tensor", scatter_dimension=1, tiled=True
        ).astype(jnp.float32)
        return (values.astype(jnp.float32) + projected).astype(jnp.bfloat16)

    before = passed_along(token_ids + 1, "seq", 1) - 1
    ids = jnp.concatenate([before, token_ids], axis=1).reshape(-1)
    onehot = (ids[:, None] == jnp.arange(vocab, dtype=jnp.int32)[None, :]).astype(jnp.bfloat16)
    streams = (
        lax.dot_general(
            onehot, projected_table, (((1,), (1,)), ((), ())), preferred_element_type=jnp.float32
        )
        .astype(jnp.bfloat16)
        .reshape(micro, 2 * length, 3, width)
    )
    own = onehot.reshape(micro, 2 * length, vocab)[:, length:].reshape(-1, vocab)
    stream_0 = jnp.dot(own, embed_table, preferred_element_type=jnp.float32).astype(jnp.bfloat16)
    wide = streams[:, length - mr - se :].astype(jnp.float32)
    reach = length + mr
    gated_ext = (
        causal_sum(wide[:, :, 1], short_coeffs[:, 1], reach)
        * causal_sum(wide[:, :, 2], short_coeffs[:, 2], reach)
    ).astype(jnp.bfloat16)
    query = causal_sum(wide[:, mr:, 0], short_coeffs[:, 0], length)
    stream_1 = finish(stream_0, query, gated_ext)
    arrived = passed_along(stream_1, "section", 1)

    normed = normalised(lax.all_gather(arrived, "tensor", axis=1, tiled=True))
    streams = (
        jnp.dot(normed, in_full, preferred_element_type=jnp.float32)
        .astype(jnp.bfloat16)
        .reshape(micro, length, 3 * width)
    )
    rim = passed_along(streams[:, length - se :], "seq", 1)
    reach = jnp.concatenate([rim, streams], axis=1).astype(jnp.float32)
    reach = reach.reshape(micro, length + se, 3, width)
    short = causal_sum(reach, short_coeffs, length)
    gated = (short[:, :, 1] * short[:, :, 2]).astype(jnp.bfloat16)
    second_rim = passed_along(gated[:, length - mr :], "seq", 1)
    stream_2 = finish(arrived, short[:, :, 0], jnp.concatenate([second_rim, gated], axis=1))
    result = jnp.where(section == 0, stream_1, stream_2)
    return result.reshape(1, micro, length, width)


def solution(mesh):
    in_specs = (
        P(None, "seq"),
        P(None, "tensor"),
        P("section", None),
        P("section", "seq", None, "tensor"),
        P("section", None, None, "tensor"),
        P("section", None, "tensor"),
        P("section", "tensor", None),
    )
    out_specs = P("section", None, "seq", "tensor")
    return jax.shard_map(body, mesh=mesh, in_specs=in_specs, out_specs=out_specs, check_vma=False)
```

```python
import functools

import jax
import jax.numpy as jnp
from jax import lax
from jax.experimental import pallas as pl
from jax.experimental.pallas import tpu as pltpu
from jax.sharding import PartitionSpec as P

EPS = 1e-06
MESH = pl.DeviceIdType.MESH
RING = 8
VMEM = pl.BlockSpec(memory_space=pltpu.VMEM)
HBM = pl.BlockSpec(memory_space=pltpu.HBM)


def place():
    seq = lax.axis_index("seq")
    return seq // (2 * RING), (seq // 2) % RING, seq % 2


def seq_of(y, z, core):
    return (y * RING + z) * 2 + core


class Gather:
    MOVES = (
        ("a1", "up", True, 0, None),
        ("b1", "down", True, 0, None),
        ("c1", "y", True, 0, None),
        ("a2", "up", True, -1, None),
        ("b2", "down", True, 1, None),
        ("a3", "up", True, -2, None),
        ("b3", "down", True, 2, None),
        ("c2", "y", True, -2, 1),
        ("c3", "y", True, 2, 0),
        ("a4", "up", True, -3, 0),
        ("b4", "down", True, 3, 1),
        ("a5", "up", False, 0, None),
        ("b5", "down", False, 0, None),
        ("c4", "y", True, -3, None),
        ("c5", "y", True, 3, None),
        ("a6", "up", False, -1, 0),
        ("b6", "down", False, 1, 1),
        ("c6", "y", True, 4, 0),
        ("c7", "y", True, 4, 1),
    )
    COUNT = len(MOVES)

    def __init__(self, slot, own, send, recv, side_send, side_recv):
        self.y, self.z, self.core = place()
        self.slot, self.own = slot, own
        self.send, self.recv = send, recv
        self.side_send, self.side_recv = side_send, side_recv
        self.index = {move[0]: at for at, move in enumerate(self.MOVES)}
        self.pending = []

    def target(self, direction):
        if direction == "up":
            return seq_of(self.y, (self.z + 1) % RING, self.core)
        if direction == "down":
            return seq_of(self.y, (self.z + RING - 1) % RING, self.core)
        return seq_of(1 - self.y, self.z, self.core)

    def block(self, same, dz, core=None):
        y = self.y if same else 1 - self.y
        return seq_of(y, (self.z + dz + RING) % RING, self.core if core is None else core)

    def copy(self, name):
        at = self.index[name]
        _, direction, same, dz, half = self.MOVES[at]
        block = self.block(same, dz)
        dst = self.slot(block, half)
        src = self.own if same and dz == 0 else dst
        return pltpu.make_async_remote_copy(
            src_ref=src,
            dst_ref=dst,
            send_sem=self.send.at[at],
            recv_sem=self.recv.at[at],
            device_id={"seq": self.target(direction)},
            device_id_type=MESH,
        )

    def start(self, *names):
        for name in names:
            self.copy(name).start()

    def landed(self, name):
        at = self.index[name]
        _, direction, same, dz, half = self.MOVES[at]
        if direction == "y":
            block = self.block(not same, dz)
        else:
            block = self.block(same, dz + (-1 if direction == "up" else 1))
        got = self.slot(block, half)
        pltpu.make_async_copy(got, got, self.recv.at[at]).wait()
        side = pltpu.make_async_remote_copy(
            src_ref=got,
            dst_ref=got,
            send_sem=self.side_send.at[at],
            recv_sem=self.side_recv.at[at],
            device_id={"seq": seq_of(self.y, self.z, 1 - self.core)},
            device_id_type=MESH,
        )
        side.start()

    def side_own(self):
        return pltpu.make_async_remote_copy(
            src_ref=self.own,
            dst_ref=self.slot(self.block(True, 0), None),
            send_sem=self.side_send.at[self.COUNT],
            recv_sem=self.side_recv.at[self.COUNT],
            device_id={"seq": seq_of(self.y, self.z, 1 - self.core)},
            device_id_type=MESH,
        )

    def run(self, local_sem):
        keep = pltpu.make_async_copy(self.own, self.slot(self.block(True, 0), None), local_sem)
        self.start("a1", "b1", "c1")
        self.side_own().start()
        keep.start()
        self.landed("a1")
        self.start("a2")
        self.landed("b1")
        self.start("b2")
        self.landed("c1")
        self.landed("a2")
        self.start("a3", "c2")
        self.landed("b2")
        self.start("b3", "c3")
        self.start("a5", "b5")
        self.landed("a3")
        self.start("a4", "c4")
        self.landed("b3")
        self.start("b4", "c5")
        self.landed("a5")
        self.start("a6")
        self.landed("b5")
        self.start("b6")
        self.landed("a4")
        self.start("c6")
        self.landed("b4")
        self.start("c7")
        for name in ("c2", "c3", "a6", "b6", "c4", "c5", "c6", "c7"):
            self.landed(name)
        keep.wait()
        for at, (name, direction, same, dz, half) in enumerate(self.MOVES):
            self.copy(name).wait_send()
            if direction == "y":
                block = (not same, dz)
            else:
                block = (same, dz + (-1 if direction == "up" else 1))
            mine = self.slot(self.block(*block), half)
            pltpu.make_async_copy(mine, mine, self.side_send.at[at]).wait()
            other = self.slot(self.block(*block, 1 - self.core), half)
            pltpu.make_async_copy(other, other, self.side_recv.at[at]).wait()
        side = self.side_own()
        side.wait_send()
        other = self.slot(self.block(True, 0, 1 - self.core), None)
        pltpu.make_async_copy(other, other, self.side_recv.at[self.COUNT]).wait()


def mixer_kernel(
    ids, tail, shard, table, gain, se, mr, weight_hbm, out,
    w, weight, tail_all, part, ids_all, sf, gf, query, mixf, mixed, send_buf, recv_buf, own_part, base, xs, xn,
    rim_send, rim_recv, far_send, far_recv,
    send, recv, side_send, side_recv, a2a_send, a2a_recv, x_send, x_recv,
    rs_send, rs_recv, ag_send, ag_recv, relay_send, relay_recv, halo_send, halo_recv, local,
):
    section = lax.axis_index("section")
    tensor = lax.axis_index("tensor")
    seq = lax.axis_index("seq")
    y, z, core = place()
    count, share, depth = tail.shape
    vocab, width = table.shape
    wide = share // 3
    half = vocab // 2
    ways = w.shape[0]
    micro = gf.shape[0]
    tiles = gf.shape[1]
    length = gf.shape[2] // 2
    taps = mr.shape[0]
    short_taps = se.shape[1]
    lane = 128
    block = 256
    chunks = ((0, 128), (128, micro * length - 128))
    ahead = (tensor + 1 + core * (ways - 2)) % ways
    behind = (tensor + ways - 1 - core * (ways - 2)) % ways
    far = (tensor + 2) % ways
    barrier = pltpu.get_barrier_semaphore()

    def greet(**axes):
        pl.semaphore_signal(barrier, inc=1, device_id=axes, device_id_type=MESH)

    def remote(src, dst, send_sem, recv_sem, **axes):
        return pltpu.make_async_remote_copy(
            src_ref=src, dst_ref=dst, send_sem=send_sem, recv_sem=recv_sem,
            device_id=axes, device_id_type=MESH,
        )

    def arrival(ref, sem):
        pltpu.make_async_copy(ref, ref, sem).wait()

    def lanes(tile):
        return pl.ds(pl.multiple_of(tile * lane, lane), lane)

    def short(tile, stream, start, rows):
        total = jnp.zeros((rows, lane), jnp.float32)
        for tap in range(short_taps):
            total += se[stream, tap : tap + 1, lanes(tile)] * sf[
                stream, tile, start - tap : start - tap + rows, :
            ]
        return total

    def gate(mb, tile, start, rows, at):
        values = short(tile, 1, start, rows) * short(tile, 2, start, rows)
        gf[mb, tile, at : at + rows, :] = values.astype(jnp.bfloat16).astype(jnp.float32)

    def medium(mb):
        def one_tile(tile, carry):
            total = jnp.zeros((length, lane), jnp.float32)
            reach = length + taps - 8
            for shift in range(8):
                begin = length - (taps - 8) - shift
                window = gf[mb, tile, begin : begin + reach, :]
                for step in range(taps // 8):
                    tap = 8 * step + shift
                    at = taps - 8 - 8 * step
                    total += mr[tap : tap + 1, lanes(tile)] * window[at : at + length]
            mixf[mb * length : (mb + 1) * length, lanes(tile)] = query[mb, tile] * total
            return carry

        lax.fori_loop(0, tiles, one_tile, 0)

    def partial_to(chunk, owner, finish):
        first, rows = chunks[chunk]
        window = slice(first, first + rows)

        def one_block(at, carry):
            inner = pl.ds(pl.multiple_of(at * block, block), block)
            outer = pl.ds(pl.multiple_of(owner * width + at * block, block), block)
            term = jnp.dot(mixed[window], weight[:, outer], preferred_element_type=jnp.float32)
            finish(window, inner, term)
            return carry

        lax.fori_loop(0, width // block, one_block, 0)

    def hop(chunk, at, to):
        first, rows = chunks[chunk]
        window = slice(first, first + rows)
        return remote(
            send_buf.at[at, window], recv_buf.at[at, window],
            rs_send.at[chunk * 3 + at], rs_recv.at[chunk * 3 + at], tensor=to,
        )

    def fill(at):
        def finish(window, inner, term):
            send_buf[at, window, inner] = term.astype(jnp.bfloat16)

        return finish

    def reduce_start(chunk):
        first, rows = chunks[chunk]
        window = slice(first, first + rows)
        mixed[window] = mixf[window].astype(jnp.bfloat16)
        partial_to(chunk, far, fill(0))
        hop(chunk, 0, ahead).start()
        partial_to(chunk, behind, fill(2))
        hop(chunk, 2, behind).start()

    def reduce_middle(chunk):
        hop(chunk, 0, ahead).wait_recv()

        def finish(window, inner, term):
            both = term + recv_buf[0, window, inner].astype(jnp.float32)
            send_buf[1, window, inner] = both.astype(jnp.bfloat16)

        partial_to(chunk, ahead, finish)
        hop(chunk, 1, ahead).start()

        def keep(window, inner, term):
            own_part[window, inner] = term

        partial_to(chunk, tensor, keep)

    def reduce_end(chunk):
        first, rows = chunks[chunk]
        hop(chunk, 2, behind).wait_recv()
        hop(chunk, 1, ahead).wait_recv()
        lines = 16

        def add(at, carry):
            window = pl.ds(pl.multiple_of(first + at * lines, lines), lines)
            total = own_part[window] + recv_buf[1, window].astype(jnp.float32)
            total += recv_buf[2, window].astype(jnp.float32)
            out[window] = (base[window] + total).astype(jnp.bfloat16)
            return carry

        lax.fori_loop(0, rows // lines, add, 0)

    def reduce_close():
        for chunk in range(2):
            hop(chunk, 0, ahead).wait_send()
            hop(chunk, 1, ahead).wait_send()
            hop(chunk, 2, behind).wait_send()

    def relay(chunk):
        first, rows = chunks[chunk]
        window = slice(first, first + rows)
        return remote(
            out.at[window], xs.at[tensor, window],
            relay_send.at[chunk], relay_recv.at[chunk], section=1,
        )

    load_weight = pltpu.make_async_copy(weight_hbm, weight, local.at[2])

    @pl.when(section == 0)
    def _():
        greet(tensor=ahead)
        greet(tensor=behind)

        def greet_seq(step, carry):
            greet(seq=(seq + step) % count)
            return carry

        lax.fori_loop(1, count, greet_seq, 0)
        pl.semaphore_wait(barrier, count + 2)
        load_weight.start()

        ids_on = remote(
            ids, ids_all.at[:, 0:length], halo_send.at[0], halo_recv.at[0],
            seq=(seq + 1) % count,
        )

        @pl.when(seq < count - 1)
        def _():
            ids_on.start()

        @pl.when(seq == 0)
        def _():
            ids_all[:, 0:length] = jnp.full((micro, length, lane), -1, jnp.int32)

        rows = pl.ds(pl.multiple_of(core * half, half), half)

        def along(at, src, owner, to):
            return remote(src, w.at[owner, rows, 0:width], x_send.at[at], x_recv.at[at], tensor=to)

        def across(at, owner):
            piece = w.at[owner, rows, 0:width]
            return remote(
                piece, piece, x_send.at[at], x_recv.at[at], seq=seq_of(y, z, 1 - core)
            )

        mine = table.at[rows]
        along(0, mine, tensor, ahead).start()
        along(1, mine, tensor, behind).start()
        keep = pltpu.make_async_copy(table, w.at[tensor, 0:vocab, 0:width], local.at[0])
        keep.start()

        def spread(step):
            to = (seq + step) % count
            return remote(
                tail.at[to],
                tail_all.at[:, pl.ds(pl.multiple_of(seq * depth, depth), depth)],
                a2a_send.at[step], a2a_recv.at[step], seq=to,
            )

        def spread_start(step, carry):
            spread(step).start()
            return carry

        lax.fori_loop(1, count, spread_start, 0)
        keep_tail = pltpu.make_async_copy(
            tail.at[seq],
            tail_all.at[:, pl.ds(pl.multiple_of(seq * depth, depth), depth)],
            local.at[1],
        )
        keep_tail.start()
        ids_all[:, length : 2 * length] = ids[...]

        along(0, mine, tensor, ahead).wait_recv()
        along(2, w.at[behind, rows, 0:width], behind, ahead).start()
        across(3, behind).start()
        along(1, mine, tensor, behind).wait_recv()
        across(4, ahead).start()
        got = w.at[far, rows, 0:width]
        arrival(got, x_recv.at[2])
        across(5, far).start()
        keep.wait()
        for at, owner in ((3, behind), (4, ahead), (5, far)):
            across(at, owner).wait_recv()
        along(0, mine, tensor, ahead).wait_send()
        along(1, mine, tensor, behind).wait_send()
        arrival(got, x_send.at[2])
        for at, owner in ((3, behind), (4, ahead), (5, far)):
            across(at, owner).wait_send()

        lines = 32

        def normalise(at, carry):
            window = pl.ds(pl.multiple_of(at * lines, lines), lines)
            total = jnp.zeros((lines, 1), jnp.float32)
            for way in range(ways):
                values = w[way, window, 0:width].astype(jnp.float32)
                total += jnp.sum(values * values, axis=1, keepdims=True)
            scale = lax.rsqrt(total / (ways * width) + EPS)
            for way in range(ways):
                values = w[way, window, 0:width].astype(jnp.float32)
                values = values * scale * gain[:, way * width : (way + 1) * width]
                w[way, window, 0:width] = values.astype(jnp.bfloat16)
            return carry

        lax.fori_loop(0, vocab // lines, normalise, 0)

        def spread_wait(step, carry):
            spread(step).wait_send()
            arrival(tail_all.at[:, pl.ds(0, depth)], a2a_recv.at[step])
            return carry

        lax.fori_loop(1, count, spread_wait, 0)
        keep_tail.wait()
        total = jnp.zeros((share, vocab), jnp.float32)
        for way in range(ways):
            total += lax.dot_general(
                tail_all[:, way * width : (way + 1) * width],
                w[way, 0:vocab, 0:width],
                (((1,), (1,)), ((), ())),
                preferred_element_type=jnp.float32,
            )
        for stream in range(3):
            part[stream] = total[stream * wide : (stream + 1) * wide].astype(jnp.bfloat16)

        def slot(owner, part_of):
            at, some = owner * wide, wide
            if part_of is not None:
                some = wide // 2
                at = at + part_of * some
            return w.at[0:3, pl.ds(pl.multiple_of(at, some), some), width : width + vocab]

        Gather(slot, part, send, recv, side_send, side_recv).run(local.at[0])
        load_weight.wait()

        @pl.when(seq > 0)
        def _():
            ids_on.wait_recv()

        onehot = w.at[3, 0 : 2 * length, width : width + vocab]

        def streams(mb):
            for part_at in range(vocab // lane):
                number = lax.broadcasted_iota(jnp.int32, (2 * length, lane), 1) + part_at * lane
                hit = jnp.where(ids_all[mb] == number, 1.0, 0.0).astype(jnp.bfloat16)
                w[3, 0 : 2 * length, width + part_at * lane : width + (part_at + 1) * lane] = hit

            def one_block(at, carry):
                stream, inner = at // (width // block), at % (width // block)
                columns = pl.ds(pl.multiple_of(inner * block, block), block)
                values = lax.dot_general(
                    onehot[...],
                    w[stream, columns, width : width + vocab],
                    (((1,), (1,)), ((), ())),
                    preferred_element_type=jnp.float32,
                ).astype(jnp.bfloat16).astype(jnp.float32)
                for side in range(block // lane):
                    sf[stream, inner * (block // lane) + side, 8 : 8 + 2 * length, :] = values[
                        :, side * lane : (side + 1) * lane
                    ]
                return carry

            lax.fori_loop(0, 3 * width // block, one_block, 0)

            def own_rows(at, carry):
                columns = pl.ds(pl.multiple_of(at * block, block), block)
                values = jnp.dot(
                    onehot[...], table[:, columns], preferred_element_type=jnp.float32
                )
                base[mb * length : (mb + 1) * length, columns] = values[length : 2 * length]
                return carry

            lax.fori_loop(0, width // block, own_rows, 0)

            def one_tile(tile, carry):
                query[mb, tile] = short(tile, 0, 8 + length, length)
                gate(mb, tile, 8, length, 0)
                gate(mb, tile, 8 + length, length, length)
                return carry

            lax.fori_loop(0, tiles, one_tile, 0)

        sf[:, :, 0:8, :] = jnp.zeros((3, tiles, 8, lane), jnp.float32)
        streams(0)
        medium(0)
        reduce_start(0)
        streams(1)
        reduce_middle(0)
        medium(1)
        reduce_end(0)
        relay(0).start()
        reduce_start(1)
        reduce_middle(1)
        reduce_end(1)
        relay(1).start()
        reduce_close()
        relay(0).wait_send()
        relay(1).wait_send()

        @pl.when(seq < count - 1)
        def _():
            ids_on.wait_send()

    @pl.when(section == 1)
    def _():
        greet(seq=seq_of(y, (z + 1) % RING, core))
        greet(seq=seq_of(y, (z + RING - 1) % RING, core))
        greet(seq=seq_of(1 - y, z, core))
        greet(seq=seq_of(y, z, 1 - core))
        greet(tensor=ahead)
        greet(tensor=behind)
        greet(section=0)

        @pl.when(seq > 0)
        def _():
            greet(seq=(seq + count - 1) % count)

        @pl.when(seq < count - 1)
        def _():
            pl.semaphore_wait(barrier, 7)

        @pl.when(seq == count - 1)
        def _():
            pl.semaphore_wait(barrier, 6)

        load_weight.start()
        per = width // depth

        def slot(owner, part_of):
            at, some = (owner % per) * depth, depth
            if part_of is not None:
                some = depth // 2
                at = at + part_of * some
            return w.at[owner // per, pl.ds(pl.multiple_of(at, some), some)]

        Gather(slot, shard, send, recv, side_send, side_recv).run(local.at[0])
        load_weight.wait()

        def share_out(chunk, at, owner, to):
            first, rows = chunks[chunk]
            piece = xs.at[owner, first : first + rows]
            return remote(
                piece, piece, ag_send.at[chunk * 3 + at], ag_recv.at[chunk * 3 + at], tensor=to
            )

        def gather_start(chunk):
            first, rows = chunks[chunk]
            arrival(xs.at[tensor, first : first + rows], relay_recv.at[chunk])
            share_out(chunk, 0, tensor, ahead).start()
            share_out(chunk, 1, tensor, behind).start()

        def gather_middle(chunk):
            first, rows = chunks[chunk]
            arrival(xs.at[behind, first : first + rows], ag_recv.at[chunk * 3])
            share_out(chunk, 2, behind, ahead).start()

        def gather_end(chunk):
            first, rows = chunks[chunk]
            arrival(xs.at[ahead, first : first + rows], ag_recv.at[chunk * 3 + 1])
            arrival(xs.at[far, first : first + rows], ag_recv.at[chunk * 3 + 2])

        def gather_close():
            for chunk in range(2):
                share_out(chunk, 0, tensor, ahead).wait_send()
                share_out(chunk, 1, tensor, behind).wait_send()
                share_out(chunk, 2, behind, ahead).wait_send()

        def project(chunk):
            first, rows = chunks[chunk]
            lines = 16

            def normalise(at, carry):
                window = pl.ds(pl.multiple_of(first + at * lines, lines), lines)
                total = jnp.zeros((lines, 1), jnp.float32)
                for way in range(ways):
                    values = xs[way, window].astype(jnp.float32)
                    total += jnp.sum(values * values, axis=1, keepdims=True)
                scale = lax.rsqrt(total / (ways * width) + EPS)
                for way in range(ways):
                    values = xs[way, window].astype(jnp.float32)
                    values = values * scale * gain[:, way * width : (way + 1) * width]
                    xn[way, window] = values.astype(jnp.bfloat16)
                base[window] = xs[tensor, window].astype(jnp.float32)
                return carry

            lax.fori_loop(0, rows // lines, normalise, 0)

            def one_block(at, carry):
                stream, inner = at // (width // block), at % (width // block)
                columns = pl.ds(pl.multiple_of(at * block, block), block)
                total = jnp.zeros((rows, block), jnp.float32)
                for way in range(ways):
                    total += jnp.dot(
                        xn[way, first : first + rows],
                        w[way, :, columns],
                        preferred_element_type=jnp.float32,
                    )
                total = total.astype(jnp.bfloat16).astype(jnp.float32)
                for side in range(block // lane):
                    tile = inner * (block // lane) + side
                    piece = total[:, side * lane : (side + 1) * lane]
                    for mb in range(micro):
                        begin = max(first, mb * length)
                        end = min(first + rows, (mb + 1) * length)
                        if begin < end:
                            to = mb * (length + 8) + 8 + begin - mb * length
                            sf[stream, tile, to : to + end - begin, :] = piece[
                                begin - first : end - first
                            ]
                return carry

            lax.fori_loop(0, 3 * width // block, one_block, 0)

        def rim(mb):
            return remote(
                rim_send.at[mb], rim_recv.at[mb], halo_send.at[mb], halo_recv.at[mb],
                seq=(seq + 1) % count,
            )

        def gated_rim(mb):
            return remote(
                far_send.at[mb], far_recv.at[mb], halo_send.at[micro + mb], halo_recv.at[micro + mb],
                seq=(seq + 1) % count,
            )

        def rim_start(mb):
            last = (mb + 1) * (length + 8)
            rim_send[mb] = sf[:, :, last - 16 : last, :].astype(jnp.bfloat16)

            @pl.when(seq < count - 1)
            def _():
                rim(mb).start()

        def shorts(mb):
            first = mb * (length + 8)

            @pl.when(seq > 0)
            def _():
                rim(mb).wait_recv()
                sf[:, :, first : first + 8, :] = rim_recv[mb].astype(jnp.float32)[:, :, 8:16]

            @pl.when(seq == 0)
            def _():
                sf[:, :, first : first + 8, :] = jnp.zeros((3, tiles, 8, lane), jnp.float32)

            def one_tile(tile, carry):
                query[mb, tile] = short(tile, 0, first + 8, length)
                gate(mb, tile, first + 8, length, length)
                far_send[mb, tile] = gf[mb, tile, 2 * length - taps : 2 * length, :].astype(
                    jnp.bfloat16
                )
                return carry

            lax.fori_loop(0, tiles, one_tile, 0)

            @pl.when(seq < count - 1)
            def _():
                gated_rim(mb).start()

        def gated_end(mb):
            @pl.when(seq > 0)
            def _():
                gated_rim(mb).wait_recv()

                def one_tile(tile, carry):
                    gf[mb, tile, length - taps : length, :] = far_recv[mb, tile].astype(
                        jnp.float32
                    )
                    return carry

                lax.fori_loop(0, tiles, one_tile, 0)

            @pl.when(seq == 0)
            def _():
                gf[mb, :, 0:length, :] = jnp.zeros((tiles, length, lane), jnp.float32)

        gather_start(0)
        gather_middle(0)
        gather_end(0)
        gather_start(1)
        project(0)
        gather_middle(1)
        gather_end(1)
        project(1)
        rim_start(0)
        rim_start(1)
        shorts(0)
        shorts(1)
        gated_end(0)
        medium(0)
        reduce_start(0)
        gated_end(1)
        reduce_middle(0)
        medium(1)
        reduce_end(0)
        reduce_start(1)
        reduce_middle(1)
        reduce_end(1)
        reduce_close()
        gather_close()

        @pl.when(seq < count - 1)
        def _():
            for mb in range(micro):
                rim(mb).wait_send()
                gated_rim(mb).wait_send()


def body(token_ids, embed_table, norm_gain, in_weight, se_filter, mr_filter, out_weight):
    micro, length = token_ids.shape
    vocab, width = embed_table.shape
    full = norm_gain.shape[1]
    count = lax.axis_size("seq")
    ways = full // width
    lane = 128
    tiles = width // lane
    rows = micro * length
    taps = mr_filter.shape[1]
    depth = in_weight.shape[1]
    share = 3 * width // count
    shard = in_weight[0].reshape(depth, 3 * width)
    tail = in_weight[0].reshape(depth, 3, count, width // count).transpose(2, 1, 3, 0)
    tail = tail.reshape(count, share, depth)
    ids = jnp.broadcast_to(token_ids[:, :, None], (micro, length, lane))
    moves = Gather.COUNT
    bf16, f32 = jnp.bfloat16, jnp.float32
    scratch, dma = pltpu.VMEM, pltpu.SemaphoreType.DMA
    result = pl.pallas_call(
        mixer_kernel,
        out_shape=jax.ShapeDtypeStruct((rows, width), bf16),
        in_specs=[VMEM, HBM, HBM, VMEM, VMEM, VMEM, VMEM, HBM],
        out_specs=VMEM,
        scratch_shapes=[
            scratch((ways, width, 3 * width), bf16),
            scratch((width, full), bf16),
            scratch((share, full), bf16),
            scratch((3, share // 3, vocab), bf16),
            scratch((micro, 2 * length, lane), jnp.int32),
            scratch((3, tiles, 2 * length + 16, lane), f32),
            scratch((micro, tiles, 2 * length, lane), f32),
            scratch((micro, tiles, length, lane), f32),
            scratch((rows, width), f32),
            scratch((rows, width), bf16),
            scratch((3, rows, width), bf16),
            scratch((3, rows, width), bf16),
            scratch((rows, width), f32),
            scratch((rows, width), f32),
            scratch((ways, rows, width), bf16),
            scratch((ways, rows, width), bf16),
            scratch((micro, 3, tiles, 16, lane), bf16),
            scratch((micro, 3, tiles, 16, lane), bf16),
            scratch((micro, tiles, taps, lane), bf16),
            scratch((micro, tiles, taps, lane), bf16),
            dma((moves,)),
            dma((moves,)),
            dma((moves + 1,)),
            dma((moves + 1,)),
            dma((count,)),
            dma((count,)),
            dma((6,)),
            dma((6,)),
            dma((6,)),
            dma((6,)),
            dma((6,)),
            dma((6,)),
            dma((2,)),
            dma((2,)),
            dma((2 * micro,)),
            dma((2 * micro,)),
            dma((3,)),
        ],
        compiler_params=pltpu.CompilerParams(
            collective_id=0, has_side_effects=True, vmem_limit_bytes=60 << 20
        ),
        name="mixer",
    )(ids, tail, shard, embed_table, norm_gain, se_filter[0], mr_filter[0], out_weight[0])
    return result.reshape(1, micro, length, width)


def solution(mesh):
    in_specs = (
        P(None, "seq"),
        P(None, "tensor"),
        P("section", None),
        P("section", "seq", None, "tensor"),
        P("section", None, None, "tensor"),
        P("section", None, "tensor"),
        P("section", "tensor", None),
    )
    out_specs = P("section", None, "seq", "tensor")
    return jax.shard_map(body, mesh=mesh, in_specs=in_specs, out_specs=out_specs, check_vma=False)
```

```python
import functools

import jax
import jax.numpy as jnp
from jax import lax
from jax.experimental import pallas as pl
from jax.experimental.pallas import tpu as pltpu
from jax.sharding import PartitionSpec as P

EPS = 1e-06
MESH = pl.DeviceIdType.MESH
RING = 8
VMEM = pl.BlockSpec(memory_space=pltpu.VMEM)
HBM = pl.BlockSpec(memory_space=pltpu.HBM)


def place():
    seq = lax.axis_index("seq")
    return seq // (2 * RING), (seq // 2) % RING, seq % 2


def seq_of(y, z, core):
    return (y * RING + z) * 2 + core


class Gather:
    MOVES = (
        ("a1", "up", True, 0, None),
        ("b1", "down", True, 0, None),
        ("c1", "y", True, 0, None),
        ("a2", "up", True, -1, None),
        ("b2", "down", True, 1, None),
        ("c2", "y", True, -1, 1),
        ("c3", "y", True, 1, 0),
        ("a3", "up", True, -2, None),
        ("b3", "down", True, 2, None),
        ("c4", "y", True, -2, 1),
        ("c5", "y", True, 2, 0),
        ("a4", "up", True, -3, 0),
        ("b4", "down", True, 3, 1),
        ("c6", "y", True, -3, 0),
        ("c7", "y", True, 3, 1),
        ("a5", "up", False, 0, 0),
        ("b5", "down", False, 0, 1),
        ("c8", "y", True, -3, 1),
        ("c9", "y", True, 3, 0),
        ("a6", "up", False, -1, 0),
        ("b6", "down", False, 1, 1),
        ("a7", "up", False, -3, 0),
        ("b7", "down", False, 3, 1),
    )
    COUNT = len(MOVES)

    def __init__(self, slot, own, send, recv, side_send, side_recv):
        self.y, self.z, self.core = place()
        self.slot, self.own = slot, own
        self.send, self.recv = send, recv
        self.side_send, self.side_recv = side_send, side_recv
        self.index = {move[0]: at for at, move in enumerate(self.MOVES)}
        self.pending = []

    def target(self, direction):
        if direction == "up":
            return seq_of(self.y, (self.z + 1) % RING, self.core)
        if direction == "down":
            return seq_of(self.y, (self.z + RING - 1) % RING, self.core)
        return seq_of(1 - self.y, self.z, self.core)

    def block(self, same, dz, core=None):
        y = self.y if same else 1 - self.y
        return seq_of(y, (self.z + dz + RING) % RING, self.core if core is None else core)

    def copy(self, name):
        at = self.index[name]
        _, direction, same, dz, half = self.MOVES[at]
        block = self.block(same, dz)
        dst = self.slot(block, half)
        src = self.own if same and dz == 0 else dst
        return pltpu.make_async_remote_copy(
            src_ref=src,
            dst_ref=dst,
            send_sem=self.send.at[at],
            recv_sem=self.recv.at[at],
            device_id={"seq": self.target(direction)},
            device_id_type=MESH,
        )

    def start(self, *names):
        for name in names:
            self.copy(name).start()

    def landed(self, name):
        at = self.index[name]
        _, direction, same, dz, half = self.MOVES[at]
        if direction == "y":
            block = self.block(not same, dz)
        else:
            block = self.block(same, dz + (-1 if direction == "up" else 1))
        got = self.slot(block, half)
        pltpu.make_async_copy(got, got, self.recv.at[at]).wait()
        side = pltpu.make_async_remote_copy(
            src_ref=got,
            dst_ref=got,
            send_sem=self.side_send.at[at],
            recv_sem=self.side_recv.at[at],
            device_id={"seq": seq_of(self.y, self.z, 1 - self.core)},
            device_id_type=MESH,
        )
        side.start()

    def side_own(self):
        return pltpu.make_async_remote_copy(
            src_ref=self.own,
            dst_ref=self.slot(self.block(True, 0), None),
            send_sem=self.side_send.at[self.COUNT],
            recv_sem=self.side_recv.at[self.COUNT],
            device_id={"seq": seq_of(self.y, self.z, 1 - self.core)},
            device_id_type=MESH,
        )

    def run(self, local_sem, late=None):
        keep = pltpu.make_async_copy(self.own, self.slot(self.block(True, 0), None), local_sem)
        self.start("a1", "b1", "c1")
        self.side_own().start()
        keep.start()
        self.landed("a1")
        self.start("a2", "c2")
        self.landed("b1")
        self.start("b2", "c3")
        self.landed("c1")
        self.landed("a2")
        self.start("a3", "c4")
        self.landed("b2")
        self.start("b3", "c5")
        self.landed("c2")
        self.landed("c3")
        self.landed("a3")
        self.start("a4", "c6", "a5")
        self.landed("b3")
        self.start("b4", "c7", "b5")
        for name in ("c4", "c5", "a4", "b4"):
            self.landed(name)
        self.start("c8", "c9")
        self.landed("a5")
        self.start("a6")
        self.landed("b5")
        self.start("b6")
        self.landed("c6")
        self.start("a7")
        self.landed("c7")
        self.start("b7")
        self.landed("a6")
        self.landed("b6")
        if late is not None:
            late()
        for name in ("c8", "c9", "a7", "b7"):
            self.landed(name)
        keep.wait()
        for at, (name, direction, same, dz, half) in enumerate(self.MOVES):
            self.copy(name).wait_send()
            if direction == "y":
                block = (not same, dz)
            else:
                block = (same, dz + (-1 if direction == "up" else 1))
            mine = self.slot(self.block(*block), half)
            pltpu.make_async_copy(mine, mine, self.side_send.at[at]).wait()
            other = self.slot(self.block(*block, 1 - self.core), half)
            pltpu.make_async_copy(other, other, self.side_recv.at[at]).wait()
        side = self.side_own()
        side.wait_send()
        other = self.slot(self.block(True, 0, 1 - self.core), None)
        pltpu.make_async_copy(other, other, self.side_recv.at[self.COUNT]).wait()


def mixer_kernel(
    ids, tail, shard, table, gain, se, mr, weight_hbm, out,
    w, weight, tail_all, part, ids_all, sf, gf, query, mixf, mixed, send_buf, recv_buf, own_part, base, xs, xn,
    rim_send, rim_recv, far_send, far_recv,
    send, recv, side_send, side_recv, a2a_send, a2a_recv, x_send, x_recv,
    rs_send, rs_recv, ag_send, ag_recv, relay_send, relay_recv, halo_send, halo_recv, local,
):
    section = lax.axis_index("section")
    tensor = lax.axis_index("tensor")
    seq = lax.axis_index("seq")
    y, z, core = place()
    depth = tail.shape[2]
    vocab, width = table.shape
    wide = part.shape[1]
    count = tail.shape[1] // wide
    share = 3 * wide
    half = vocab // 2
    ways = w.shape[0]
    micro = gf.shape[0]
    tiles = gf.shape[1]
    length = gf.shape[2] // 2
    taps = mr.shape[0]
    short_taps = se.shape[1]
    lane = 128
    block = 256
    chunks = ((0, 64), (64, 64), (128, 80), (208, micro * length - 208))
    groups = ((0, 128), (128, micro * length - 128))
    ahead = (tensor + 1 + core * (ways - 2)) % ways
    behind = (tensor + ways - 1 - core * (ways - 2)) % ways
    far = (tensor + 2) % ways
    barrier = pltpu.get_barrier_semaphore()

    def greet(**axes):
        pl.semaphore_signal(barrier, inc=1, device_id=axes, device_id_type=MESH)

    def remote(src, dst, send_sem, recv_sem, **axes):
        return pltpu.make_async_remote_copy(
            src_ref=src, dst_ref=dst, send_sem=send_sem, recv_sem=recv_sem,
            device_id=axes, device_id_type=MESH,
        )

    def arrival(ref, sem):
        pltpu.make_async_copy(ref, ref, sem).wait()

    def lanes(tile):
        return pl.ds(pl.multiple_of(tile * lane, lane), lane)

    def short(tile, stream, start, rows):
        total = jnp.zeros((rows, lane), jnp.float32)
        for tap in range(short_taps):
            total += se[stream, tap, :, lanes(tile)] * sf[
                stream, tile, start - tap : start - tap + rows, :
            ]
        return total

    def gate(mb, tile, start, rows, at):
        values = short(tile, 1, start, rows) * short(tile, 2, start, rows)
        gf[mb, tile, at : at + rows, :] = values.astype(jnp.bfloat16).astype(jnp.float32)

    def medium(mb, begin, rows):
        def one_tile(tile, carry):
            total = jnp.zeros((rows, lane), jnp.float32)
            reach = rows + taps - 8
            for shift in range(8):
                first = length + begin - (taps - 8) - shift
                window = gf[mb, tile, first : first + reach, :]
                for step in range(taps // 8):
                    tap = 8 * step + shift
                    at = taps - 8 - 8 * step
                    total += mr[tap : tap + 1, lanes(tile)] * window[at : at + rows]
            to = mb * length + begin
            mixf[to : to + rows, lanes(tile)] = query[mb, tile, begin : begin + rows] * total
            return carry

        lax.fori_loop(0, tiles, one_tile, 0)

    def partial_to(chunk, owner, finish):
        first, rows = chunks[chunk]
        window = slice(first, first + rows)

        def one_block(at, carry):
            inner = pl.ds(pl.multiple_of(at * block, block), block)
            outer = pl.ds(pl.multiple_of(owner * width + at * block, block), block)
            term = jnp.dot(mixed[window], weight[:, outer], preferred_element_type=jnp.float32)
            finish(window, inner, term)
            return carry

        lax.fori_loop(0, width // block, one_block, 0)

    def hop(chunk, at, to):
        first, rows = chunks[chunk]
        window = slice(first, first + rows)
        return remote(
            send_buf.at[at, window], recv_buf.at[at, window],
            rs_send.at[chunk * 3 + at], rs_recv.at[chunk * 3 + at], tensor=to,
        )

    def fill(at):
        def finish(window, inner, term):
            send_buf[at, window, inner] = term.astype(jnp.bfloat16)

        return finish

    def reduce_start(chunk):
        first, rows = chunks[chunk]
        window = slice(first, first + rows)
        mixed[window] = mixf[window].astype(jnp.bfloat16)
        partial_to(chunk, far, fill(0))
        hop(chunk, 0, ahead).start()
        partial_to(chunk, behind, fill(2))
        hop(chunk, 2, behind).start()

    def reduce_middle(chunk):
        hop(chunk, 0, ahead).wait_recv()

        def finish(window, inner, term):
            both = term + recv_buf[0, window, inner].astype(jnp.float32)
            send_buf[1, window, inner] = both.astype(jnp.bfloat16)

        partial_to(chunk, ahead, finish)
        hop(chunk, 1, ahead).start()

        def keep(window, inner, term):
            own_part[window, inner] = term

        partial_to(chunk, tensor, keep)

    def reduce_end(chunk):
        first, rows = chunks[chunk]
        hop(chunk, 2, behind).wait_recv()
        hop(chunk, 1, ahead).wait_recv()
        lines = 16

        def add(at, carry):
            window = pl.ds(pl.multiple_of(first + at * lines, lines), lines)
            total = own_part[window] + recv_buf[1, window].astype(jnp.float32)
            total += recv_buf[2, window].astype(jnp.float32)
            out[window] = (base[window] + total).astype(jnp.bfloat16)
            return carry

        lax.fori_loop(0, rows // lines, add, 0)

    def reduce_close():
        for chunk in range(len(chunks)):
            hop(chunk, 0, ahead).wait_send()
            hop(chunk, 1, ahead).wait_send()
            hop(chunk, 2, behind).wait_send()

    def relay(chunk):
        first, rows = chunks[chunk]
        window = slice(first, first + rows)
        return remote(
            out.at[window], xs.at[tensor, window],
            relay_send.at[chunk], relay_recv.at[chunk], section=1,
        )

    load_weight = pltpu.make_async_copy(weight_hbm, weight, local.at[2])

    @pl.when(section == 0)
    def _():
        greet(tensor=ahead)
        greet(tensor=behind)

        def greet_seq(step, carry):
            greet(seq=(seq + step) % count)
            return carry

        lax.fori_loop(1, count, greet_seq, 0)
        pl.semaphore_wait(barrier, count + 2)
        load_weight.start()

        ids_on = remote(
            ids, ids_all.at[:, 0:length], halo_send.at[0], halo_recv.at[0],
            seq=(seq + 1) % count,
        )

        @pl.when(seq < count - 1)
        def _():
            ids_on.start()

        @pl.when(seq == 0)
        def _():
            ids_all[:, 0:length] = jnp.full((micro, length, lane), -1, jnp.int32)

        rows = pl.ds(pl.multiple_of(core * half, half), half)

        def table_of(owner):
            return w.at[1 + owner // 2, owner % 2, 0:vocab]

        def along(at, src, owner, to):
            return remote(src, table_of(owner).at[rows], x_send.at[at], x_recv.at[at], tensor=to)

        def across(at, owner):
            piece = table_of(owner).at[rows]
            return remote(
                piece, piece, x_send.at[at], x_recv.at[at], seq=seq_of(y, z, 1 - core)
            )

        mine = table.at[rows]
        along(0, mine, tensor, ahead).start()
        along(1, mine, tensor, behind).start()
        keep = pltpu.make_async_copy(table, table_of(tensor), local.at[0])
        keep.start()

        def spread(step):
            to = (seq + step) % count
            return remote(
                tail.at[:, pl.ds(pl.multiple_of(to * wide, wide), wide)],
                tail_all.at[:, :, pl.ds(pl.multiple_of(seq * depth, depth), depth)],
                a2a_send.at[step], a2a_recv.at[step], seq=to,
            )

        def spread_start(step, carry):
            spread(step).start()
            return carry

        lax.fori_loop(1, count, spread_start, 0)
        keep_tail = pltpu.make_async_copy(
            tail.at[:, pl.ds(pl.multiple_of(seq * wide, wide), wide)],
            tail_all.at[:, :, pl.ds(pl.multiple_of(seq * depth, depth), depth)],
            local.at[1],
        )
        keep_tail.start()
        ids_all[:, length : 2 * length] = ids[...]

        along(0, mine, tensor, ahead).wait_recv()
        along(2, table_of(behind).at[rows], behind, ahead).start()
        across(3, behind).start()
        along(1, mine, tensor, behind).wait_recv()
        across(4, ahead).start()
        got = table_of(far).at[rows]
        arrival(got, x_recv.at[2])
        across(5, far).start()
        keep.wait()
        for at, owner in ((3, behind), (4, ahead), (5, far)):
            across(at, owner).wait_recv()
        along(0, mine, tensor, ahead).wait_send()
        along(1, mine, tensor, behind).wait_send()
        arrival(got, x_send.at[2])
        for at, owner in ((3, behind), (4, ahead), (5, far)):
            across(at, owner).wait_send()

        lines = 32

        def normalise(at, carry):
            window = pl.ds(pl.multiple_of(at * lines, lines), lines)
            total = jnp.zeros((lines, 1), jnp.float32)
            for way in range(ways):
                values = w[1 + way // 2, way % 2, window].astype(jnp.float32)
                total += jnp.sum(values * values, axis=1, keepdims=True)
            scale = lax.rsqrt(total / (ways * width) + EPS)
            for way in range(ways):
                values = w[1 + way // 2, way % 2, window].astype(jnp.float32)
                values = values * scale * gain[:, way * width : (way + 1) * width]
                w[1 + way // 2, way % 2, window] = values.astype(jnp.bfloat16)
            return carry

        lax.fori_loop(0, vocab // lines, normalise, 0)

        def spread_wait(step, carry):
            spread(step).wait_send()
            arrival(tail_all.at[:, :, pl.ds(0, depth)], a2a_recv.at[step])
            return carry

        lax.fori_loop(1, count, spread_wait, 0)
        keep_tail.wait()
        total = jnp.zeros((share, vocab), jnp.float32)
        for way in range(ways):
            total += lax.dot_general(
                tail_all[:, :, way * width : (way + 1) * width].reshape(share, width),
                w[1 + way // 2, way % 2, 0:vocab],
                (((1,), (1,)), ((), ())),
                preferred_element_type=jnp.float32,
            )
        for stream in range(3):
            part[stream] = total[stream * wide : (stream + 1) * wide].astype(jnp.bfloat16)

        def slot(owner, part_of):
            at, some = owner * wide, wide
            if part_of is not None:
                some = wide // 2
                at = at + part_of * some
            return w.at[0, :, pl.ds(pl.multiple_of(at, some), some), 0:vocab]

        Gather(slot, part, send, recv, side_send, side_recv).run(local.at[0])
        load_weight.wait()

        @pl.when(seq > 0)
        def _():
            ids_on.wait_recv()

        onehot = w.at[3, 0, 0 : 2 * length, 0:vocab]

        def streams(mb):
            for part_at in range(vocab // lane):
                number = lax.broadcasted_iota(jnp.int32, (2 * length, lane), 1) + part_at * lane
                hit = jnp.where(ids_all[mb] == number, 1.0, 0.0).astype(jnp.bfloat16)
                w[3, 0, 0 : 2 * length, part_at * lane : (part_at + 1) * lane] = hit

            def one_block(at, carry):
                stream, inner = at // (width // block), at % (width // block)
                columns = pl.ds(pl.multiple_of(inner * block, block), block)
                values = lax.dot_general(
                    onehot[...],
                    w[0, stream, columns, 0:vocab],
                    (((1,), (1,)), ((), ())),
                    preferred_element_type=jnp.float32,
                ).astype(jnp.bfloat16).astype(jnp.float32)
                for side in range(block // lane):
                    sf[stream, inner * (block // lane) + side, 8 : 8 + 2 * length, :] = values[
                        :, side * lane : (side + 1) * lane
                    ]
                return carry

            lax.fori_loop(0, 3 * width // block, one_block, 0)

            def own_rows(at, carry):
                columns = pl.ds(pl.multiple_of(at * block, block), block)
                values = jnp.dot(
                    onehot[...], table[:, columns], preferred_element_type=jnp.float32
                )
                base[mb * length : (mb + 1) * length, columns] = values[length : 2 * length]
                return carry

            lax.fori_loop(0, width // block, own_rows, 0)

            def one_tile(tile, carry):
                query[mb, tile] = short(tile, 0, 8 + length, length)
                gate(mb, tile, 8, length, 0)
                gate(mb, tile, 8 + length, length, length)
                return carry

            lax.fori_loop(0, tiles, one_tile, 0)

        sf[:, :, 0:8, :] = jnp.zeros((3, tiles, 8, lane), jnp.float32)
        def pass_on(chunk):
            reduce_end(chunk)
            relay(chunk).start()

        streams(0)
        medium(0, 0, 64)
        reduce_start(0)
        medium(0, 64, length - 64)
        reduce_start(1)
        reduce_middle(0)
        streams(1)
        reduce_middle(1)
        pass_on(0)
        medium(1, 0, 208 - length)
        reduce_start(2)
        pass_on(1)
        medium(1, 208 - length, 2 * length - 208)
        reduce_start(3)
        reduce_middle(2)
        reduce_middle(3)
        pass_on(2)
        pass_on(3)
        reduce_close()
        for chunk in range(len(chunks)):
            relay(chunk).wait_send()

        @pl.when(seq < count - 1)
        def _():
            ids_on.wait_send()

    @pl.when(section == 1)
    def _():
        greet(seq=seq_of(y, (z + 1) % RING, core))
        greet(seq=seq_of(y, (z + RING - 1) % RING, core))
        greet(seq=seq_of(1 - y, z, core))
        greet(seq=seq_of(y, z, 1 - core))
        greet(tensor=ahead)
        greet(tensor=behind)
        greet(section=0)

        @pl.when(seq > 0)
        def _():
            greet(seq=(seq + count - 1) % count)

        @pl.when(seq < count - 1)
        def _():
            pl.semaphore_wait(barrier, 7)

        @pl.when(seq == count - 1)
        def _():
            pl.semaphore_wait(barrier, 6)

        load_weight.start()
        per = width // depth

        def slot(owner, part_of):
            at, some = (owner % per) * depth, depth
            if part_of is not None:
                some = depth // 2
                at = at + part_of * some
            return w.at[owner // per, :, pl.ds(pl.multiple_of(at, some), some)]

        def share_out(chunk, at, owner, to):
            first, rows = chunks[chunk]
            piece = xs.at[owner, first : first + rows]
            return remote(
                piece, piece, ag_send.at[chunk * 3 + at], ag_recv.at[chunk * 3 + at], tensor=to
            )

        def gather_start(chunk):
            first, rows = chunks[chunk]
            arrival(xs.at[tensor, first : first + rows], relay_recv.at[chunk])
            share_out(chunk, 0, tensor, ahead).start()
            share_out(chunk, 1, tensor, behind).start()

        def gather_middle(chunk):
            first, rows = chunks[chunk]
            arrival(xs.at[behind, first : first + rows], ag_recv.at[chunk * 3])
            share_out(chunk, 2, behind, ahead).start()

        def gather_end(chunk):
            first, rows = chunks[chunk]
            arrival(xs.at[ahead, first : first + rows], ag_recv.at[chunk * 3 + 1])
            arrival(xs.at[far, first : first + rows], ag_recv.at[chunk * 3 + 2])

        def gather_close():
            for chunk in range(len(chunks)):
                share_out(chunk, 0, tensor, ahead).wait_send()
                share_out(chunk, 1, tensor, behind).wait_send()
                share_out(chunk, 2, behind, ahead).wait_send()

        def project(group):
            first, rows = groups[group]
            lines = 16

            def normalise(at, carry):
                window = pl.ds(pl.multiple_of(first + at * lines, lines), lines)
                total = jnp.zeros((lines, 1), jnp.float32)
                for way in range(ways):
                    values = xs[way, window].astype(jnp.float32)
                    total += jnp.sum(values * values, axis=1, keepdims=True)
                scale = lax.rsqrt(total / (ways * width) + EPS)
                for way in range(ways):
                    values = xs[way, window].astype(jnp.float32)
                    values = values * scale * gain[:, way * width : (way + 1) * width]
                    xn[way, window] = values.astype(jnp.bfloat16)
                base[window] = xs[tensor, window].astype(jnp.float32)
                return carry

            lax.fori_loop(0, rows // lines, normalise, 0)

            def one_block(at, carry):
                stream, inner = at // (width // block), at % (width // block)
                columns = pl.ds(pl.multiple_of(inner * block, block), block)
                total = jnp.zeros((rows, block), jnp.float32)
                for way in range(ways):
                    total += jnp.dot(
                        xn[way, first : first + rows],
                        w[way, stream, :, columns],
                        preferred_element_type=jnp.float32,
                    )
                total = total.astype(jnp.bfloat16).astype(jnp.float32)
                for side in range(block // lane):
                    tile = inner * (block // lane) + side
                    piece = total[:, side * lane : (side + 1) * lane]
                    for mb in range(micro):
                        begin = max(first, mb * length)
                        end = min(first + rows, (mb + 1) * length)
                        if begin < end:
                            to = mb * (length + 8) + 8 + begin - mb * length
                            sf[stream, tile, to : to + end - begin, :] = piece[
                                begin - first : end - first
                            ]
                return carry

            lax.fori_loop(0, 3 * width // block, one_block, 0)

        def rim(mb):
            return remote(
                rim_send.at[mb], rim_recv.at[mb], halo_send.at[mb], halo_recv.at[mb],
                seq=(seq + 1) % count,
            )

        def gated_rim(mb):
            return remote(
                far_send.at[mb], far_recv.at[mb], halo_send.at[micro + mb], halo_recv.at[micro + mb],
                seq=(seq + 1) % count,
            )

        def rim_start(mb):
            last = (mb + 1) * (length + 8)
            rim_send[mb] = sf[:, :, last - 16 : last, :].astype(jnp.bfloat16)

            @pl.when(seq < count - 1)
            def _():
                rim(mb).start()

        def shorts(mb):
            first = mb * (length + 8)

            @pl.when(seq > 0)
            def _():
                rim(mb).wait_recv()
                sf[:, :, first : first + 8, :] = rim_recv[mb].astype(jnp.float32)[:, :, 8:16]

            @pl.when(seq == 0)
            def _():
                sf[:, :, first : first + 8, :] = jnp.zeros((3, tiles, 8, lane), jnp.float32)

            def one_tile(tile, carry):
                query[mb, tile] = short(tile, 0, first + 8, length)
                gate(mb, tile, first + 8, length, length)
                far_send[mb, tile] = gf[mb, tile, 2 * length - taps : 2 * length, :].astype(
                    jnp.bfloat16
                )
                return carry

            lax.fori_loop(0, tiles, one_tile, 0)

            @pl.when(seq < count - 1)
            def _():
                gated_rim(mb).start()

        def gated_end(mb):
            @pl.when(seq > 0)
            def _():
                gated_rim(mb).wait_recv()

                def one_tile(tile, carry):
                    gf[mb, tile, length - taps : length, :] = far_recv[mb, tile].astype(
                        jnp.float32
                    )
                    return carry

                lax.fori_loop(0, tiles, one_tile, 0)

            @pl.when(seq == 0)
            def _():
                gf[mb, :, 0:length, :] = jnp.zeros((tiles, length, lane), jnp.float32)

        def early():
            gather_start(0)
            gather_middle(0)
            gather_start(1)

        Gather(slot, shard, send, recv, side_send, side_recv).run(local.at[0], early)
        load_weight.wait()
        gather_middle(1)
        gather_end(0)
        gather_end(1)
        project(0)
        gather_start(2)
        gather_start(3)
        gather_middle(2)
        gather_middle(3)
        gather_end(2)
        gather_end(3)
        project(1)
        rim_start(0)
        rim_start(1)
        shorts(0)
        shorts(1)
        gated_end(0)
        medium(0, 0, 64)
        reduce_start(0)
        medium(0, 64, length - 64)
        reduce_start(1)
        reduce_middle(0)
        gated_end(1)
        medium(1, 0, 208 - length)
        reduce_start(2)
        reduce_middle(1)
        reduce_end(0)
        medium(1, 208 - length, 2 * length - 208)
        reduce_start(3)
        reduce_end(1)
        reduce_middle(2)
        reduce_middle(3)
        reduce_end(2)
        reduce_end(3)
        reduce_close()
        gather_close()

        @pl.when(seq < count - 1)
        def _():
            for mb in range(micro):
                rim(mb).wait_send()
                gated_rim(mb).wait_send()


def body(token_ids, embed_table, norm_gain, in_weight, se_filter, mr_filter, out_weight):
    micro, length = token_ids.shape
    vocab, width = embed_table.shape
    full = norm_gain.shape[1]
    count = lax.axis_size("seq")
    ways = full // width
    lane = 128
    tiles = width // lane
    rows = micro * length
    taps = mr_filter.shape[1]
    depth = in_weight.shape[1]
    wide = width // count
    shard = in_weight[0].transpose(1, 0, 2)
    tail = shard.transpose(0, 2, 1)
    ids = jnp.broadcast_to(token_ids[:, :, None], (micro, length, lane))
    moves = Gather.COUNT
    bf16, f32 = jnp.bfloat16, jnp.float32
    scratch, dma = pltpu.VMEM, pltpu.SemaphoreType.DMA
    result = pl.pallas_call(
        mixer_kernel,
        out_shape=jax.ShapeDtypeStruct((rows, width), bf16),
        in_specs=[VMEM, HBM, HBM, VMEM, VMEM, VMEM, VMEM, HBM],
        out_specs=VMEM,
        scratch_shapes=[
            scratch((ways, 3, width, width), bf16),
            scratch((width, full), bf16),
            scratch((3, wide, full), bf16),
            scratch((3, wide, vocab), bf16),
            scratch((micro, 2 * length, lane), jnp.int32),
            scratch((3, tiles, 2 * length + 16, lane), f32),
            scratch((micro, tiles, 2 * length, lane), f32),
            scratch((micro, tiles, length, lane), f32),
            scratch((rows, width), f32),
            scratch((rows, width), bf16),
            scratch((3, rows, width), bf16),
            scratch((3, rows, width), bf16),
            scratch((rows, width), f32),
            scratch((rows, width), f32),
            scratch((ways, rows, width), bf16),
            scratch((ways, rows, width), bf16),
            scratch((micro, 3, tiles, 16, lane), bf16),
            scratch((micro, 3, tiles, 16, lane), bf16),
            scratch((micro, tiles, taps, lane), bf16),
            scratch((micro, tiles, taps, lane), bf16),
            dma((moves,)),
            dma((moves,)),
            dma((moves + 1,)),
            dma((moves + 1,)),
            dma((count,)),
            dma((count,)),
            dma((6,)),
            dma((6,)),
            dma((12,)),
            dma((12,)),
            dma((12,)),
            dma((12,)),
            dma((4,)),
            dma((4,)),
            dma((2 * micro,)),
            dma((2 * micro,)),
            dma((3,)),
        ],
        compiler_params=pltpu.CompilerParams(
            collective_id=0, has_side_effects=True, vmem_limit_bytes=60 << 20
        ),
        name="mixer",
    )(ids, tail, shard, embed_table, norm_gain, se_filter[0][:, :, None], mr_filter[0], out_weight[0])
    return result.reshape(1, micro, length, width)


def solution(mesh):
    in_specs = (
        P(None, "seq"),
        P(None, "tensor"),
        P("section", None),
        P("section", "seq", None, "tensor"),
        P("section", None, None, "tensor"),
        P("section", None, "tensor"),
        P("section", "tensor", None),
    )
    out_specs = P("section", None, "seq", "tensor")
    return jax.shard_map(body, mesh=mesh, in_specs=in_specs, out_specs=out_specs, check_vma=False)
```

```python
import functools

import jax
import jax.numpy as jnp
from jax import lax
from jax.experimental import pallas as pl
from jax.experimental.pallas import tpu as pltpu
from jax.sharding import PartitionSpec as P

EPS = 1e-06
MESH = pl.DeviceIdType.MESH
RING = 8
VMEM = pl.BlockSpec(memory_space=pltpu.VMEM)
HBM = pl.BlockSpec(memory_space=pltpu.HBM)


def place():
    seq = lax.axis_index("seq")
    return seq // (2 * RING), (seq // 2) % RING, seq % 2


def seq_of(y, z, core):
    return (y * RING + z) * 2 + core


class Gather:
    MOVES = (
        ("a1", "up", True, 0, None),
        ("b1", "down", True, 0, None),
        ("c1", "y", True, 0, None),
        ("a2", "up", True, -1, None),
        ("b2", "down", True, 1, None),
        ("c2", "y", True, -1, 1),
        ("c3", "y", True, 1, 0),
        ("a3", "up", True, -2, None),
        ("b3", "down", True, 2, None),
        ("c4", "y", True, -2, 1),
        ("c5", "y", True, 2, 0),
        ("a4", "up", True, -3, 0),
        ("b4", "down", True, 3, 1),
        ("c6", "y", True, -3, 0),
        ("c7", "y", True, 3, 1),
        ("a5", "up", False, 0, 0),
        ("b5", "down", False, 0, 1),
        ("c8", "y", True, -3, 1),
        ("c9", "y", True, 3, 0),
        ("a6", "up", False, -1, 0),
        ("b6", "down", False, 1, 1),
        ("a7", "up", False, -3, 0),
        ("b7", "down", False, 3, 1),
    )
    COUNT = len(MOVES)

    def __init__(self, slot, own, send, recv, side_send, side_recv):
        self.y, self.z, self.core = place()
        self.slot, self.own = slot, own
        self.send, self.recv = send, recv
        self.side_send, self.side_recv = side_send, side_recv
        self.index = {move[0]: at for at, move in enumerate(self.MOVES)}
        self.pending = []

    def target(self, direction):
        if direction == "up":
            return seq_of(self.y, (self.z + 1) % RING, self.core)
        if direction == "down":
            return seq_of(self.y, (self.z + RING - 1) % RING, self.core)
        return seq_of(1 - self.y, self.z, self.core)

    def block(self, same, dz, core=None):
        y = self.y if same else 1 - self.y
        return seq_of(y, (self.z + dz + RING) % RING, self.core if core is None else core)

    def copy(self, name):
        at = self.index[name]
        _, direction, same, dz, half = self.MOVES[at]
        block = self.block(same, dz)
        dst = self.slot(block, half)
        src = self.own if same and dz == 0 else dst
        return pltpu.make_async_remote_copy(
            src_ref=src,
            dst_ref=dst,
            send_sem=self.send.at[at],
            recv_sem=self.recv.at[at],
            device_id={"seq": self.target(direction)},
            device_id_type=MESH,
        )

    def start(self, *names):
        for name in names:
            self.copy(name).start()

    def landed(self, name):
        at = self.index[name]
        _, direction, same, dz, half = self.MOVES[at]
        if direction == "y":
            block = self.block(not same, dz)
        else:
            block = self.block(same, dz + (-1 if direction == "up" else 1))
        got = self.slot(block, half)
        pltpu.make_async_copy(got, got, self.recv.at[at]).wait()
        side = pltpu.make_async_remote_copy(
            src_ref=got,
            dst_ref=got,
            send_sem=self.side_send.at[at],
            recv_sem=self.side_recv.at[at],
            device_id={"seq": seq_of(self.y, self.z, 1 - self.core)},
            device_id_type=MESH,
        )
        side.start()

    def side_own(self):
        return pltpu.make_async_remote_copy(
            src_ref=self.own,
            dst_ref=self.slot(self.block(True, 0), None),
            send_sem=self.side_send.at[self.COUNT],
            recv_sem=self.side_recv.at[self.COUNT],
            device_id={"seq": seq_of(self.y, self.z, 1 - self.core)},
            device_id_type=MESH,
        )

    def run(self, local_sem, late=None):
        keep = pltpu.make_async_copy(self.own, self.slot(self.block(True, 0), None), local_sem)
        self.start("a1", "b1", "c1")
        self.side_own().start()
        keep.start()
        self.landed("a1")
        self.start("a2", "c2")
        self.landed("b1")
        self.start("b2", "c3")
        self.landed("c1")
        self.landed("a2")
        self.start("a3", "c4")
        self.landed("b2")
        self.start("b3", "c5")
        self.landed("c2")
        self.landed("c3")
        self.landed("a3")
        self.start("a4", "c6", "a5")
        self.landed("b3")
        self.start("b4", "c7", "b5")
        for name in ("c4", "c5", "a4", "b4"):
            self.landed(name)
        self.start("c8", "c9")
        self.landed("a5")
        self.start("a6")
        self.landed("b5")
        self.start("b6")
        self.landed("c6")
        self.start("a7")
        self.landed("c7")
        self.start("b7")
        self.landed("a6")
        self.landed("b6")
        if late is not None:
            late()
        for name in ("c8", "c9", "a7", "b7"):
            self.landed(name)
        keep.wait()
        for at, (name, direction, same, dz, half) in enumerate(self.MOVES):
            self.copy(name).wait_send()
            if direction == "y":
                block = (not same, dz)
            else:
                block = (same, dz + (-1 if direction == "up" else 1))
            mine = self.slot(self.block(*block), half)
            pltpu.make_async_copy(mine, mine, self.side_send.at[at]).wait()
            other = self.slot(self.block(*block, 1 - self.core), half)
            pltpu.make_async_copy(other, other, self.side_recv.at[at]).wait()
        side = self.side_own()
        side.wait_send()
        other = self.slot(self.block(True, 0, 1 - self.core), None)
        pltpu.make_async_copy(other, other, self.side_recv.at[self.COUNT]).wait()


def mixer_kernel(
    ids, tail, shard, table, gain, se, mr, weight_hbm, out,
    w, weight, tail_all, part, ids_all, sf, gf, query, mixf, mixed, send_buf, recv_buf, own_part, base, xs, xn,
    rim_send, rim_recv, far_send, far_recv,
    send, recv, side_send, side_recv, a2a_send, a2a_recv, x_send, x_recv,
    rs_send, rs_recv, ag_send, ag_recv, relay_send, relay_recv, halo_send, halo_recv, local,
):
    section = lax.axis_index("section")
    tensor = lax.axis_index("tensor")
    seq = lax.axis_index("seq")
    y, z, core = place()
    depth = tail.shape[2]
    vocab, width = table.shape
    wide = part.shape[1]
    count = tail.shape[1] // wide
    share = 3 * wide
    half = vocab // 2
    ways = w.shape[0]
    micro = gf.shape[0]
    tiles = gf.shape[1]
    length = gf.shape[2] // 2
    taps = mr.shape[0]
    short_taps = se.shape[1]
    lane = 128
    block = 256
    broad = 512
    pitch = length + 8
    chunks = ((0, 64), (64, pitch - 64), (pitch, 80), (pitch + 80, pitch - 80))
    fine = tuple((at, *chunk) for at, chunk in enumerate(chunks))
    coarse = ((0, 0, pitch),) + tuple((at - 1, *chunks[at]) for at in (2, 3))
    ahead = (tensor + 1 + core * (ways - 2)) % ways
    behind = (tensor + ways - 1 - core * (ways - 2)) % ways
    far = (tensor + 2) % ways
    barrier = pltpu.get_barrier_semaphore()

    def greet(**axes):
        pl.semaphore_signal(barrier, inc=1, device_id=axes, device_id_type=MESH)

    def remote(src, dst, send_sem, recv_sem, **axes):
        return pltpu.make_async_remote_copy(
            src_ref=src, dst_ref=dst, send_sem=send_sem, recv_sem=recv_sem,
            device_id=axes, device_id_type=MESH,
        )

    def arrival(ref, sem):
        pltpu.make_async_copy(ref, ref, sem).wait()

    def lanes(tile):
        return pl.ds(pl.multiple_of(tile * lane, lane), lane)

    def short(tile, stream, start, rows):
        total = jnp.zeros((rows, lane), jnp.float32)
        for tap in range(short_taps):
            total += se[stream, tap, :, lanes(tile)] * sf[
                stream, tile, start - tap : start - tap + rows, :
            ]
        return total

    def gate(mb, tile, start, rows, at):
        values = short(tile, 1, start, rows) * short(tile, 2, start, rows)
        gf[mb, tile, at : at + rows, :] = values.astype(jnp.bfloat16).astype(jnp.float32)

    def medium(mb, begin, rows):
        def one_tile(tile, carry):
            total = jnp.zeros((rows, lane), jnp.float32)
            first = length + begin - taps
            window = gf[mb, tile, first : first + rows + taps, :]
            for shift in range(8):
                part_sum = jnp.zeros((rows + 8, lane), jnp.float32)
                for step in range(taps // 8):
                    tap = 8 * step + shift
                    at = taps - 8 - 8 * step
                    part_sum += mr[tap : tap + 1, lanes(tile)] * window[at : at + rows + 8]
                total += part_sum[8 - shift : 8 - shift + rows]
            to = mb * pitch + begin
            mixf[to : to + rows, lanes(tile)] = query[mb, tile, begin : begin + rows] * total
            return carry

        lax.fori_loop(0, tiles, one_tile, 0)

    def partial_to(chunk, owner, finish):
        index, first, rows = chunk
        window = slice(first, first + rows)

        def one_block(at, carry):
            inner = pl.ds(pl.multiple_of(at * broad, broad), broad)
            outer = pl.ds(pl.multiple_of(owner * width + at * broad, broad), broad)
            term = jnp.dot(mixed[window], weight[:, outer], preferred_element_type=jnp.float32)
            finish(window, inner, term)
            return carry

        lax.fori_loop(0, width // broad, one_block, 0)

    def hop(chunk, at, to):
        index, first, rows = chunk
        window = slice(first, first + rows)
        return remote(
            send_buf.at[at, window], recv_buf.at[at, window],
            rs_send.at[index * 3 + at], rs_recv.at[index * 3 + at], tensor=to,
        )

    def fill(at):
        def finish(window, inner, term):
            send_buf[at, window, inner] = term.astype(jnp.bfloat16)

        return finish

    def reduce_start(chunk):
        index, first, rows = chunk
        window = slice(first, first + rows)
        mixed[window] = mixf[window].astype(jnp.bfloat16)
        partial_to(chunk, far, fill(0))
        hop(chunk, 0, ahead).start()
        partial_to(chunk, behind, fill(2))
        hop(chunk, 2, behind).start()

    def reduce_middle(chunk):
        hop(chunk, 0, ahead).wait_recv()

        def finish(window, inner, term):
            both = term + recv_buf[0, window, inner].astype(jnp.float32)
            send_buf[1, window, inner] = both.astype(jnp.bfloat16)

        partial_to(chunk, ahead, finish)
        hop(chunk, 1, ahead).start()

        def keep(window, inner, term):
            own_part[window, inner] = term

        partial_to(chunk, tensor, keep)

    def reduce_end(chunk):
        index, first, rows = chunk
        hop(chunk, 2, behind).wait_recv()
        hop(chunk, 1, ahead).wait_recv()
        lines = 16

        def add(at, carry):
            window = pl.ds(pl.multiple_of(first + at * lines, lines), lines)
            total = own_part[window] + recv_buf[1, window].astype(jnp.float32)
            total += recv_buf[2, window].astype(jnp.float32)
            out[window] = (base[window] + total).astype(jnp.bfloat16)
            return carry

        lax.fori_loop(0, rows // lines, add, 0)

    def reduce_close(pieces):
        for chunk in pieces:
            hop(chunk, 0, ahead).wait_send()
            hop(chunk, 1, ahead).wait_send()
            hop(chunk, 2, behind).wait_send()

    def relay(chunk):
        first, rows = chunks[chunk]
        window = slice(first, first + rows)
        return remote(
            out.at[window], xs.at[tensor, window],
            relay_send.at[chunk], relay_recv.at[chunk], section=1,
        )

    load_weight = pltpu.make_async_copy(weight_hbm, weight, local.at[2])

    @pl.when(section == 0)
    def _():
        greet(tensor=ahead)
        greet(tensor=behind)

        def greet_seq(step, carry):
            greet(seq=(seq + step) % count)
            return carry

        lax.fori_loop(1, count, greet_seq, 0)
        pl.semaphore_wait(barrier, count + 2)
        load_weight.start()

        ids_on = remote(
            ids, ids_all.at[:, 0:length], halo_send.at[0], halo_recv.at[0],
            seq=(seq + 1) % count,
        )

        @pl.when(seq < count - 1)
        def _():
            ids_on.start()

        @pl.when(seq == 0)
        def _():
            ids_all[:, 0:length] = jnp.full((micro, length, lane), -1, jnp.int32)

        rows = pl.ds(pl.multiple_of(core * half, half), half)

        def table_of(owner):
            return w.at[1 + owner // 2, owner % 2, 0:vocab]

        def along(at, src, owner, to):
            return remote(src, table_of(owner).at[rows], x_send.at[at], x_recv.at[at], tensor=to)

        def across(at, owner):
            piece = table_of(owner).at[rows]
            return remote(
                piece, piece, x_send.at[at], x_recv.at[at], seq=seq_of(y, z, 1 - core)
            )

        mine = table.at[rows]
        along(0, mine, tensor, ahead).start()
        along(1, mine, tensor, behind).start()
        keep = pltpu.make_async_copy(table, table_of(tensor), local.at[0])
        keep.start()

        def spread(step):
            to = (seq + step) % count
            return remote(
                tail.at[:, pl.ds(pl.multiple_of(to * wide, wide), wide)],
                tail_all.at[:, :, pl.ds(pl.multiple_of(seq * depth, depth), depth)],
                a2a_send.at[step], a2a_recv.at[step], seq=to,
            )

        def spread_start(step, carry):
            spread(step).start()
            return carry

        lax.fori_loop(1, count, spread_start, 0)
        keep_tail = pltpu.make_async_copy(
            tail.at[:, pl.ds(pl.multiple_of(seq * wide, wide), wide)],
            tail_all.at[:, :, pl.ds(pl.multiple_of(seq * depth, depth), depth)],
            local.at[1],
        )
        keep_tail.start()
        ids_all[:, length : 2 * length] = ids[...]

        along(0, mine, tensor, ahead).wait_recv()
        along(2, table_of(behind).at[rows], behind, ahead).start()
        across(3, behind).start()
        along(1, mine, tensor, behind).wait_recv()
        across(4, ahead).start()
        got = table_of(far).at[rows]
        arrival(got, x_recv.at[2])
        across(5, far).start()
        keep.wait()
        for at, owner in ((3, behind), (4, ahead), (5, far)):
            across(at, owner).wait_recv()
        along(0, mine, tensor, ahead).wait_send()
        along(1, mine, tensor, behind).wait_send()
        arrival(got, x_send.at[2])
        for at, owner in ((3, behind), (4, ahead), (5, far)):
            across(at, owner).wait_send()

        lines = 32

        def normalise(at, carry):
            window = pl.ds(pl.multiple_of(at * lines, lines), lines)
            total = jnp.zeros((lines, 1), jnp.float32)
            for way in range(ways):
                values = w[1 + way // 2, way % 2, window].astype(jnp.float32)
                total += jnp.sum(values * values, axis=1, keepdims=True)
            scale = lax.rsqrt(total / (ways * width) + EPS)
            for way in range(ways):
                values = w[1 + way // 2, way % 2, window].astype(jnp.float32)
                values = values * scale * gain[:, way * width : (way + 1) * width]
                w[1 + way // 2, way % 2, window] = values.astype(jnp.bfloat16)
            return carry

        lax.fori_loop(0, vocab // lines, normalise, 0)

        def spread_wait(step, carry):
            spread(step).wait_send()
            arrival(tail_all.at[:, :, pl.ds(0, depth)], a2a_recv.at[step])
            return carry

        lax.fori_loop(1, count, spread_wait, 0)
        keep_tail.wait()
        total = jnp.zeros((share, vocab), jnp.float32)
        for way in range(ways):
            total += lax.dot_general(
                tail_all[:, :, way * width : (way + 1) * width].reshape(share, width),
                w[1 + way // 2, way % 2, 0:vocab],
                (((1,), (1,)), ((), ())),
                preferred_element_type=jnp.float32,
            )
        for stream in range(3):
            part[stream] = total[stream * wide : (stream + 1) * wide].astype(jnp.bfloat16)

        def slot(owner, part_of):
            at, some = owner * wide, wide
            if part_of is not None:
                some = wide // 2
                at = at + part_of * some
            return w.at[0, :, pl.ds(pl.multiple_of(at, some), some), 0:vocab]

        Gather(slot, part, send, recv, side_send, side_recv).run(local.at[0])
        load_weight.wait()

        @pl.when(seq > 0)
        def _():
            ids_on.wait_recv()

        onehot = w.at[3, 0, 0 : 2 * length, 0:vocab]

        def streams(mb):
            for part_at in range(vocab // lane):
                number = lax.broadcasted_iota(jnp.int32, (2 * length, lane), 1) + part_at * lane
                hit = jnp.where(ids_all[mb] == number, 1.0, 0.0).astype(jnp.bfloat16)
                w[3, 0, 0 : 2 * length, part_at * lane : (part_at + 1) * lane] = hit

            def one_block(at, carry):
                stream, inner = at // (width // block), at % (width // block)
                columns = pl.ds(pl.multiple_of(inner * block, block), block)
                values = lax.dot_general(
                    onehot[...],
                    w[0, stream, columns, 0:vocab],
                    (((1,), (1,)), ((), ())),
                    preferred_element_type=jnp.float32,
                ).astype(jnp.bfloat16).astype(jnp.float32)
                for side in range(block // lane):
                    sf[stream, inner * (block // lane) + side, 8 : 8 + 2 * length, :] = values[
                        :, side * lane : (side + 1) * lane
                    ]
                return carry

            lax.fori_loop(0, 3 * width // block, one_block, 0)

            def own_rows(at, carry):
                columns = pl.ds(pl.multiple_of(at * block, block), block)
                values = jnp.dot(
                    onehot[...], table[:, columns], preferred_element_type=jnp.float32
                )
                base[mb * pitch : mb * pitch + length, columns] = values[length : 2 * length]
                return carry

            lax.fori_loop(0, width // block, own_rows, 0)

            def one_tile(tile, carry):
                query[mb, tile] = short(tile, 0, 8 + length, length)
                gate(mb, tile, 8, length, 0)
                gate(mb, tile, 8 + length, length, length)
                return carry

            lax.fori_loop(0, tiles, one_tile, 0)

        sf[:, :, 0:8, :] = jnp.zeros((3, tiles, 8, lane), jnp.float32)
        def pass_on(chunk):
            reduce_end(fine[chunk])
            relay(chunk).start()

        streams(0)
        medium(0, 0, 64)
        reduce_start(fine[0])
        medium(0, 64, length - 64)
        reduce_start(fine[1])
        reduce_middle(fine[0])
        streams(1)
        reduce_middle(fine[1])
        pass_on(0)
        medium(1, 0, 80)
        reduce_start(fine[2])
        pass_on(1)
        medium(1, 80, length - 80)
        reduce_start(fine[3])
        reduce_middle(fine[2])
        reduce_middle(fine[3])
        pass_on(2)
        pass_on(3)
        reduce_close(fine)
        for chunk in range(len(chunks)):
            relay(chunk).wait_send()

        @pl.when(seq < count - 1)
        def _():
            ids_on.wait_send()

    @pl.when(section == 1)
    def _():
        greet(seq=seq_of(y, (z + 1) % RING, core))
        greet(seq=seq_of(y, (z + RING - 1) % RING, core))
        greet(seq=seq_of(1 - y, z, core))
        greet(seq=seq_of(y, z, 1 - core))
        greet(tensor=ahead)
        greet(tensor=behind)
        greet(section=0)

        @pl.when(seq > 0)
        def _():
            greet(seq=(seq + count - 1) % count)

        @pl.when(seq < count - 1)
        def _():
            pl.semaphore_wait(barrier, 7)

        @pl.when(seq == count - 1)
        def _():
            pl.semaphore_wait(barrier, 6)

        load_weight.start()
        per = width // depth

        def slot(owner, part_of):
            at, some = (owner % per) * depth, depth
            if part_of is not None:
                some = depth // 2
                at = at + part_of * some
            return w.at[owner // per, :, pl.ds(pl.multiple_of(at, some), some)]

        def share_out(chunk, at, owner, to):
            first, rows = chunks[chunk]
            piece = xs.at[owner, first : first + rows]
            return remote(
                piece, piece, ag_send.at[chunk * 3 + at], ag_recv.at[chunk * 3 + at], tensor=to
            )

        def gather_start(chunk):
            first, rows = chunks[chunk]
            arrival(xs.at[tensor, first : first + rows], relay_recv.at[chunk])
            share_out(chunk, 0, tensor, ahead).start()
            share_out(chunk, 1, tensor, behind).start()

        def gather_middle(chunk):
            first, rows = chunks[chunk]
            arrival(xs.at[behind, first : first + rows], ag_recv.at[chunk * 3])
            share_out(chunk, 2, behind, ahead).start()

        def gather_end(chunk):
            first, rows = chunks[chunk]
            arrival(xs.at[ahead, first : first + rows], ag_recv.at[chunk * 3 + 1])
            arrival(xs.at[far, first : first + rows], ag_recv.at[chunk * 3 + 2])

        def gather_close():
            for chunk in range(len(chunks)):
                share_out(chunk, 0, tensor, ahead).wait_send()
                share_out(chunk, 1, tensor, behind).wait_send()
                share_out(chunk, 2, behind, ahead).wait_send()

        def project(group):
            first, rows = group * pitch, pitch
            lines = 16

            def normalise(at, carry):
                window = pl.ds(pl.multiple_of(first + at * lines, lines), lines)
                total = jnp.zeros((lines, 1), jnp.float32)
                for way in range(ways):
                    values = xs[way, window].astype(jnp.float32)
                    total += jnp.sum(values * values, axis=1, keepdims=True)
                scale = lax.rsqrt(total / (ways * width) + EPS)
                for way in range(ways):
                    values = xs[way, window].astype(jnp.float32)
                    values = values * scale * gain[:, way * width : (way + 1) * width]
                    xn[way, window] = values.astype(jnp.bfloat16)
                base[window] = xs[tensor, window].astype(jnp.float32)
                return carry

            lax.fori_loop(0, rows // lines, normalise, 0)

            def one_block(at, carry):
                stream, inner = at // (width // block), at % (width // block)
                columns = pl.ds(pl.multiple_of(inner * block, block), block)
                total = jnp.zeros((rows, block), jnp.float32)
                for way in range(ways):
                    total += jnp.dot(
                        xn[way, first : first + rows],
                        w[way, stream, :, columns],
                        preferred_element_type=jnp.float32,
                    )
                total = total.astype(jnp.bfloat16).astype(jnp.float32)
                for side in range(block // lane):
                    tile = inner * (block // lane) + side
                    piece = total[:, side * lane : (side + 1) * lane]
                    sf[stream, tile, first + 8 : first + 8 + length, :] = piece[0:length]
                return carry

            lax.fori_loop(0, 3 * width // block, one_block, 0)

        def rim(mb):
            return remote(
                rim_send.at[mb], rim_recv.at[mb], halo_send.at[mb], halo_recv.at[mb],
                seq=(seq + 1) % count,
            )

        def gated_rim(mb):
            return remote(
                far_send.at[mb], far_recv.at[mb], halo_send.at[micro + mb], halo_recv.at[micro + mb],
                seq=(seq + 1) % count,
            )

        def rim_start(mb):
            last = (mb + 1) * pitch
            rim_send[mb] = sf[:, :, last - 16 : last, :].astype(jnp.bfloat16)

            @pl.when(seq < count - 1)
            def _():
                rim(mb).start()

        def shorts(mb):
            first = mb * pitch

            @pl.when(seq > 0)
            def _():
                rim(mb).wait_recv()
                sf[:, :, first : first + 8, :] = rim_recv[mb].astype(jnp.float32)[:, :, 8:16]

            @pl.when(seq == 0)
            def _():
                sf[:, :, first : first + 8, :] = jnp.zeros((3, tiles, 8, lane), jnp.float32)

            def one_tile(tile, carry):
                query[mb, tile] = short(tile, 0, first + 8, length)
                gate(mb, tile, first + 8, length, length)
                far_send[mb, tile] = gf[mb, tile, 2 * length - taps : 2 * length, :].astype(
                    jnp.bfloat16
                )
                return carry

            lax.fori_loop(0, tiles, one_tile, 0)

            @pl.when(seq < count - 1)
            def _():
                gated_rim(mb).start()

        def gated_end(mb):
            @pl.when(seq > 0)
            def _():
                gated_rim(mb).wait_recv()

                def one_tile(tile, carry):
                    gf[mb, tile, length - taps : length, :] = far_recv[mb, tile].astype(
                        jnp.float32
                    )
                    return carry

                lax.fori_loop(0, tiles, one_tile, 0)

            @pl.when(seq == 0)
            def _():
                gf[mb, :, 0:length, :] = jnp.zeros((tiles, length, lane), jnp.float32)

        def early():
            gather_start(0)
            gather_middle(0)
            gather_start(1)

        Gather(slot, shard, send, recv, side_send, side_recv).run(local.at[0], early)
        load_weight.wait()
        gather_middle(1)
        gather_end(0)
        gather_end(1)
        project(0)
        rim_start(0)
        gather_start(2)
        shorts(0)
        gather_middle(2)
        gather_start(3)
        gated_end(0)
        medium(0, 0, 64)
        gather_middle(3)
        medium(0, 64, length - 64)
        reduce_start(coarse[0])
        gather_end(2)
        gather_end(3)
        project(1)
        rim_start(1)
        reduce_middle(coarse[0])
        shorts(1)
        gated_end(1)
        medium(1, 0, 80)
        reduce_start(coarse[1])
        medium(1, 80, length - 80)
        reduce_start(coarse[2])
        reduce_middle(coarse[1])
        reduce_middle(coarse[2])
        reduce_end(coarse[0])
        reduce_end(coarse[1])
        reduce_end(coarse[2])
        reduce_close(coarse)
        gather_close()

        @pl.when(seq < count - 1)
        def _():
            for mb in range(micro):
                rim(mb).wait_send()
                gated_rim(mb).wait_send()


def body(token_ids, embed_table, norm_gain, in_weight, se_filter, mr_filter, out_weight):
    micro, length = token_ids.shape
    vocab, width = embed_table.shape
    full = norm_gain.shape[1]
    count = lax.axis_size("seq")
    ways = full // width
    lane = 128
    tiles = width // lane
    rows = micro * (length + 8)
    taps = mr_filter.shape[1]
    depth = in_weight.shape[1]
    wide = width // count
    shard = in_weight[0].transpose(1, 0, 2)
    tail = shard.transpose(0, 2, 1)
    ids = jnp.broadcast_to(token_ids[:, :, None], (micro, length, lane))
    moves = Gather.COUNT
    bf16, f32 = jnp.bfloat16, jnp.float32
    scratch, dma = pltpu.VMEM, pltpu.SemaphoreType.DMA
    result = pl.pallas_call(
        mixer_kernel,
        out_shape=jax.ShapeDtypeStruct((rows, width), bf16),
        in_specs=[VMEM, HBM, HBM, VMEM, VMEM, VMEM, VMEM, HBM],
        out_specs=VMEM,
        scratch_shapes=[
            scratch((ways, 3, width, width), bf16),
            scratch((width, full), bf16),
            scratch((3, wide, full), bf16),
            scratch((3, wide, vocab), bf16),
            scratch((micro, 2 * length, lane), jnp.int32),
            scratch((3, tiles, 2 * length + 16, lane), f32),
            scratch((micro, tiles, 2 * length, lane), f32),
            scratch((micro, tiles, length, lane), f32),
            scratch((rows, width), f32),
            scratch((rows, width), bf16),
            scratch((3, rows, width), bf16),
            scratch((3, rows, width), bf16),
            scratch((rows, width), f32),
            scratch((rows, width), f32),
            scratch((ways, rows, width), bf16),
            scratch((ways, rows, width), bf16),
            scratch((micro, 3, tiles, 16, lane), bf16),
            scratch((micro, 3, tiles, 16, lane), bf16),
            scratch((micro, tiles, taps, lane), bf16),
            scratch((micro, tiles, taps, lane), bf16),
            dma((moves,)),
            dma((moves,)),
            dma((moves + 1,)),
            dma((moves + 1,)),
            dma((count,)),
            dma((count,)),
            dma((6,)),
            dma((6,)),
            dma((12,)),
            dma((12,)),
            dma((12,)),
            dma((12,)),
            dma((4,)),
            dma((4,)),
            dma((2 * micro,)),
            dma((2 * micro,)),
            dma((3,)),
        ],
        compiler_params=pltpu.CompilerParams(
            collective_id=0, has_side_effects=True, vmem_limit_bytes=60 << 20
        ),
        name="mixer",
    )(ids, tail, shard, embed_table, norm_gain, se_filter[0][:, :, None], mr_filter[0], out_weight[0])
    return result.reshape(1, micro, length + 8, width)[:, :, :length]


def solution(mesh):
    in_specs = (
        P(None, "seq"),
        P(None, "tensor"),
        P("section", None),
        P("section", "seq", None, "tensor"),
        P("section", None, None, "tensor"),
        P("section", None, "tensor"),
        P("section", "tensor", None),
    )
    out_specs = P("section", None, "seq", "tensor")
    return jax.shard_map(body, mesh=mesh, in_specs=in_specs, out_specs=out_specs, check_vma=False)
```

```python
import functools

import jax
import jax.numpy as jnp
from jax import lax
from jax.experimental import pallas as pl
from jax.experimental.pallas import tpu as pltpu
from jax.sharding import PartitionSpec as P

EPS = 1e-06
MESH = pl.DeviceIdType.MESH
RING = 8
VMEM = pl.BlockSpec(memory_space=pltpu.VMEM)
HBM = pl.BlockSpec(memory_space=pltpu.HBM)


def place():
    seq = lax.axis_index("seq")
    return seq // (2 * RING), (seq // 2) % RING, seq % 2


def seq_of(y, z, core):
    return (y * RING + z) * 2 + core


class Gather:
    MOVES = (
        ("a1", "up", True, 0, None),
        ("b1", "down", True, 0, None),
        ("c1", "y", True, 0, None),
        ("a2", "up", True, -1, None),
        ("b2", "down", True, 1, None),
        ("c2", "y", True, -1, 1),
        ("c3", "y", True, 1, 0),
        ("a3", "up", True, -2, None),
        ("b3", "down", True, 2, None),
        ("c4", "y", True, -2, 1),
        ("c5", "y", True, 2, 0),
        ("a4", "up", True, -3, 0),
        ("b4", "down", True, 3, 1),
        ("c6", "y", True, -3, 0),
        ("c7", "y", True, 3, 1),
        ("a5", "up", False, 0, 0),
        ("b5", "down", False, 0, 1),
        ("c8", "y", True, -3, 1),
        ("c9", "y", True, 3, 0),
        ("a6", "up", False, -1, 0),
        ("b6", "down", False, 1, 1),
        ("a7", "up", False, -3, 0),
        ("b7", "down", False, 3, 1),
    )
    COUNT = len(MOVES)

    def __init__(self, slot, own, send, recv, side_send, side_recv):
        self.y, self.z, self.core = place()
        self.slot, self.own = slot, own
        self.send, self.recv = send, recv
        self.side_send, self.side_recv = side_send, side_recv
        self.index = {move[0]: at for at, move in enumerate(self.MOVES)}
        self.pending = []

    def target(self, direction):
        if direction == "up":
            return seq_of(self.y, (self.z + 1) % RING, self.core)
        if direction == "down":
            return seq_of(self.y, (self.z + RING - 1) % RING, self.core)
        return seq_of(1 - self.y, self.z, self.core)

    def block(self, same, dz, core=None):
        y = self.y if same else 1 - self.y
        return seq_of(y, (self.z + dz + RING) % RING, self.core if core is None else core)

    def copy(self, name):
        at = self.index[name]
        _, direction, same, dz, half = self.MOVES[at]
        block = self.block(same, dz)
        dst = self.slot(block, half)
        src = self.own if same and dz == 0 else dst
        return pltpu.make_async_remote_copy(
            src_ref=src,
            dst_ref=dst,
            send_sem=self.send.at[at],
            recv_sem=self.recv.at[at],
            device_id={"seq": self.target(direction)},
            device_id_type=MESH,
        )

    def start(self, *names):
        for name in names:
            self.copy(name).start()

    def landed(self, name):
        at = self.index[name]
        _, direction, same, dz, half = self.MOVES[at]
        if direction == "y":
            block = self.block(not same, dz)
        else:
            block = self.block(same, dz + (-1 if direction == "up" else 1))
        got = self.slot(block, half)
        pltpu.make_async_copy(got, got, self.recv.at[at]).wait()
        side = pltpu.make_async_remote_copy(
            src_ref=got,
            dst_ref=got,
            send_sem=self.side_send.at[at],
            recv_sem=self.side_recv.at[at],
            device_id={"seq": seq_of(self.y, self.z, 1 - self.core)},
            device_id_type=MESH,
        )
        side.start()

    def side_own(self):
        return pltpu.make_async_remote_copy(
            src_ref=self.own,
            dst_ref=self.slot(self.block(True, 0), None),
            send_sem=self.side_send.at[self.COUNT],
            recv_sem=self.side_recv.at[self.COUNT],
            device_id={"seq": seq_of(self.y, self.z, 1 - self.core)},
            device_id_type=MESH,
        )

    def run(self, local_sem, late=None):
        keep = pltpu.make_async_copy(self.own, self.slot(self.block(True, 0), None), local_sem)
        self.start("a1", "b1", "c1")
        self.side_own().start()
        keep.start()
        self.landed("a1")
        self.start("a2", "c2")
        self.landed("b1")
        self.start("b2", "c3")
        self.landed("c1")
        self.landed("a2")
        self.start("a3", "c4")
        self.landed("b2")
        self.start("b3", "c5")
        self.landed("c2")
        self.landed("c3")
        self.landed("a3")
        self.start("a4", "c6", "a5")
        self.landed("b3")
        self.start("b4", "c7", "b5")
        for name in ("c4", "c5", "a4", "b4"):
            self.landed(name)
        self.start("c8", "c9")
        self.landed("a5")
        self.start("a6")
        self.landed("b5")
        self.start("b6")
        self.landed("c6")
        self.start("a7")
        self.landed("c7")
        self.start("b7")
        self.landed("a6")
        self.landed("b6")
        if late is not None:
            late()
        for name in ("c8", "c9", "a7", "b7"):
            self.landed(name)
        keep.wait()
        for at, (name, direction, same, dz, half) in enumerate(self.MOVES):
            self.copy(name).wait_send()
            if direction == "y":
                block = (not same, dz)
            else:
                block = (same, dz + (-1 if direction == "up" else 1))
            mine = self.slot(self.block(*block), half)
            pltpu.make_async_copy(mine, mine, self.side_send.at[at]).wait()
            other = self.slot(self.block(*block, 1 - self.core), half)
            pltpu.make_async_copy(other, other, self.side_recv.at[at]).wait()
        side = self.side_own()
        side.wait_send()
        other = self.slot(self.block(True, 0, 1 - self.core), None)
        pltpu.make_async_copy(other, other, self.side_recv.at[self.COUNT]).wait()


def mixer_kernel(
    ids, shard, table, gain, se, mr, weight_hbm, out,
    w, weight, tail_all, part, ids_all, sf, gf, query, mixf, mixed, send_buf, recv_buf, own_part, base, xs, xn,
    rim_send, rim_recv, far_send, far_recv,
    send, recv, side_send, side_recv, a2a_send, a2a_recv, x_send, x_recv,
    rs_send, rs_recv, ag_send, ag_recv, relay_send, relay_recv, halo_send, halo_recv, local,
):
    section = lax.axis_index("section")
    tensor = lax.axis_index("tensor")
    seq = lax.axis_index("seq")
    y, z, core = place()
    depth = shard.shape[1]
    vocab, width = table.shape
    wide = part.shape[1]
    count = width // wide
    share = 3 * wide
    half = vocab // 2
    ways = w.shape[0]
    micro = gf.shape[0]
    tiles = gf.shape[1]
    length = gf.shape[2] // 2
    taps = mr.shape[0]
    short_taps = se.shape[1]
    lane = 128
    block = 256
    broad = 512
    pitch = length + 8
    chunks = ((0, 64), (64, pitch - 64), (pitch, 80), (pitch + 80, pitch - 80))
    fine = tuple((at, *chunk) for at, chunk in enumerate(chunks))
    coarse = ((0, 0, pitch),) + tuple((at - 1, *chunks[at]) for at in (2, 3))
    ahead = (tensor + 1 + core * (ways - 2)) % ways
    behind = (tensor + ways - 1 - core * (ways - 2)) % ways
    far = (tensor + 2) % ways
    barrier = pltpu.get_barrier_semaphore()

    def greet(**axes):
        pl.semaphore_signal(barrier, inc=1, device_id=axes, device_id_type=MESH)

    def remote(src, dst, send_sem, recv_sem, **axes):
        return pltpu.make_async_remote_copy(
            src_ref=src, dst_ref=dst, send_sem=send_sem, recv_sem=recv_sem,
            device_id=axes, device_id_type=MESH,
        )

    def arrival(ref, sem):
        pltpu.make_async_copy(ref, ref, sem).wait()

    def lanes(tile):
        return pl.ds(pl.multiple_of(tile * lane, lane), lane)

    def short(tile, stream, start, rows):
        total = jnp.zeros((rows, lane), jnp.float32)
        for tap in range(short_taps):
            total += se[stream, tap, :, lanes(tile)] * sf[
                stream, tile, start - tap : start - tap + rows, :
            ]
        return total

    def gate(mb, tile, start, rows, at):
        values = short(tile, 1, start, rows) * short(tile, 2, start, rows)
        gf[mb, tile, at : at + rows, :] = values.astype(jnp.bfloat16).astype(jnp.float32)

    def medium(mb, begin, rows):
        def one_tile(tile, carry):
            total = jnp.zeros((rows, lane), jnp.float32)
            first = length + begin - taps
            window = gf[mb, tile, first : first + rows + taps, :]
            for shift in range(8):
                part_sum = jnp.zeros((rows + 8, lane), jnp.float32)
                for step in range(taps // 8):
                    tap = 8 * step + shift
                    at = taps - 8 - 8 * step
                    part_sum += mr[tap : tap + 1, lanes(tile)] * window[at : at + rows + 8]
                total += part_sum[8 - shift : 8 - shift + rows]
            to = mb * pitch + begin
            mixf[to : to + rows, lanes(tile)] = query[mb, tile, begin : begin + rows] * total
            return carry

        lax.fori_loop(0, tiles, one_tile, 0)

    def partial_to(chunk, owner, finish):
        index, first, rows = chunk
        window = slice(first, first + rows)

        def one_block(at, carry):
            inner = pl.ds(pl.multiple_of(at * broad, broad), broad)
            outer = pl.ds(pl.multiple_of(owner * width + at * broad, broad), broad)
            term = jnp.dot(mixed[window], weight[:, outer], preferred_element_type=jnp.float32)
            finish(window, inner, term)
            return carry

        lax.fori_loop(0, width // broad, one_block, 0)

    def hop(chunk, at, to):
        index, first, rows = chunk
        window = slice(first, first + rows)
        return remote(
            send_buf.at[at, window], recv_buf.at[at, window],
            rs_send.at[index * 3 + at], rs_recv.at[index * 3 + at], tensor=to,
        )

    def fill(at):
        def finish(window, inner, term):
            send_buf[at, window, inner] = term.astype(jnp.bfloat16)

        return finish

    def reduce_start(chunk):
        index, first, rows = chunk
        window = slice(first, first + rows)
        mixed[window] = mixf[window].astype(jnp.bfloat16)
        partial_to(chunk, far, fill(0))
        hop(chunk, 0, ahead).start()
        partial_to(chunk, behind, fill(2))
        hop(chunk, 2, behind).start()

    def reduce_middle(chunk):
        hop(chunk, 0, ahead).wait_recv()

        def finish(window, inner, term):
            both = term + recv_buf[0, window, inner].astype(jnp.float32)
            send_buf[1, window, inner] = both.astype(jnp.bfloat16)

        partial_to(chunk, ahead, finish)
        hop(chunk, 1, ahead).start()

        def keep(window, inner, term):
            own_part[window, inner] = term

        partial_to(chunk, tensor, keep)

    def reduce_end(chunk):
        index, first, rows = chunk
        hop(chunk, 2, behind).wait_recv()
        hop(chunk, 1, ahead).wait_recv()
        lines = 16

        def add(at, carry):
            window = pl.ds(pl.multiple_of(first + at * lines, lines), lines)
            total = own_part[window] + recv_buf[1, window].astype(jnp.float32)
            total += recv_buf[2, window].astype(jnp.float32)
            out[window] = (base[window] + total).astype(jnp.bfloat16)
            return carry

        lax.fori_loop(0, rows // lines, add, 0)

    def reduce_close(pieces):
        for chunk in pieces:
            hop(chunk, 0, ahead).wait_send()
            hop(chunk, 1, ahead).wait_send()
            hop(chunk, 2, behind).wait_send()

    def relay(chunk):
        first, rows = chunks[chunk]
        window = slice(first, first + rows)
        return remote(
            out.at[window], xs.at[tensor, window],
            relay_send.at[chunk], relay_recv.at[chunk], section=1,
        )

    load_weight = pltpu.make_async_copy(weight_hbm, weight, local.at[2])

    @pl.when(section == 0)
    def _():
        greet(tensor=ahead)
        greet(tensor=behind)

        def greet_seq(step, carry):
            greet(seq=(seq + step) % count)
            return carry

        load_shard = pltpu.make_async_copy(shard, xn.at[0:3, 0:depth], local.at[0])
        load_shard.start()
        lax.fori_loop(1, count, greet_seq, 0)
        load_shard.wait()
        tail = w.at[3, :, :, vocab : vocab + depth]
        for stream in range(3):
            w[3, stream, :, vocab : vocab + depth] = xn[stream, 0:depth].T
        for mb in range(micro):
            for begin, rows in ((0, lane), (lane, length - lane)):
                line = ids[mb : mb + 1, begin : begin + rows]
                ids_all[mb, length + begin : length + begin + rows] = jnp.broadcast_to(
                    line, (lane, rows)
                ).T
        pl.semaphore_wait(barrier, count + 2)
        load_weight.start()

        ids_on = remote(
            ids_all.at[:, length : 2 * length], ids_all.at[:, 0:length], halo_send.at[0], halo_recv.at[0],
            seq=(seq + 1) % count,
        )

        @pl.when(seq < count - 1)
        def _():
            ids_on.start()

        @pl.when(seq == 0)
        def _():
            ids_all[:, 0:length] = jnp.full((micro, length, lane), -1, jnp.int32)

        rows = pl.ds(pl.multiple_of(core * half, half), half)

        def table_of(owner):
            return w.at[1 + owner // 2, owner % 2, 0:vocab]

        def along(at, src, owner, to):
            return remote(src, table_of(owner).at[rows], x_send.at[at], x_recv.at[at], tensor=to)

        def across(at, owner):
            piece = table_of(owner).at[rows]
            return remote(
                piece, piece, x_send.at[at], x_recv.at[at], seq=seq_of(y, z, 1 - core)
            )

        mine = table.at[rows]
        along(0, mine, tensor, ahead).start()
        along(1, mine, tensor, behind).start()
        keep = pltpu.make_async_copy(table, table_of(tensor), local.at[0])
        keep.start()

        def spread(step):
            to = (seq + step) % count
            return remote(
                tail.at[:, pl.ds(pl.multiple_of(to * wide, wide), wide)],
                tail_all.at[:, :, pl.ds(pl.multiple_of(seq * depth, depth), depth)],
                a2a_send.at[step], a2a_recv.at[step], seq=to,
            )

        def spread_start(step, carry):
            spread(step).start()
            return carry

        lax.fori_loop(1, count, spread_start, 0)
        keep_tail = pltpu.make_async_copy(
            tail.at[:, pl.ds(pl.multiple_of(seq * wide, wide), wide)],
            tail_all.at[:, :, pl.ds(pl.multiple_of(seq * depth, depth), depth)],
            local.at[1],
        )
        keep_tail.start()

        along(0, mine, tensor, ahead).wait_recv()
        along(2, table_of(behind).at[rows], behind, ahead).start()
        across(3, behind).start()
        along(1, mine, tensor, behind).wait_recv()
        across(4, ahead).start()
        got = table_of(far).at[rows]
        arrival(got, x_recv.at[2])
        across(5, far).start()
        keep.wait()
        for at, owner in ((3, behind), (4, ahead), (5, far)):
            across(at, owner).wait_recv()
        along(0, mine, tensor, ahead).wait_send()
        along(1, mine, tensor, behind).wait_send()
        arrival(got, x_send.at[2])
        for at, owner in ((3, behind), (4, ahead), (5, far)):
            across(at, owner).wait_send()

        lines = 32

        def normalise(at, carry):
            window = pl.ds(pl.multiple_of(at * lines, lines), lines)
            total = jnp.zeros((lines, 1), jnp.float32)
            for way in range(ways):
                values = w[1 + way // 2, way % 2, window].astype(jnp.float32)
                total += jnp.sum(values * values, axis=1, keepdims=True)
            scale = lax.rsqrt(total / (ways * width) + EPS)
            for way in range(ways):
                values = w[1 + way // 2, way % 2, window].astype(jnp.float32)
                values = values * scale * gain[:, way * width : (way + 1) * width]
                w[1 + way // 2, way % 2, window] = values.astype(jnp.bfloat16)
            return carry

        lax.fori_loop(0, vocab // lines, normalise, 0)

        def spread_wait(step, carry):
            spread(step).wait_send()
            arrival(tail_all.at[:, :, pl.ds(0, depth)], a2a_recv.at[step])
            return carry

        lax.fori_loop(1, count, spread_wait, 0)
        keep_tail.wait()
        total = jnp.zeros((share, vocab), jnp.float32)
        for way in range(ways):
            total += lax.dot_general(
                tail_all[:, :, way * width : (way + 1) * width].reshape(share, width),
                w[1 + way // 2, way % 2, 0:vocab],
                (((1,), (1,)), ((), ())),
                preferred_element_type=jnp.float32,
            )
        for stream in range(3):
            part[stream] = total[stream * wide : (stream + 1) * wide].astype(jnp.bfloat16)

        def slot(owner, part_of):
            at, some = owner * wide, wide
            if part_of is not None:
                some = wide // 2
                at = at + part_of * some
            return w.at[0, :, pl.ds(pl.multiple_of(at, some), some), 0:vocab]

        Gather(slot, part, send, recv, side_send, side_recv).run(local.at[0])
        load_weight.wait()

        @pl.when(seq > 0)
        def _():
            ids_on.wait_recv()

        onehot = w.at[3, 0, 0 : 2 * length, 0:vocab]

        def streams(mb):
            for part_at in range(vocab // lane):
                number = lax.broadcasted_iota(jnp.int32, (2 * length, lane), 1) + part_at * lane
                hit = jnp.where(ids_all[mb] == number, 1.0, 0.0).astype(jnp.bfloat16)
                w[3, 0, 0 : 2 * length, part_at * lane : (part_at + 1) * lane] = hit

            def one_block(at, carry):
                stream, inner = at // (width // block), at % (width // block)
                columns = pl.ds(pl.multiple_of(inner * block, block), block)
                values = lax.dot_general(
                    onehot[...],
                    w[0, stream, columns, 0:vocab],
                    (((1,), (1,)), ((), ())),
                    preferred_element_type=jnp.float32,
                ).astype(jnp.bfloat16).astype(jnp.float32)
                for side in range(block // lane):
                    sf[stream, inner * (block // lane) + side, 8 : 8 + 2 * length, :] = values[
                        :, side * lane : (side + 1) * lane
                    ]
                return carry

            lax.fori_loop(0, 3 * width // block, one_block, 0)

            def own_rows(at, carry):
                columns = pl.ds(pl.multiple_of(at * block, block), block)
                values = jnp.dot(
                    onehot[...], table[:, columns], preferred_element_type=jnp.float32
                )
                base[mb * pitch : mb * pitch + length, columns] = values[length : 2 * length]
                return carry

            lax.fori_loop(0, width // block, own_rows, 0)

            def one_tile(tile, carry):
                query[mb, tile] = short(tile, 0, 8 + length, length)
                gate(mb, tile, 8, length, 0)
                gate(mb, tile, 8 + length, length, length)
                return carry

            lax.fori_loop(0, tiles, one_tile, 0)

        sf[:, :, 0:8, :] = jnp.zeros((3, tiles, 8, lane), jnp.float32)
        def pass_on(chunk):
            reduce_end(fine[chunk])
            relay(chunk).start()

        streams(0)
        medium(0, 0, 64)
        reduce_start(fine[0])
        medium(0, 64, length - 64)
        reduce_start(fine[1])
        reduce_middle(fine[0])
        streams(1)
        reduce_middle(fine[1])
        pass_on(0)
        medium(1, 0, 80)
        reduce_start(fine[2])
        pass_on(1)
        medium(1, 80, length - 80)
        reduce_start(fine[3])
        reduce_middle(fine[2])
        reduce_middle(fine[3])
        pass_on(2)
        pass_on(3)
        reduce_close(fine)
        for chunk in range(len(chunks)):
            relay(chunk).wait_send()

        @pl.when(seq < count - 1)
        def _():
            ids_on.wait_send()

    @pl.when(section == 1)
    def _():
        greet(seq=seq_of(y, (z + 1) % RING, core))
        greet(seq=seq_of(y, (z + RING - 1) % RING, core))
        greet(seq=seq_of(1 - y, z, core))
        greet(seq=seq_of(y, z, 1 - core))
        greet(tensor=ahead)
        greet(tensor=behind)
        greet(section=0)

        @pl.when(seq > 0)
        def _():
            greet(seq=(seq + count - 1) % count)

        @pl.when(seq < count - 1)
        def _():
            pl.semaphore_wait(barrier, 7)

        @pl.when(seq == count - 1)
        def _():
            pl.semaphore_wait(barrier, 6)

        load_weight.start()
        per = width // depth

        def slot(owner, part_of):
            at, some = (owner % per) * depth, depth
            if part_of is not None:
                some = depth // 2
                at = at + part_of * some
            return w.at[owner // per, :, pl.ds(pl.multiple_of(at, some), some)]

        def share_out(chunk, at, owner, to):
            first, rows = chunks[chunk]
            piece = xs.at[owner, first : first + rows]
            return remote(
                piece, piece, ag_send.at[chunk * 3 + at], ag_recv.at[chunk * 3 + at], tensor=to
            )

        def gather_start(chunk):
            first, rows = chunks[chunk]
            arrival(xs.at[tensor, first : first + rows], relay_recv.at[chunk])
            share_out(chunk, 0, tensor, ahead).start()
            share_out(chunk, 1, tensor, behind).start()

        def gather_middle(chunk):
            first, rows = chunks[chunk]
            arrival(xs.at[behind, first : first + rows], ag_recv.at[chunk * 3])
            share_out(chunk, 2, behind, ahead).start()

        def gather_end(chunk):
            first, rows = chunks[chunk]
            arrival(xs.at[ahead, first : first + rows], ag_recv.at[chunk * 3 + 1])
            arrival(xs.at[far, first : first + rows], ag_recv.at[chunk * 3 + 2])

        def gather_close():
            for chunk in range(len(chunks)):
                share_out(chunk, 0, tensor, ahead).wait_send()
                share_out(chunk, 1, tensor, behind).wait_send()
                share_out(chunk, 2, behind, ahead).wait_send()

        def project(group):
            first, rows = group * pitch, pitch
            lines = 16

            def normalise(at, carry):
                window = pl.ds(pl.multiple_of(first + at * lines, lines), lines)
                total = jnp.zeros((lines, 1), jnp.float32)
                for way in range(ways):
                    values = xs[way, window].astype(jnp.float32)
                    total += jnp.sum(values * values, axis=1, keepdims=True)
                scale = lax.rsqrt(total / (ways * width) + EPS)
                for way in range(ways):
                    values = xs[way, window].astype(jnp.float32)
                    values = values * scale * gain[:, way * width : (way + 1) * width]
                    xn[way, window] = values.astype(jnp.bfloat16)
                base[window] = xs[tensor, window].astype(jnp.float32)
                return carry

            lax.fori_loop(0, rows // lines, normalise, 0)

            def one_block(at, carry):
                stream, inner = at // (width // block), at % (width // block)
                columns = pl.ds(pl.multiple_of(inner * block, block), block)
                total = jnp.zeros((rows, block), jnp.float32)
                for way in range(ways):
                    total += jnp.dot(
                        xn[way, first : first + rows],
                        w[way, stream, :, columns],
                        preferred_element_type=jnp.float32,
                    )
                total = total.astype(jnp.bfloat16).astype(jnp.float32)
                for side in range(block // lane):
                    tile = inner * (block // lane) + side
                    piece = total[:, side * lane : (side + 1) * lane]
                    sf[stream, tile, first + 8 : first + 8 + length, :] = piece[0:length]
                return carry

            lax.fori_loop(0, 3 * width // block, one_block, 0)

        def rim(mb):
            return remote(
                rim_send.at[mb], rim_recv.at[mb], halo_send.at[mb], halo_recv.at[mb],
                seq=(seq + 1) % count,
            )

        def gated_rim(mb):
            return remote(
                far_send.at[mb], far_recv.at[mb], halo_send.at[micro + mb], halo_recv.at[micro + mb],
                seq=(seq + 1) % count,
            )

        def rim_start(mb):
            last = (mb + 1) * pitch
            rim_send[mb] = sf[:, :, last - 16 : last, :].astype(jnp.bfloat16)

            @pl.when(seq < count - 1)
            def _():
                rim(mb).start()

        def shorts(mb):
            first = mb * pitch

            def one_gate(tile, carry):
                gate(mb, tile, first + 16, length - 8, length + 8)
                far_send[mb, tile] = gf[mb, tile, 2 * length - taps : 2 * length, :].astype(
                    jnp.bfloat16
                )
                return carry

            lax.fori_loop(0, tiles, one_gate, 0)

            @pl.when(seq < count - 1)
            def _():
                gated_rim(mb).start()

            @pl.when(seq > 0)
            def _():
                rim(mb).wait_recv()
                sf[:, :, first : first + 8, :] = rim_recv[mb].astype(jnp.float32)[:, :, 8:16]

            @pl.when(seq == 0)
            def _():
                sf[:, :, first : first + 8, :] = jnp.zeros((3, tiles, 8, lane), jnp.float32)

            def one_tile(tile, carry):
                gate(mb, tile, first + 8, 8, length)
                query[mb, tile] = short(tile, 0, first + 8, length)
                return carry

            lax.fori_loop(0, tiles, one_tile, 0)

        def gated_end(mb):
            @pl.when(seq > 0)
            def _():
                gated_rim(mb).wait_recv()

                def one_tile(tile, carry):
                    gf[mb, tile, length - taps : length, :] = far_recv[mb, tile].astype(
                        jnp.float32
                    )
                    return carry

                lax.fori_loop(0, tiles, one_tile, 0)

            @pl.when(seq == 0)
            def _():
                gf[mb, :, 0:length, :] = jnp.zeros((tiles, length, lane), jnp.float32)

        def early():
            gather_start(0)
            gather_middle(0)
            gather_start(1)

        Gather(slot, shard, send, recv, side_send, side_recv).run(local.at[0], early)
        load_weight.wait()
        gather_middle(1)
        gather_end(0)
        gather_end(1)
        project(0)
        rim_start(0)
        gather_start(2)
        shorts(0)
        gather_middle(2)
        gather_start(3)
        gated_end(0)
        medium(0, 0, 64)
        gather_middle(3)
        medium(0, 64, length - 64)
        reduce_start(coarse[0])
        gather_end(2)
        gather_end(3)
        project(1)
        rim_start(1)
        reduce_middle(coarse[0])
        shorts(1)
        gated_end(1)
        medium(1, 0, 80)
        reduce_start(coarse[1])
        medium(1, 80, length - 80)
        reduce_start(coarse[2])
        reduce_middle(coarse[1])
        reduce_middle(coarse[2])
        reduce_end(coarse[0])
        reduce_end(coarse[1])
        reduce_end(coarse[2])
        reduce_close(coarse)
        gather_close()

        @pl.when(seq < count - 1)
        def _():
            for mb in range(micro):
                rim(mb).wait_send()
                gated_rim(mb).wait_send()


def body(token_ids, embed_table, norm_gain, in_weight, se_filter, mr_filter, out_weight):
    micro, length = token_ids.shape
    vocab, width = embed_table.shape
    full = norm_gain.shape[1]
    count = lax.axis_size("seq")
    ways = full // width
    lane = 128
    tiles = width // lane
    rows = micro * (length + 8)
    taps = mr_filter.shape[1]
    depth = in_weight.shape[1]
    wide = width // count
    shard = in_weight[0].transpose(1, 0, 2)
    moves = Gather.COUNT
    bf16, f32 = jnp.bfloat16, jnp.float32
    scratch, dma = pltpu.VMEM, pltpu.SemaphoreType.DMA
    result = pl.pallas_call(
        mixer_kernel,
        out_shape=jax.ShapeDtypeStruct((rows, width), bf16),
        in_specs=[VMEM, HBM, VMEM, VMEM, VMEM, VMEM, HBM],
        out_specs=VMEM,
        scratch_shapes=[
            scratch((ways, 3, width, width), bf16),
            scratch((width, full), bf16),
            scratch((3, wide, full), bf16),
            scratch((3, wide, vocab), bf16),
            scratch((micro, 2 * length, lane), jnp.int32),
            scratch((3, tiles, 2 * length + 16, lane), f32),
            scratch((micro, tiles, 2 * length, lane), f32),
            scratch((micro, tiles, length, lane), f32),
            scratch((rows, width), f32),
            scratch((rows, width), bf16),
            scratch((3, rows, width), bf16),
            scratch((3, rows, width), bf16),
            scratch((rows, width), f32),
            scratch((rows, width), f32),
            scratch((ways, rows, width), bf16),
            scratch((ways, rows, width), bf16),
            scratch((micro, 3, tiles, 16, lane), bf16),
            scratch((micro, 3, tiles, 16, lane), bf16),
            scratch((micro, tiles, taps, lane), bf16),
            scratch((micro, tiles, taps, lane), bf16),
            dma((moves,)),
            dma((moves,)),
            dma((moves + 1,)),
            dma((moves + 1,)),
            dma((count,)),
            dma((count,)),
            dma((6,)),
            dma((6,)),
            dma((12,)),
            dma((12,)),
            dma((12,)),
            dma((12,)),
            dma((4,)),
            dma((4,)),
            dma((2 * micro,)),
            dma((2 * micro,)),
            dma((3,)),
        ],
        compiler_params=pltpu.CompilerParams(
            collective_id=0, has_side_effects=True, vmem_limit_bytes=60 << 20
        ),
        name="mixer",
    )(token_ids, shard, embed_table, norm_gain, se_filter[0][:, :, None], mr_filter[0], out_weight[0])
    return result.reshape(1, micro, length + 8, width)[:, :, :length]


def solution(mesh):
    in_specs = (
        P(None, "seq"),
        P(None, "tensor"),
        P("section", None),
        P("section", "seq", None, "tensor"),
        P("section", None, None, "tensor"),
        P("section", None, "tensor"),
        P("section", "tensor", None),
    )
    out_specs = P("section", None, "seq", "tensor")
    return jax.shard_map(body, mesh=mesh, in_specs=in_specs, out_specs=out_specs, check_vma=False)
```

```python
import functools

import jax
import jax.numpy as jnp
from jax import lax
from jax.experimental import pallas as pl
from jax.experimental.pallas import tpu as pltpu
from jax.sharding import PartitionSpec as P

EPS = 1e-06
MESH = pl.DeviceIdType.MESH
RING = 8
VMEM = pl.BlockSpec(memory_space=pltpu.VMEM)
HBM = pl.BlockSpec(memory_space=pltpu.HBM)


def place():
    seq = lax.axis_index("seq")
    return seq // (2 * RING), (seq // 2) % RING, seq % 2


def seq_of(y, z, core):
    return (y * RING + z) * 2 + core


class Gather:
    MOVES = (
        ("a1", "up", True, 0, None),
        ("b1", "down", True, 0, None),
        ("c1", "y", True, 0, None),
        ("a2", "up", True, -1, None),
        ("b2", "down", True, 1, None),
        ("c2", "y", True, -1, 1),
        ("c3", "y", True, 1, 0),
        ("a3", "up", True, -2, None),
        ("b3", "down", True, 2, None),
        ("c4", "y", True, -2, 1),
        ("c5", "y", True, 2, 0),
        ("a4", "up", True, -3, 0),
        ("b4", "down", True, 3, 1),
        ("c6", "y", True, -3, 0),
        ("c7", "y", True, 3, 1),
        ("a5", "up", False, 0, 0),
        ("b5", "down", False, 0, 1),
        ("c8", "y", True, -3, 1),
        ("c9", "y", True, 3, 0),
        ("a6", "up", False, -1, 0),
        ("b6", "down", False, 1, 1),
        ("a7", "up", False, -3, 0),
        ("b7", "down", False, 3, 1),
    )
    COUNT = len(MOVES)

    def __init__(self, slot, own, send, recv, side_send, side_recv):
        self.y, self.z, self.core = place()
        self.slot, self.own = slot, own
        self.send, self.recv = send, recv
        self.side_send, self.side_recv = side_send, side_recv
        self.index = {move[0]: at for at, move in enumerate(self.MOVES)}
        self.pending = []

    def target(self, direction):
        if direction == "up":
            return seq_of(self.y, (self.z + 1) % RING, self.core)
        if direction == "down":
            return seq_of(self.y, (self.z + RING - 1) % RING, self.core)
        return seq_of(1 - self.y, self.z, self.core)

    def block(self, same, dz, core=None):
        y = self.y if same else 1 - self.y
        return seq_of(y, (self.z + dz + RING) % RING, self.core if core is None else core)

    def copy(self, name):
        at = self.index[name]
        _, direction, same, dz, half = self.MOVES[at]
        block = self.block(same, dz)
        dst = self.slot(block, half)
        src = self.own if same and dz == 0 else dst
        return pltpu.make_async_remote_copy(
            src_ref=src,
            dst_ref=dst,
            send_sem=self.send.at[at],
            recv_sem=self.recv.at[at],
            device_id={"seq": self.target(direction)},
            device_id_type=MESH,
        )

    def start(self, *names):
        for name in names:
            self.copy(name).start()

    def landed(self, name):
        at = self.index[name]
        _, direction, same, dz, half = self.MOVES[at]
        if direction == "y":
            block = self.block(not same, dz)
        else:
            block = self.block(same, dz + (-1 if direction == "up" else 1))
        got = self.slot(block, half)
        pltpu.make_async_copy(got, got, self.recv.at[at]).wait()
        side = pltpu.make_async_remote_copy(
            src_ref=got,
            dst_ref=got,
            send_sem=self.side_send.at[at],
            recv_sem=self.side_recv.at[at],
            device_id={"seq": seq_of(self.y, self.z, 1 - self.core)},
            device_id_type=MESH,
        )
        side.start()

    def side_own(self):
        return pltpu.make_async_remote_copy(
            src_ref=self.own,
            dst_ref=self.slot(self.block(True, 0), None),
            send_sem=self.side_send.at[self.COUNT],
            recv_sem=self.side_recv.at[self.COUNT],
            device_id={"seq": seq_of(self.y, self.z, 1 - self.core)},
            device_id_type=MESH,
        )

    def run(self, local_sem, late=None):
        keep = pltpu.make_async_copy(self.own, self.slot(self.block(True, 0), None), local_sem)
        self.start("a1", "b1", "c1")
        self.side_own().start()
        keep.start()
        self.landed("a1")
        self.start("a2", "c2")
        self.landed("b1")
        self.start("b2", "c3")
        self.landed("c1")
        self.landed("a2")
        self.start("a3", "c4")
        self.landed("b2")
        self.start("b3", "c5")
        self.landed("c2")
        self.landed("c3")
        self.landed("a3")
        self.start("a4", "c6", "a5")
        self.landed("b3")
        self.start("b4", "c7", "b5")
        for name in ("c4", "c5", "a4", "b4"):
            self.landed(name)
        self.start("c8", "c9")
        self.landed("a5")
        self.start("a6")
        self.landed("b5")
        self.start("b6")
        self.landed("c6")
        self.start("a7")
        self.landed("c7")
        self.start("b7")
        self.landed("a6")
        self.landed("b6")
        if late is not None:
            late()
        for name in ("c8", "c9", "a7", "b7"):
            self.landed(name)
        keep.wait()
        for at, (name, direction, same, dz, half) in enumerate(self.MOVES):
            other = self.slot(self.block(*self.came(at), 1 - self.core), half)
            pltpu.make_async_copy(other, other, self.side_recv.at[at]).wait()
        other = self.slot(self.block(True, 0, 1 - self.core), None)
        pltpu.make_async_copy(other, other, self.side_recv.at[self.COUNT]).wait()

    def came(self, at):
        _, direction, same, dz, _ = self.MOVES[at]
        if direction == "y":
            return not same, dz
        return same, dz + (-1 if direction == "up" else 1)

    def close(self):
        for at, (name, direction, same, dz, half) in enumerate(self.MOVES):
            self.copy(name).wait_send()
            mine = self.slot(self.block(*self.came(at)), half)
            pltpu.make_async_copy(mine, mine, self.side_send.at[at]).wait()
        self.side_own().wait_send()


def mixer_kernel(
    ids, shard, table, gain, se, mr, weight_hbm, out,
    w, weight, tail_all, part, ids_all, sf, gf, query, mixf, mixed, send_buf, recv_buf, own_part, base, xs, xn,
    rim_send, rim_recv, far_send, far_recv,
    send, recv, side_send, side_recv, a2a_send, a2a_recv, x_send, x_recv,
    rs_send, rs_recv, ag_send, ag_recv, relay_send, relay_recv, halo_send, halo_recv, local,
):
    section = lax.axis_index("section")
    tensor = lax.axis_index("tensor")
    seq = lax.axis_index("seq")
    y, z, core = place()
    depth = shard.shape[1]
    vocab, width = table.shape
    wide = part.shape[1]
    count = width // wide
    share = 3 * wide
    half = vocab // 2
    ways = w.shape[0]
    micro = gf.shape[0]
    tiles = gf.shape[1]
    length = gf.shape[2] // 2
    taps = mr.shape[0]
    short_taps = se.shape[1]
    lane = 128
    block = 512
    broad = 512
    pitch = length + 8
    chunks = ((0, 64), (64, pitch - 64), (pitch, 80), (pitch + 80, pitch - 80))
    fine = tuple((at, *chunk) for at, chunk in enumerate(chunks))
    coarse = ((0, 0, pitch),) + tuple((at - 1, *chunks[at]) for at in (2, 3))
    ahead = (tensor + 1 + core * (ways - 2)) % ways
    behind = (tensor + ways - 1 - core * (ways - 2)) % ways
    far = (tensor + 2) % ways
    barrier = pltpu.get_barrier_semaphore()

    def greet(**axes):
        pl.semaphore_signal(barrier, inc=1, device_id=axes, device_id_type=MESH)

    def remote(src, dst, send_sem, recv_sem, **axes):
        return pltpu.make_async_remote_copy(
            src_ref=src, dst_ref=dst, send_sem=send_sem, recv_sem=recv_sem,
            device_id=axes, device_id_type=MESH,
        )

    def arrival(ref, sem):
        pltpu.make_async_copy(ref, ref, sem).wait()

    def lanes(tile):
        return pl.ds(pl.multiple_of(tile * lane, lane), lane)

    def short(tile, stream, start, rows):
        total = jnp.zeros((rows, lane), jnp.float32)
        for tap in range(short_taps):
            total += se[stream, tap, :, lanes(tile)] * sf[
                stream, tile, start - tap : start - tap + rows, :
            ]
        return total

    def gate(mb, tile, start, rows, at):
        values = short(tile, 1, start, rows) * short(tile, 2, start, rows)
        gf[mb, tile, at : at + rows, :] = values.astype(jnp.bfloat16).astype(jnp.float32)

    def medium(mb, begin, rows):
        def one_tile(tile, carry):
            total = jnp.zeros((rows, lane), jnp.float32)
            first = length + begin - taps
            window = gf[mb, tile, first : first + rows + taps, :]
            for shift in range(8):
                part_sum = jnp.zeros((rows + 8, lane), jnp.float32)
                for step in range(taps // 8):
                    tap = 8 * step + shift
                    at = taps - 8 - 8 * step
                    part_sum += mr[tap : tap + 1, lanes(tile)] * window[at : at + rows + 8]
                total += part_sum[8 - shift : 8 - shift + rows]
            to = mb * pitch + begin
            mixf[to : to + rows, lanes(tile)] = query[mb, tile, begin : begin + rows] * total
            return carry

        lax.fori_loop(0, tiles, one_tile, 0)

    def partial_to(chunk, owner, finish):
        index, first, rows = chunk
        window = slice(first, first + rows)

        def one_block(at, carry):
            inner = pl.ds(pl.multiple_of(at * broad, broad), broad)
            outer = pl.ds(pl.multiple_of(owner * width + at * broad, broad), broad)
            term = jnp.dot(mixed[window], weight[:, outer], preferred_element_type=jnp.float32)
            finish(window, inner, term)
            return carry

        lax.fori_loop(0, width // broad, one_block, 0)

    def hop(chunk, at, to):
        index, first, rows = chunk
        window = slice(first, first + rows)
        return remote(
            send_buf.at[at, window], recv_buf.at[at, window],
            rs_send.at[index * 3 + at], rs_recv.at[index * 3 + at], tensor=to,
        )

    def fill(at):
        def finish(window, inner, term):
            send_buf[at, window, inner] = term.astype(jnp.bfloat16)

        return finish

    def reduce_start(chunk):
        index, first, rows = chunk
        window = slice(first, first + rows)
        mixed[window] = mixf[window].astype(jnp.bfloat16)
        partial_to(chunk, far, fill(0))
        hop(chunk, 0, ahead).start()
        partial_to(chunk, behind, fill(2))
        hop(chunk, 2, behind).start()

        def onward(window, inner, term):
            mixf[window, inner] = term

        def keep(window, inner, term):
            own_part[window, inner] = term

        partial_to(chunk, ahead, onward)
        partial_to(chunk, tensor, keep)

    def reduce_middle(chunk):
        index, first, rows = chunk
        hop(chunk, 0, ahead).wait_recv()
        lines = 16

        def join(at, carry):
            window = pl.ds(pl.multiple_of(first + at * lines, lines), lines)
            both = mixf[window] + recv_buf[0, window].astype(jnp.float32)
            send_buf[1, window] = both.astype(jnp.bfloat16)
            return carry

        lax.fori_loop(0, rows // lines, join, 0)
        hop(chunk, 1, ahead).start()

    def reduce_end(chunk):
        index, first, rows = chunk
        hop(chunk, 2, behind).wait_recv()
        hop(chunk, 1, ahead).wait_recv()
        lines = 16

        def add(at, carry):
            window = pl.ds(pl.multiple_of(first + at * lines, lines), lines)
            total = own_part[window] + recv_buf[1, window].astype(jnp.float32)
            total += recv_buf[2, window].astype(jnp.float32)
            out[window] = (base[window] + total).astype(jnp.bfloat16)
            return carry

        lax.fori_loop(0, rows // lines, add, 0)

    def reduce_close(pieces):
        for chunk in pieces:
            hop(chunk, 0, ahead).wait_send()
            hop(chunk, 1, ahead).wait_send()
            hop(chunk, 2, behind).wait_send()

    def relay(chunk):
        first, rows = chunks[chunk]
        window = slice(first, first + rows)
        return remote(
            out.at[window], xs.at[tensor, window],
            relay_send.at[chunk], relay_recv.at[chunk], section=1,
        )

    load_weight = pltpu.make_async_copy(weight_hbm, weight, local.at[2])

    @pl.when(section == 0)
    def _():
        greet(tensor=ahead)
        greet(tensor=behind)

        def greet_seq(step, carry):
            greet(seq=(seq + step) % count)
            return carry

        load_shard = pltpu.make_async_copy(shard, xn.at[0:3, 0:depth], local.at[0])
        load_shard.start()
        lax.fori_loop(1, count, greet_seq, 0)
        load_shard.wait()
        tail = w.at[3, :, :, vocab : vocab + depth]
        for stream in range(3):
            w[3, stream, :, vocab : vocab + depth] = xn[stream, 0:depth].T
        for mb in range(micro):
            for begin, rows in ((0, lane), (lane, length - lane)):
                line = ids[mb : mb + 1, begin : begin + rows]
                ids_all[mb, length + begin : length + begin + rows] = jnp.broadcast_to(
                    line, (lane, rows)
                ).T
        pl.semaphore_wait(barrier, count + 2)
        load_weight.start()

        ids_on = remote(
            ids_all.at[:, length : 2 * length], ids_all.at[:, 0:length], halo_send.at[0], halo_recv.at[0],
            seq=(seq + 1) % count,
        )

        @pl.when(seq < count - 1)
        def _():
            ids_on.start()

        @pl.when(seq == 0)
        def _():
            ids_all[:, 0:length] = jnp.full((micro, length, lane), -1, jnp.int32)

        rows = pl.ds(pl.multiple_of(core * half, half), half)

        def table_of(owner):
            return w.at[1 + owner // 2, owner % 2, 0:vocab]

        def along(at, src, owner, to):
            return remote(src, table_of(owner).at[rows], x_send.at[at], x_recv.at[at], tensor=to)

        def across(at, owner):
            piece = table_of(owner).at[rows]
            return remote(
                piece, piece, x_send.at[at], x_recv.at[at], seq=seq_of(y, z, 1 - core)
            )

        mine = table.at[rows]
        along(0, mine, tensor, ahead).start()
        along(1, mine, tensor, behind).start()
        keep = pltpu.make_async_copy(table, table_of(tensor), local.at[0])
        keep.start()

        def spread(step):
            to = (seq + step) % count
            return remote(
                tail.at[:, pl.ds(pl.multiple_of(to * wide, wide), wide)],
                tail_all.at[:, :, pl.ds(pl.multiple_of(seq * depth, depth), depth)],
                a2a_send.at[step], a2a_recv.at[step], seq=to,
            )

        def spread_start(step, carry):
            spread(step).start()
            return carry

        lax.fori_loop(1, count, spread_start, 0)
        keep_tail = pltpu.make_async_copy(
            tail.at[:, pl.ds(pl.multiple_of(seq * wide, wide), wide)],
            tail_all.at[:, :, pl.ds(pl.multiple_of(seq * depth, depth), depth)],
            local.at[1],
        )
        keep_tail.start()

        along(0, mine, tensor, ahead).wait_recv()
        along(2, table_of(behind).at[rows], behind, ahead).start()
        across(3, behind).start()
        along(1, mine, tensor, behind).wait_recv()
        across(4, ahead).start()
        got = table_of(far).at[rows]
        arrival(got, x_recv.at[2])
        across(5, far).start()
        keep.wait()
        for at, owner in ((3, behind), (4, ahead), (5, far)):
            across(at, owner).wait_recv()
        along(0, mine, tensor, ahead).wait_send()
        along(1, mine, tensor, behind).wait_send()
        arrival(got, x_send.at[2])
        for at, owner in ((3, behind), (4, ahead), (5, far)):
            across(at, owner).wait_send()

        lines = 32

        def normalise(at, carry):
            window = pl.ds(pl.multiple_of(at * lines, lines), lines)
            total = jnp.zeros((lines, 1), jnp.float32)
            for way in range(ways):
                values = w[1 + way // 2, way % 2, window].astype(jnp.float32)
                total += jnp.sum(values * values, axis=1, keepdims=True)
            scale = lax.rsqrt(total / (ways * width) + EPS)
            for way in range(ways):
                values = w[1 + way // 2, way % 2, window].astype(jnp.float32)
                values = values * scale * gain[:, way * width : (way + 1) * width]
                w[1 + way // 2, way % 2, window] = values.astype(jnp.bfloat16)
            return carry

        lax.fori_loop(0, vocab // lines, normalise, 0)

        def spread_wait(step, carry):
            spread(step).wait_send()
            arrival(tail_all.at[:, :, pl.ds(0, depth)], a2a_recv.at[step])
            return carry

        lax.fori_loop(1, count, spread_wait, 0)
        keep_tail.wait()
        total = jnp.zeros((share, vocab), jnp.float32)
        for way in range(ways):
            total += lax.dot_general(
                tail_all[:, :, way * width : (way + 1) * width].reshape(share, width),
                w[1 + way // 2, way % 2, 0:vocab],
                (((1,), (1,)), ((), ())),
                preferred_element_type=jnp.float32,
            )
        for stream in range(3):
            part[stream] = total[stream * wide : (stream + 1) * wide].astype(jnp.bfloat16)

        def slot(owner, part_of):
            at, some = owner * wide, wide
            if part_of is not None:
                some = wide // 2
                at = at + part_of * some
            return w.at[0, :, pl.ds(pl.multiple_of(at, some), some), 0:vocab]

        spread_table = Gather(slot, part, send, recv, side_send, side_recv)
        spread_table.run(local.at[0])
        load_weight.wait()

        @pl.when(seq > 0)
        def _():
            ids_on.wait_recv()

        onehot = w.at[3, 0, 0 : 2 * length, 0:vocab]

        def streams(mb):
            for part_at in range(vocab // lane):
                number = lax.broadcasted_iota(jnp.int32, (2 * length, lane), 1) + part_at * lane
                hit = jnp.where(ids_all[mb] == number, 1.0, 0.0).astype(jnp.bfloat16)
                w[3, 0, 0 : 2 * length, part_at * lane : (part_at + 1) * lane] = hit

            def one_block(at, carry):
                stream, inner = at // (width // block), at % (width // block)
                columns = pl.ds(pl.multiple_of(inner * block, block), block)
                values = lax.dot_general(
                    onehot[...],
                    w[0, stream, columns, 0:vocab],
                    (((1,), (1,)), ((), ())),
                    preferred_element_type=jnp.float32,
                ).astype(jnp.bfloat16).astype(jnp.float32)
                for side in range(block // lane):
                    sf[stream, inner * (block // lane) + side, 8 : 8 + 2 * length, :] = values[
                        :, side * lane : (side + 1) * lane
                    ]
                return carry

            lax.fori_loop(0, 3 * width // block, one_block, 0)

            def own_rows(at, carry):
                columns = pl.ds(pl.multiple_of(at * block, block), block)
                values = jnp.dot(
                    onehot[...], table[:, columns], preferred_element_type=jnp.float32
                )
                base[mb * pitch : mb * pitch + length, columns] = values[length : 2 * length]
                return carry

            lax.fori_loop(0, width // block, own_rows, 0)

            def one_tile(tile, carry):
                query[mb, tile] = short(tile, 0, 8 + length, length)
                gate(mb, tile, 8, length, 0)
                gate(mb, tile, 8 + length, length, length)
                return carry

            lax.fori_loop(0, tiles, one_tile, 0)

        sf[:, :, 0:8, :] = jnp.zeros((3, tiles, 8, lane), jnp.float32)
        def pass_on(chunk):
            reduce_end(fine[chunk])
            relay(chunk).start()

        streams(0)
        medium(0, 0, 64)
        reduce_start(fine[0])
        medium(0, 64, length - 64)
        reduce_start(fine[1])
        reduce_middle(fine[0])
        streams(1)
        reduce_middle(fine[1])
        pass_on(0)
        medium(1, 0, 80)
        reduce_start(fine[2])
        pass_on(1)
        medium(1, 80, length - 80)
        reduce_middle(fine[2])
        reduce_start(fine[3])
        reduce_middle(fine[3])
        pass_on(2)
        pass_on(3)
        reduce_close(fine)
        spread_table.close()
        for chunk in range(len(chunks)):
            relay(chunk).wait_send()

        @pl.when(seq < count - 1)
        def _():
            ids_on.wait_send()

    @pl.when(section == 1)
    def _():
        greet(seq=seq_of(y, (z + 1) % RING, core))
        greet(seq=seq_of(y, (z + RING - 1) % RING, core))
        greet(seq=seq_of(1 - y, z, core))
        greet(seq=seq_of(y, z, 1 - core))
        greet(tensor=ahead)
        greet(tensor=behind)
        greet(section=0)

        @pl.when(seq > 0)
        def _():
            greet(seq=(seq + count - 1) % count)

        @pl.when(seq < count - 1)
        def _():
            pl.semaphore_wait(barrier, 7)

        @pl.when(seq == count - 1)
        def _():
            pl.semaphore_wait(barrier, 6)

        load_weight.start()
        per = width // depth

        def slot(owner, part_of):
            at, some = (owner % per) * depth, depth
            if part_of is not None:
                some = depth // 2
                at = at + part_of * some
            return w.at[owner // per, :, pl.ds(pl.multiple_of(at, some), some)]

        def share_out(chunk, at, owner, to):
            first, rows = chunks[chunk]
            piece = xs.at[owner, first : first + rows]
            return remote(
                piece, piece, ag_send.at[chunk * 3 + at], ag_recv.at[chunk * 3 + at], tensor=to
            )

        def gather_start(chunk):
            first, rows = chunks[chunk]
            arrival(xs.at[tensor, first : first + rows], relay_recv.at[chunk])
            share_out(chunk, 0, tensor, ahead).start()
            share_out(chunk, 1, tensor, behind).start()

        def gather_middle(chunk):
            first, rows = chunks[chunk]
            arrival(xs.at[behind, first : first + rows], ag_recv.at[chunk * 3])
            share_out(chunk, 2, behind, ahead).start()

        def gather_end(chunk):
            first, rows = chunks[chunk]
            arrival(xs.at[ahead, first : first + rows], ag_recv.at[chunk * 3 + 1])
            arrival(xs.at[far, first : first + rows], ag_recv.at[chunk * 3 + 2])

        def gather_close():
            for chunk in range(len(chunks)):
                share_out(chunk, 0, tensor, ahead).wait_send()
                share_out(chunk, 1, tensor, behind).wait_send()
                share_out(chunk, 2, behind, ahead).wait_send()

        def project(group):
            first, rows = group * pitch, pitch
            lines = 16

            def normalise(at, carry):
                window = pl.ds(pl.multiple_of(first + at * lines, lines), lines)
                total = jnp.zeros((lines, 1), jnp.float32)
                for way in range(ways):
                    values = xs[way, window].astype(jnp.float32)
                    total += jnp.sum(values * values, axis=1, keepdims=True)
                scale = lax.rsqrt(total / (ways * width) + EPS)
                for way in range(ways):
                    values = xs[way, window].astype(jnp.float32)
                    values = values * scale * gain[:, way * width : (way + 1) * width]
                    xn[way, window] = values.astype(jnp.bfloat16)
                base[window] = xs[tensor, window].astype(jnp.float32)
                return carry

            lax.fori_loop(0, rows // lines, normalise, 0)

            def one_block(at, carry):
                stream, inner = at // (width // block), at % (width // block)
                columns = pl.ds(pl.multiple_of(inner * block, block), block)
                total = jnp.zeros((rows, block), jnp.float32)
                for way in range(ways):
                    total += jnp.dot(
                        xn[way, first : first + rows],
                        w[way, stream, :, columns],
                        preferred_element_type=jnp.float32,
                    )
                total = total.astype(jnp.bfloat16).astype(jnp.float32)
                for side in range(block // lane):
                    tile = inner * (block // lane) + side
                    piece = total[:, side * lane : (side + 1) * lane]
                    sf[stream, tile, first + 8 : first + 8 + length, :] = piece[0:length]
                return carry

            lax.fori_loop(0, 3 * width // block, one_block, 0)

        def rim(mb):
            return remote(
                rim_send.at[mb], rim_recv.at[mb], halo_send.at[mb], halo_recv.at[mb],
                seq=(seq + 1) % count,
            )

        def gated_rim(mb):
            return remote(
                far_send.at[mb], far_recv.at[mb], halo_send.at[micro + mb], halo_recv.at[micro + mb],
                seq=(seq + 1) % count,
            )

        def rim_start(mb):
            last = (mb + 1) * pitch
            rim_send[mb] = sf[:, :, last - 16 : last, :].astype(jnp.bfloat16)

            @pl.when(seq < count - 1)
            def _():
                rim(mb).start()

        def shorts(mb):
            first = mb * pitch

            def one_gate(tile, carry):
                gate(mb, tile, first + 16, length - 8, length + 8)
                far_send[mb, tile] = gf[mb, tile, 2 * length - taps : 2 * length, :].astype(
                    jnp.bfloat16
                )
                return carry

            lax.fori_loop(0, tiles, one_gate, 0)

            @pl.when(seq < count - 1)
            def _():
                gated_rim(mb).start()

            @pl.when(seq > 0)
            def _():
                rim(mb).wait_recv()
                sf[:, :, first : first + 8, :] = rim_recv[mb].astype(jnp.float32)[:, :, 8:16]

            @pl.when(seq == 0)
            def _():
                sf[:, :, first : first + 8, :] = jnp.zeros((3, tiles, 8, lane), jnp.float32)

            def one_tile(tile, carry):
                gate(mb, tile, first + 8, 8, length)
                query[mb, tile] = short(tile, 0, first + 8, length)
                return carry

            lax.fori_loop(0, tiles, one_tile, 0)

        def gated_end(mb):
            @pl.when(seq > 0)
            def _():
                gated_rim(mb).wait_recv()

                def one_tile(tile, carry):
                    gf[mb, tile, length - taps : length, :] = far_recv[mb, tile].astype(
                        jnp.float32
                    )
                    return carry

                lax.fori_loop(0, tiles, one_tile, 0)

            @pl.when(seq == 0)
            def _():
                gf[mb, :, 0:length, :] = jnp.zeros((tiles, length, lane), jnp.float32)

        def early():
            gather_start(0)
            gather_middle(0)
            gather_start(1)

        spread_weight = Gather(slot, shard, send, recv, side_send, side_recv)
        spread_weight.run(local.at[0], early)
        load_weight.wait()
        gather_middle(1)
        gather_end(0)
        gather_end(1)
        project(0)
        rim_start(0)
        gather_start(2)
        shorts(0)
        gather_middle(2)
        gather_start(3)
        spread_weight.close()
        gated_end(0)
        medium(0, 0, 64)
        gather_middle(3)
        medium(0, 64, length - 64)
        reduce_start(coarse[0])
        gather_end(2)
        gather_end(3)
        project(1)
        rim_start(1)
        reduce_middle(coarse[0])
        shorts(1)
        gated_end(1)
        medium(1, 0, 80)
        reduce_start(coarse[1])
        medium(1, 80, length - 80)
        reduce_middle(coarse[1])
        reduce_start(coarse[2])
        reduce_middle(coarse[2])
        gather_close()
        reduce_end(coarse[0])
        reduce_end(coarse[1])
        reduce_end(coarse[2])
        reduce_close(coarse)

        @pl.when(seq < count - 1)
        def _():
            for mb in range(micro):
                rim(mb).wait_send()
                gated_rim(mb).wait_send()


def body(token_ids, embed_table, norm_gain, in_weight, se_filter, mr_filter, out_weight):
    micro, length = token_ids.shape
    vocab, width = embed_table.shape
    full = norm_gain.shape[1]
    count = lax.axis_size("seq")
    ways = full // width
    lane = 128
    tiles = width // lane
    rows = micro * (length + 8)
    taps = mr_filter.shape[1]
    depth = in_weight.shape[1]
    wide = width // count
    shard = in_weight[0].transpose(1, 0, 2)
    moves = Gather.COUNT
    bf16, f32 = jnp.bfloat16, jnp.float32
    scratch, dma = pltpu.VMEM, pltpu.SemaphoreType.DMA
    result = pl.pallas_call(
        mixer_kernel,
        out_shape=jax.ShapeDtypeStruct((rows, width), bf16),
        in_specs=[VMEM, HBM, VMEM, VMEM, VMEM, VMEM, HBM],
        out_specs=VMEM,
        scratch_shapes=[
            scratch((ways, 3, width, width), bf16),
            scratch((width, full), bf16),
            scratch((3, wide, full), bf16),
            scratch((3, wide, vocab), bf16),
            scratch((micro, 2 * length, lane), jnp.int32),
            scratch((3, tiles, 2 * length + 16, lane), f32),
            scratch((micro, tiles, 2 * length, lane), f32),
            scratch((micro, tiles, length, lane), f32),
            scratch((rows, width), f32),
            scratch((rows, width), bf16),
            scratch((3, rows, width), bf16),
            scratch((3, rows, width), bf16),
            scratch((rows, width), f32),
            scratch((rows, width), f32),
            scratch((ways, rows, width), bf16),
            scratch((ways, rows, width), bf16),
            scratch((micro, 3, tiles, 16, lane), bf16),
            scratch((micro, 3, tiles, 16, lane), bf16),
            scratch((micro, tiles, taps, lane), bf16),
            scratch((micro, tiles, taps, lane), bf16),
            dma((moves,)),
            dma((moves,)),
            dma((moves + 1,)),
            dma((moves + 1,)),
            dma((count,)),
            dma((count,)),
            dma((6,)),
            dma((6,)),
            dma((12,)),
            dma((12,)),
            dma((12,)),
            dma((12,)),
            dma((4,)),
            dma((4,)),
            dma((2 * micro,)),
            dma((2 * micro,)),
            dma((3,)),
        ],
        compiler_params=pltpu.CompilerParams(
            collective_id=0, has_side_effects=True, vmem_limit_bytes=60 << 20
        ),
        name="mixer",
    )(token_ids, shard, embed_table, norm_gain, se_filter[0][:, :, None], mr_filter[0], out_weight[0])
    return result.reshape(1, micro, length + 8, width)[:, :, :length]


def solution(mesh):
    in_specs = (
        P(None, "seq"),
        P(None, "tensor"),
        P("section", None),
        P("section", "seq", None, "tensor"),
        P("section", None, None, "tensor"),
        P("section", None, "tensor"),
        P("section", "tensor", None),
    )
    out_specs = P("section", None, "seq", "tensor")
    return jax.shard_map(body, mesh=mesh, in_specs=in_specs, out_specs=out_specs, check_vma=False)
```

```python
import functools

import jax
import jax.numpy as jnp
from jax import lax
from jax.experimental import pallas as pl
from jax.experimental.pallas import tpu as pltpu
from jax.sharding import PartitionSpec as P

EPS = 1e-06
MESH = pl.DeviceIdType.MESH
RING = 8
VMEM = pl.BlockSpec(memory_space=pltpu.VMEM)
HBM = pl.BlockSpec(memory_space=pltpu.HBM)


def place():
    seq = lax.axis_index("seq")
    return seq // (2 * RING), (seq // 2) % RING, seq % 2


def seq_of(y, z, core):
    return (y * RING + z) * 2 + core


class Gather:
    MOVES = (
        ("a1", "up", True, 0, None),
        ("b1", "down", True, 0, None),
        ("c1", "y", True, 0, None),
        ("a2", "up", True, -1, None),
        ("b2", "down", True, 1, None),
        ("c2", "y", True, -1, 1),
        ("c3", "y", True, 1, 0),
        ("a3", "up", True, -2, None),
        ("b3", "down", True, 2, None),
        ("c4", "y", True, -2, 1),
        ("c5", "y", True, 2, 0),
        ("a4", "up", True, -3, 0),
        ("b4", "down", True, 3, 1),
        ("c6", "y", True, -3, 0),
        ("c7", "y", True, 3, 1),
        ("a5", "up", False, 0, 0),
        ("b5", "down", False, 0, 1),
        ("c8", "y", True, -3, 1),
        ("c9", "y", True, 3, 0),
        ("a6", "up", False, -1, 0),
        ("b6", "down", False, 1, 1),
        ("a7", "up", False, -3, 0),
        ("b7", "down", False, 3, 1),
    )
    COUNT = len(MOVES)

    def __init__(self, slot, own, send, recv, side_send, side_recv):
        self.y, self.z, self.core = place()
        self.slot, self.own = slot, own
        self.send, self.recv = send, recv
        self.side_send, self.side_recv = side_send, side_recv
        self.index = {move[0]: at for at, move in enumerate(self.MOVES)}
        self.pending = []

    def target(self, direction):
        if direction == "up":
            return seq_of(self.y, (self.z + 1) % RING, self.core)
        if direction == "down":
            return seq_of(self.y, (self.z + RING - 1) % RING, self.core)
        return seq_of(1 - self.y, self.z, self.core)

    def block(self, same, dz, core=None):
        y = self.y if same else 1 - self.y
        return seq_of(y, (self.z + dz + RING) % RING, self.core if core is None else core)

    def copy(self, name):
        at = self.index[name]
        _, direction, same, dz, half = self.MOVES[at]
        block = self.block(same, dz)
        dst = self.slot(block, half)
        src = self.own if same and dz == 0 else dst
        return pltpu.make_async_remote_copy(
            src_ref=src,
            dst_ref=dst,
            send_sem=self.send.at[at],
            recv_sem=self.recv.at[at],
            device_id={"seq": self.target(direction)},
            device_id_type=MESH,
        )

    def start(self, *names):
        for name in names:
            self.copy(name).start()

    def landed(self, name):
        at = self.index[name]
        _, direction, same, dz, half = self.MOVES[at]
        if direction == "y":
            block = self.block(not same, dz)
        else:
            block = self.block(same, dz + (-1 if direction == "up" else 1))
        got = self.slot(block, half)
        pltpu.make_async_copy(got, got, self.recv.at[at]).wait()
        side = pltpu.make_async_remote_copy(
            src_ref=got,
            dst_ref=got,
            send_sem=self.side_send.at[at],
            recv_sem=self.side_recv.at[at],
            device_id={"seq": seq_of(self.y, self.z, 1 - self.core)},
            device_id_type=MESH,
        )
        side.start()

    def side_own(self):
        return pltpu.make_async_remote_copy(
            src_ref=self.own,
            dst_ref=self.slot(self.block(True, 0), None),
            send_sem=self.side_send.at[self.COUNT],
            recv_sem=self.side_recv.at[self.COUNT],
            device_id={"seq": seq_of(self.y, self.z, 1 - self.core)},
            device_id_type=MESH,
        )

    def run(self, local_sem, late=None, last=None):
        keep = pltpu.make_async_copy(self.own, self.slot(self.block(True, 0), None), local_sem)
        self.start("a1", "b1", "c1")
        self.side_own().start()
        keep.start()
        self.landed("a1")
        self.start("a2", "c2")
        self.landed("b1")
        self.start("b2", "c3")
        self.landed("c1")
        self.landed("a2")
        self.start("a3", "c4")
        self.landed("b2")
        self.start("b3", "c5")
        self.landed("c2")
        self.landed("c3")
        self.landed("a3")
        self.start("a4", "c6", "a5")
        self.landed("b3")
        self.start("b4", "c7", "b5")
        for name in ("c4", "c5", "a4", "b4"):
            self.landed(name)
        self.start("c8", "c9")
        self.landed("a5")
        self.start("a6")
        self.landed("b5")
        self.start("b6")
        self.landed("c6")
        self.start("a7")
        self.landed("c7")
        self.start("b7")
        self.landed("a6")
        self.landed("b6")
        if late is not None:
            late()
        self.landed("c8")
        self.landed("c9")
        if last is not None:
            last()
        self.landed("a7")
        self.landed("b7")
        keep.wait()
        for at, (name, direction, same, dz, half) in enumerate(self.MOVES):
            other = self.slot(self.block(*self.came(at), 1 - self.core), half)
            pltpu.make_async_copy(other, other, self.side_recv.at[at]).wait()
        other = self.slot(self.block(True, 0, 1 - self.core), None)
        pltpu.make_async_copy(other, other, self.side_recv.at[self.COUNT]).wait()

    def came(self, at):
        _, direction, same, dz, _ = self.MOVES[at]
        if direction == "y":
            return not same, dz
        return same, dz + (-1 if direction == "up" else 1)

    def close(self):
        for at, (name, direction, same, dz, half) in enumerate(self.MOVES):
            self.copy(name).wait_send()
            mine = self.slot(self.block(*self.came(at)), half)
            pltpu.make_async_copy(mine, mine, self.side_send.at[at]).wait()
        self.side_own().wait_send()


def mixer_kernel(
    ids, shard, table, gain, se, mr, weight_hbm, out,
    w, weight, tail_all, part, ids_all, sf, gf, query, mixf, mixed, send_buf, recv_buf, own_part, base, xs, xn,
    rim_send, rim_recv, far_send, far_recv,
    send, recv, side_send, side_recv, a2a_send, a2a_recv, x_send, x_recv,
    rs_send, rs_recv, ag_send, ag_recv, relay_send, relay_recv, halo_send, halo_recv, local,
):
    section = lax.axis_index("section")
    tensor = lax.axis_index("tensor")
    seq = lax.axis_index("seq")
    y, z, core = place()
    depth = shard.shape[1]
    vocab, width = table.shape
    wide = part.shape[1]
    count = width // wide
    share = 3 * wide
    half = vocab // 2
    ways = w.shape[0]
    micro = gf.shape[0]
    tiles = gf.shape[1]
    length = gf.shape[2] // 2
    taps = mr.shape[0]
    short_taps = se.shape[1]
    lane = 128
    block = 512
    broad = 512
    pitch = length + 8
    chunks = ((0, 64), (64, pitch - 64), (pitch, 80), (pitch + 80, pitch - 80))
    fine = tuple((at, *chunk) for at, chunk in enumerate(chunks))
    coarse = ((0, 0, pitch),) + tuple((at - 1, *chunks[at]) for at in (2, 3))
    ahead = (tensor + 1 + core * (ways - 2)) % ways
    behind = (tensor + ways - 1 - core * (ways - 2)) % ways
    far = (tensor + 2) % ways
    barrier = pltpu.get_barrier_semaphore()

    def greet(**axes):
        pl.semaphore_signal(barrier, inc=1, device_id=axes, device_id_type=MESH)

    def remote(src, dst, send_sem, recv_sem, **axes):
        return pltpu.make_async_remote_copy(
            src_ref=src, dst_ref=dst, send_sem=send_sem, recv_sem=recv_sem,
            device_id=axes, device_id_type=MESH,
        )

    def arrival(ref, sem):
        pltpu.make_async_copy(ref, ref, sem).wait()

    def lanes(tile):
        return pl.ds(pl.multiple_of(tile * lane, lane), lane)

    def short(tile, stream, start, rows):
        total = jnp.zeros((rows, lane), jnp.float32)
        for tap in range(short_taps):
            total += se[stream, tap, :, lanes(tile)] * sf[
                stream, tile, start - tap : start - tap + rows, :
            ]
        return total

    def gate(mb, tile, start, rows, at):
        values = short(tile, 1, start, rows) * short(tile, 2, start, rows)
        gf[mb, tile, at : at + rows, :] = values.astype(jnp.bfloat16).astype(jnp.float32)

    def medium(mb, begin, rows):
        def one_tile(tile, carry):
            total = jnp.zeros((rows, lane), jnp.float32)
            first = length + begin - taps
            window = gf[mb, tile, first : first + rows + taps, :]
            for shift in range(8):
                part_sum = jnp.zeros((rows + 8, lane), jnp.float32)
                for step in range(taps // 8):
                    tap = 8 * step + shift
                    at = taps - 8 - 8 * step
                    part_sum += mr[tap : tap + 1, lanes(tile)] * window[at : at + rows + 8]
                total += part_sum[8 - shift : 8 - shift + rows]
            to = mb * pitch + begin
            mixf[to : to + rows, lanes(tile)] = query[mb, tile, begin : begin + rows] * total
            return carry

        lax.fori_loop(0, tiles, one_tile, 0)

    def partial_to(chunk, owner, finish):
        index, first, rows = chunk
        window = slice(first, first + rows)

        def one_block(at, carry):
            inner = pl.ds(pl.multiple_of(at * broad, broad), broad)
            outer = pl.ds(pl.multiple_of(owner * width + at * broad, broad), broad)
            term = jnp.dot(mixed[window], weight[:, outer], preferred_element_type=jnp.float32)
            finish(window, inner, term)
            return carry

        lax.fori_loop(0, width // broad, one_block, 0)

    def hop(chunk, at, to):
        index, first, rows = chunk
        window = slice(first, first + rows)
        return remote(
            send_buf.at[at, window], recv_buf.at[at, window],
            rs_send.at[index * 3 + at], rs_recv.at[index * 3 + at], tensor=to,
        )

    def fill(at):
        def finish(window, inner, term):
            send_buf[at, window, inner] = term.astype(jnp.bfloat16)

        return finish

    def reduce_start(chunk):
        index, first, rows = chunk
        window = slice(first, first + rows)
        mixed[window] = mixf[window].astype(jnp.bfloat16)
        partial_to(chunk, far, fill(0))
        hop(chunk, 0, ahead).start()
        partial_to(chunk, behind, fill(2))
        hop(chunk, 2, behind).start()

        def onward(window, inner, term):
            mixf[window, inner] = term

        def keep(window, inner, term):
            own_part[window, inner] = term

        partial_to(chunk, ahead, onward)
        partial_to(chunk, tensor, keep)

    def reduce_middle(chunk):
        index, first, rows = chunk
        hop(chunk, 0, ahead).wait_recv()
        lines = 16

        def join(at, carry):
            window = pl.ds(pl.multiple_of(first + at * lines, lines), lines)
            both = mixf[window] + recv_buf[0, window].astype(jnp.float32)
            send_buf[1, window] = both.astype(jnp.bfloat16)
            return carry

        lax.fori_loop(0, rows // lines, join, 0)
        hop(chunk, 1, ahead).start()

    def reduce_end(chunk):
        index, first, rows = chunk
        hop(chunk, 2, behind).wait_recv()
        hop(chunk, 1, ahead).wait_recv()
        lines = 16

        def add(at, carry):
            window = pl.ds(pl.multiple_of(first + at * lines, lines), lines)
            total = own_part[window] + recv_buf[1, window].astype(jnp.float32)
            total += recv_buf[2, window].astype(jnp.float32)
            out[window] = (base[window] + total).astype(jnp.bfloat16)
            return carry

        lax.fori_loop(0, rows // lines, add, 0)

    def reduce_close(pieces):
        for chunk in pieces:
            hop(chunk, 0, ahead).wait_send()
            hop(chunk, 1, ahead).wait_send()
            hop(chunk, 2, behind).wait_send()

    def relay(chunk):
        first, rows = chunks[chunk]
        window = slice(first, first + rows)
        return remote(
            out.at[window], xs.at[tensor, window],
            relay_send.at[chunk], relay_recv.at[chunk], section=1,
        )

    load_weight = pltpu.make_async_copy(weight_hbm, weight, local.at[2])

    @pl.when(section == 0)
    def _():
        greet(tensor=ahead)
        greet(tensor=behind)

        def greet_seq(step, carry):
            greet(seq=(seq + step) % count)
            return carry

        load_shard = pltpu.make_async_copy(shard, xn.at[0:3, 0:depth], local.at[0])
        load_shard.start()
        lax.fori_loop(1, count, greet_seq, 0)
        load_shard.wait()
        tail = w.at[3, :, :, vocab : vocab + depth]
        for stream in range(3):
            w[3, stream, :, vocab : vocab + depth] = xn[stream, 0:depth].T
        for mb in range(micro):
            for begin, rows in ((0, lane), (lane, length - lane)):
                line = ids[mb : mb + 1, begin : begin + rows]
                ids_all[mb, length + begin : length + begin + rows] = jnp.broadcast_to(
                    line, (lane, rows)
                ).T
        pl.semaphore_wait(barrier, count + 2)
        load_weight.start()

        ids_on = remote(
            ids_all.at[:, length : 2 * length], ids_all.at[:, 0:length], halo_send.at[0], halo_recv.at[0],
            seq=(seq + 1) % count,
        )

        @pl.when(seq < count - 1)
        def _():
            ids_on.start()

        @pl.when(seq == 0)
        def _():
            ids_all[:, 0:length] = jnp.full((micro, length, lane), -1, jnp.int32)

        rows = pl.ds(pl.multiple_of(core * half, half), half)

        def table_of(owner):
            return w.at[1 + owner // 2, owner % 2, 0:vocab]

        def along(at, src, owner, to):
            return remote(src, table_of(owner).at[rows], x_send.at[at], x_recv.at[at], tensor=to)

        def across(at, owner):
            piece = table_of(owner).at[rows]
            return remote(
                piece, piece, x_send.at[at], x_recv.at[at], seq=seq_of(y, z, 1 - core)
            )

        mine = table.at[rows]
        along(0, mine, tensor, ahead).start()
        along(1, mine, tensor, behind).start()
        keep = pltpu.make_async_copy(table, table_of(tensor), local.at[0])
        keep.start()

        def spread(step):
            to = (seq + step) % count
            return remote(
                tail.at[:, pl.ds(pl.multiple_of(to * wide, wide), wide)],
                tail_all.at[:, :, pl.ds(pl.multiple_of(seq * depth, depth), depth)],
                a2a_send.at[step], a2a_recv.at[step], seq=to,
            )

        def spread_start(step, carry):
            spread(step).start()
            return carry

        lax.fori_loop(1, count, spread_start, 0)
        keep_tail = pltpu.make_async_copy(
            tail.at[:, pl.ds(pl.multiple_of(seq * wide, wide), wide)],
            tail_all.at[:, :, pl.ds(pl.multiple_of(seq * depth, depth), depth)],
            local.at[1],
        )
        keep_tail.start()

        along(0, mine, tensor, ahead).wait_recv()
        along(2, table_of(behind).at[rows], behind, ahead).start()
        across(3, behind).start()
        along(1, mine, tensor, behind).wait_recv()
        across(4, ahead).start()
        got = table_of(far).at[rows]
        arrival(got, x_recv.at[2])
        across(5, far).start()
        keep.wait()
        for at, owner in ((3, behind), (4, ahead), (5, far)):
            across(at, owner).wait_recv()
        along(0, mine, tensor, ahead).wait_send()
        along(1, mine, tensor, behind).wait_send()
        arrival(got, x_send.at[2])
        for at, owner in ((3, behind), (4, ahead), (5, far)):
            across(at, owner).wait_send()

        lines = 32

        def normalise(at, carry):
            window = pl.ds(pl.multiple_of(at * lines, lines), lines)
            total = jnp.zeros((lines, 1), jnp.float32)
            for way in range(ways):
                values = w[1 + way // 2, way % 2, window].astype(jnp.float32)
                total += jnp.sum(values * values, axis=1, keepdims=True)
            scale = lax.rsqrt(total / (ways * width) + EPS)
            for way in range(ways):
                values = w[1 + way // 2, way % 2, window].astype(jnp.float32)
                values = values * scale * gain[:, way * width : (way + 1) * width]
                w[1 + way // 2, way % 2, window] = values.astype(jnp.bfloat16)
            return carry

        lax.fori_loop(0, vocab // lines, normalise, 0)

        def spread_wait(step, carry):
            spread(step).wait_send()
            arrival(tail_all.at[:, :, pl.ds(0, depth)], a2a_recv.at[step])
            return carry

        lax.fori_loop(1, count, spread_wait, 0)
        keep_tail.wait()
        total = jnp.zeros((share, vocab), jnp.float32)
        for way in range(ways):
            total += lax.dot_general(
                tail_all[:, :, way * width : (way + 1) * width].reshape(share, width),
                w[1 + way // 2, way % 2, 0:vocab],
                (((1,), (1,)), ((), ())),
                preferred_element_type=jnp.float32,
            )
        for stream in range(3):
            part[stream] = total[stream * wide : (stream + 1) * wide].astype(jnp.bfloat16)

        def slot(owner, part_of):
            at, some = owner * wide, wide
            if part_of is not None:
                some = wide // 2
                at = at + part_of * some
            return w.at[0, :, pl.ds(pl.multiple_of(at, some), some), 0:vocab]

        spread_table = Gather(slot, part, send, recv, side_send, side_recv)
        spread_table.run(local.at[0])
        load_weight.wait()

        @pl.when(seq > 0)
        def _():
            ids_on.wait_recv()

        onehot = w.at[3, 0, 0 : 2 * length, 0:vocab]

        def streams(mb):
            for part_at in range(vocab // lane):
                number = lax.broadcasted_iota(jnp.int32, (2 * length, lane), 1) + part_at * lane
                hit = jnp.where(ids_all[mb] == number, 1.0, 0.0).astype(jnp.bfloat16)
                w[3, 0, 0 : 2 * length, part_at * lane : (part_at + 1) * lane] = hit

            def one_block(at, carry):
                stream, inner = at // (width // block), at % (width // block)
                columns = pl.ds(pl.multiple_of(inner * block, block), block)
                values = lax.dot_general(
                    onehot[...],
                    w[0, stream, columns, 0:vocab],
                    (((1,), (1,)), ((), ())),
                    preferred_element_type=jnp.float32,
                ).astype(jnp.bfloat16).astype(jnp.float32)
                for side in range(block // lane):
                    sf[stream, inner * (block // lane) + side, 8 : 8 + 2 * length, :] = values[
                        :, side * lane : (side + 1) * lane
                    ]
                return carry

            lax.fori_loop(0, 3 * width // block, one_block, 0)

        def shorts_of(mb):
            def own_rows(at, carry):
                columns = pl.ds(pl.multiple_of(at * block, block), block)
                values = jnp.dot(
                    onehot[...], table[:, columns], preferred_element_type=jnp.float32
                )
                base[mb * pitch : mb * pitch + length, columns] = values[length : 2 * length]
                return carry

            lax.fori_loop(0, width // block, own_rows, 0)

            def one_tile(tile, carry):
                query[mb, tile] = short(tile, 0, 8 + length, length)
                gate(mb, tile, 8, length, 0)
                gate(mb, tile, 8 + length, length, length)
                return carry

            lax.fori_loop(0, tiles, one_tile, 0)

        sf[:, :, 0:8, :] = jnp.zeros((3, tiles, 8, lane), jnp.float32)
        def pass_on(chunk):
            reduce_end(fine[chunk])
            relay(chunk).start()

        streams(0)
        shorts_of(0)
        medium(0, 0, 64)
        reduce_start(fine[0])
        medium(0, 64, length - 64)
        reduce_start(fine[1])
        reduce_middle(fine[0])
        streams(1)
        reduce_middle(fine[1])
        pass_on(0)
        shorts_of(1)
        pass_on(1)
        medium(1, 0, 80)
        reduce_start(fine[2])
        medium(1, 80, length - 80)
        reduce_middle(fine[2])
        reduce_start(fine[3])
        reduce_middle(fine[3])
        pass_on(2)
        pass_on(3)
        reduce_close(fine)
        spread_table.close()
        for chunk in range(len(chunks)):
            relay(chunk).wait_send()

        @pl.when(seq < count - 1)
        def _():
            ids_on.wait_send()

    @pl.when(section == 1)
    def _():
        greet(seq=seq_of(y, (z + 1) % RING, core))
        greet(seq=seq_of(y, (z + RING - 1) % RING, core))
        greet(seq=seq_of(1 - y, z, core))
        greet(seq=seq_of(y, z, 1 - core))
        greet(tensor=ahead)
        greet(tensor=behind)
        greet(section=0)

        @pl.when(seq > 0)
        def _():
            greet(seq=(seq + count - 1) % count)

        @pl.when(seq < count - 1)
        def _():
            pl.semaphore_wait(barrier, 7)

        @pl.when(seq == count - 1)
        def _():
            pl.semaphore_wait(barrier, 6)

        load_weight.start()
        per = width // depth

        def slot(owner, part_of):
            at, some = (owner % per) * depth, depth
            if part_of is not None:
                some = depth // 2
                at = at + part_of * some
            return w.at[owner // per, :, pl.ds(pl.multiple_of(at, some), some)]

        def share_out(chunk, at, owner, to):
            first, rows = chunks[chunk]
            piece = xs.at[owner, first : first + rows]
            return remote(
                piece, piece, ag_send.at[chunk * 3 + at], ag_recv.at[chunk * 3 + at], tensor=to
            )

        def gather_start(chunk):
            first, rows = chunks[chunk]
            arrival(xs.at[tensor, first : first + rows], relay_recv.at[chunk])
            share_out(chunk, 0, tensor, ahead).start()
            share_out(chunk, 1, tensor, behind).start()

        def gather_middle(chunk):
            first, rows = chunks[chunk]
            arrival(xs.at[behind, first : first + rows], ag_recv.at[chunk * 3])
            share_out(chunk, 2, behind, ahead).start()

        def gather_end(chunk):
            first, rows = chunks[chunk]
            arrival(xs.at[ahead, first : first + rows], ag_recv.at[chunk * 3 + 1])
            arrival(xs.at[far, first : first + rows], ag_recv.at[chunk * 3 + 2])

        def gather_close():
            for chunk in range(len(chunks)):
                share_out(chunk, 0, tensor, ahead).wait_send()
                share_out(chunk, 1, tensor, behind).wait_send()
                share_out(chunk, 2, behind, ahead).wait_send()

        def project(group):
            first, rows = group * pitch, pitch
            lines = 16

            def normalise(at, carry):
                window = pl.ds(pl.multiple_of(first + at * lines, lines), lines)
                total = jnp.zeros((lines, 1), jnp.float32)
                for way in range(ways):
                    values = xs[way, window].astype(jnp.float32)
                    total += jnp.sum(values * values, axis=1, keepdims=True)
                scale = lax.rsqrt(total / (ways * width) + EPS)
                for way in range(ways):
                    values = xs[way, window].astype(jnp.float32)
                    values = values * scale * gain[:, way * width : (way + 1) * width]
                    xn[way, window] = values.astype(jnp.bfloat16)
                base[window] = xs[tensor, window].astype(jnp.float32)
                return carry

            lax.fori_loop(0, rows // lines, normalise, 0)

            def one_block(at, carry):
                stream, inner = at // (width // block), at % (width // block)
                columns = pl.ds(pl.multiple_of(inner * block, block), block)
                total = jnp.zeros((rows, block), jnp.float32)
                for way in range(ways):
                    total += jnp.dot(
                        xn[way, first : first + rows],
                        w[way, stream, :, columns],
                        preferred_element_type=jnp.float32,
                    )
                total = total.astype(jnp.bfloat16).astype(jnp.float32)
                for side in range(block // lane):
                    tile = inner * (block // lane) + side
                    piece = total[:, side * lane : (side + 1) * lane]
                    sf[stream, tile, first + 8 : first + 8 + length, :] = piece[0:length]
                return carry

            lax.fori_loop(0, 3 * width // block, one_block, 0)

        def rim(mb):
            return remote(
                rim_send.at[mb], rim_recv.at[mb], halo_send.at[mb], halo_recv.at[mb],
                seq=(seq + 1) % count,
            )

        def gated_rim(mb):
            return remote(
                far_send.at[mb], far_recv.at[mb], halo_send.at[micro + mb], halo_recv.at[micro + mb],
                seq=(seq + 1) % count,
            )

        def rim_start(mb):
            last = (mb + 1) * pitch
            rim_send[mb] = sf[:, :, last - 16 : last, :].astype(jnp.bfloat16)

            @pl.when(seq < count - 1)
            def _():
                rim(mb).start()

        def shorts(mb):
            first = mb * pitch

            def one_gate(tile, carry):
                gate(mb, tile, first + 16, length - 8, length + 8)
                far_send[mb, tile] = gf[mb, tile, 2 * length - taps : 2 * length, :].astype(
                    jnp.bfloat16
                )
                return carry

            lax.fori_loop(0, tiles, one_gate, 0)

            @pl.when(seq < count - 1)
            def _():
                gated_rim(mb).start()

            @pl.when(seq > 0)
            def _():
                rim(mb).wait_recv()
                sf[:, :, first : first + 8, :] = rim_recv[mb].astype(jnp.float32)[:, :, 8:16]

            @pl.when(seq == 0)
            def _():
                sf[:, :, first : first + 8, :] = jnp.zeros((3, tiles, 8, lane), jnp.float32)

            def one_tile(tile, carry):
                gate(mb, tile, first + 8, 8, length)
                query[mb, tile] = short(tile, 0, first + 8, length)
                return carry

            lax.fori_loop(0, tiles, one_tile, 0)

        def gated_end(mb):
            @pl.when(seq > 0)
            def _():
                gated_rim(mb).wait_recv()

                def one_tile(tile, carry):
                    gf[mb, tile, length - taps : length, :] = far_recv[mb, tile].astype(
                        jnp.float32
                    )
                    return carry

                lax.fori_loop(0, tiles, one_tile, 0)

            @pl.when(seq == 0)
            def _():
                gf[mb, :, 0:length, :] = jnp.zeros((tiles, length, lane), jnp.float32)

        def early():
            gather_start(0)
            gather_middle(0)
            gather_start(1)

        def later():
            gather_middle(1)

        spread_weight = Gather(slot, shard, send, recv, side_send, side_recv)
        spread_weight.run(local.at[0], early, later)
        load_weight.wait()
        gather_end(0)
        gather_end(1)
        project(0)
        rim_start(0)
        gather_start(2)
        shorts(0)
        gather_middle(2)
        gather_start(3)
        spread_weight.close()
        gated_end(0)
        medium(0, 0, 64)
        gather_middle(3)
        medium(0, 64, length - 64)
        reduce_start(coarse[0])
        gather_end(2)
        gather_end(3)
        project(1)
        rim_start(1)
        reduce_middle(coarse[0])
        shorts(1)
        gated_end(1)
        medium(1, 0, 80)
        reduce_start(coarse[1])
        medium(1, 80, length - 80)
        reduce_middle(coarse[1])
        reduce_start(coarse[2])
        reduce_middle(coarse[2])
        gather_close()
        reduce_end(coarse[0])
        reduce_end(coarse[1])
        reduce_end(coarse[2])
        reduce_close(coarse)

        @pl.when(seq < count - 1)
        def _():
            for mb in range(micro):
                rim(mb).wait_send()
                gated_rim(mb).wait_send()


def body(token_ids, embed_table, norm_gain, in_weight, se_filter, mr_filter, out_weight):
    micro, length = token_ids.shape
    vocab, width = embed_table.shape
    full = norm_gain.shape[1]
    count = lax.axis_size("seq")
    ways = full // width
    lane = 128
    tiles = width // lane
    rows = micro * (length + 8)
    taps = mr_filter.shape[1]
    depth = in_weight.shape[1]
    wide = width // count
    shard = in_weight[0].transpose(1, 0, 2)
    moves = Gather.COUNT
    bf16, f32 = jnp.bfloat16, jnp.float32
    scratch, dma = pltpu.VMEM, pltpu.SemaphoreType.DMA
    result = pl.pallas_call(
        mixer_kernel,
        out_shape=jax.ShapeDtypeStruct((rows, width), bf16),
        in_specs=[VMEM, HBM, VMEM, VMEM, VMEM, VMEM, HBM],
        out_specs=VMEM,
        scratch_shapes=[
            scratch((ways, 3, width, width), bf16),
            scratch((width, full), bf16),
            scratch((3, wide, full), bf16),
            scratch((3, wide, vocab), bf16),
            scratch((micro, 2 * length, lane), jnp.int32),
            scratch((3, tiles, 2 * length + 16, lane), f32),
            scratch((micro, tiles, 2 * length, lane), f32),
            scratch((micro, tiles, length, lane), f32),
            scratch((rows, width), f32),
            scratch((rows, width), bf16),
            scratch((3, rows, width), bf16),
            scratch((3, rows, width), bf16),
            scratch((rows, width), f32),
            scratch((rows, width), f32),
            scratch((ways, rows, width), bf16),
            scratch((ways, rows, width), bf16),
            scratch((micro, 3, tiles, 16, lane), bf16),
            scratch((micro, 3, tiles, 16, lane), bf16),
            scratch((micro, tiles, taps, lane), bf16),
            scratch((micro, tiles, taps, lane), bf16),
            dma((moves,)),
            dma((moves,)),
            dma((moves + 1,)),
            dma((moves + 1,)),
            dma((count,)),
            dma((count,)),
            dma((6,)),
            dma((6,)),
            dma((12,)),
            dma((12,)),
            dma((12,)),
            dma((12,)),
            dma((4,)),
            dma((4,)),
            dma((2 * micro,)),
            dma((2 * micro,)),
            dma((3,)),
        ],
        compiler_params=pltpu.CompilerParams(
            collective_id=0, has_side_effects=True, vmem_limit_bytes=60 << 20
        ),
        name="mixer",
    )(token_ids, shard, embed_table, norm_gain, se_filter[0][:, :, None], mr_filter[0], out_weight[0])
    return result.reshape(1, micro, length + 8, width)[:, :, :length]


def solution(mesh):
    in_specs = (
        P(None, "seq"),
        P(None, "tensor"),
        P("section", None),
        P("section", "seq", None, "tensor"),
        P("section", None, None, "tensor"),
        P("section", None, "tensor"),
        P("section", "tensor", None),
    )
    out_specs = P("section", None, "seq", "tensor")
    return jax.shard_map(body, mesh=mesh, in_specs=in_specs, out_specs=out_specs, check_vma=False)
```

```python
import functools

import jax
import jax.numpy as jnp
from jax import lax
from jax.experimental import pallas as pl
from jax.experimental.pallas import tpu as pltpu
from jax.sharding import PartitionSpec as P

EPS = 1e-06
MESH = pl.DeviceIdType.MESH
RING = 8
VMEM = pl.BlockSpec(memory_space=pltpu.VMEM)
HBM = pl.BlockSpec(memory_space=pltpu.HBM)


def place():
    seq = lax.axis_index("seq")
    return seq // (2 * RING), (seq // 2) % RING, seq % 2


def seq_of(y, z, core):
    return (y * RING + z) * 2 + core


class Gather:
    MOVES = (
        ("a1", "up", True, 0, None),
        ("b1", "down", True, 0, None),
        ("c1", "y", True, 0, None),
        ("a2", "up", True, -1, None),
        ("b2", "down", True, 1, None),
        ("c2", "y", True, -1, 1),
        ("c3", "y", True, 1, 0),
        ("a3", "up", True, -2, None),
        ("b3", "down", True, 2, None),
        ("c4", "y", True, -2, 1),
        ("c5", "y", True, 2, 0),
        ("a4", "up", True, -3, 0),
        ("b4", "down", True, 3, 1),
        ("c6", "y", True, -3, 0),
        ("c7", "y", True, 3, 1),
        ("a5", "up", False, 0, 0),
        ("b5", "down", False, 0, 1),
        ("c8", "y", True, -3, 1),
        ("c9", "y", True, 3, 0),
        ("a6", "up", False, -1, 0),
        ("b6", "down", False, 1, 1),
        ("a7", "up", False, -3, 0),
        ("b7", "down", False, 3, 1),
    )
    COUNT = len(MOVES)

    def __init__(self, slot, own, send, recv, side_send, side_recv):
        self.y, self.z, self.core = place()
        self.slot, self.own = slot, own
        self.send, self.recv = send, recv
        self.side_send, self.side_recv = side_send, side_recv
        self.index = {move[0]: at for at, move in enumerate(self.MOVES)}
        self.pending = []

    def target(self, direction):
        if direction == "up":
            return seq_of(self.y, (self.z + 1) % RING, self.core)
        if direction == "down":
            return seq_of(self.y, (self.z + RING - 1) % RING, self.core)
        return seq_of(1 - self.y, self.z, self.core)

    def block(self, same, dz, core=None):
        y = self.y if same else 1 - self.y
        return seq_of(y, (self.z + dz + RING) % RING, self.core if core is None else core)

    def copy(self, name):
        at = self.index[name]
        _, direction, same, dz, half = self.MOVES[at]
        block = self.block(same, dz)
        dst = self.slot(block, half)
        src = self.own if same and dz == 0 else dst
        return pltpu.make_async_remote_copy(
            src_ref=src,
            dst_ref=dst,
            send_sem=self.send.at[at],
            recv_sem=self.recv.at[at],
            device_id={"seq": self.target(direction)},
            device_id_type=MESH,
        )

    def start(self, *names):
        for name in names:
            self.copy(name).start()

    def landed(self, name):
        at = self.index[name]
        _, direction, same, dz, half = self.MOVES[at]
        if direction == "y":
            block = self.block(not same, dz)
        else:
            block = self.block(same, dz + (-1 if direction == "up" else 1))
        got = self.slot(block, half)
        pltpu.make_async_copy(got, got, self.recv.at[at]).wait()
        side = pltpu.make_async_remote_copy(
            src_ref=got,
            dst_ref=got,
            send_sem=self.side_send.at[at],
            recv_sem=self.side_recv.at[at],
            device_id={"seq": seq_of(self.y, self.z, 1 - self.core)},
            device_id_type=MESH,
        )
        side.start()

    def side_own(self):
        return pltpu.make_async_remote_copy(
            src_ref=self.own,
            dst_ref=self.slot(self.block(True, 0), None),
            send_sem=self.side_send.at[self.COUNT],
            recv_sem=self.side_recv.at[self.COUNT],
            device_id={"seq": seq_of(self.y, self.z, 1 - self.core)},
            device_id_type=MESH,
        )

    def run(self, local_sem, late=None, last=None):
        keep = pltpu.make_async_copy(self.own, self.slot(self.block(True, 0), None), local_sem)
        self.start("a1", "b1", "c1")
        self.side_own().start()
        keep.start()
        self.landed("a1")
        self.start("a2", "c2")
        self.landed("b1")
        self.start("b2", "c3")
        self.landed("c1")
        self.landed("a2")
        self.start("a3", "c4")
        self.landed("b2")
        self.start("b3", "c5")
        self.landed("c2")
        self.landed("c3")
        self.landed("a3")
        self.start("a4", "c6", "a5")
        self.landed("b3")
        self.start("b4", "c7", "b5")
        for name in ("c4", "c5", "a4", "b4"):
            self.landed(name)
        self.start("c8", "c9")
        self.landed("a5")
        self.start("a6")
        self.landed("b5")
        self.start("b6")
        self.landed("c6")
        self.start("a7")
        self.landed("c7")
        self.start("b7")
        self.landed("a6")
        self.landed("b6")
        if late is not None:
            late()
        self.landed("c8")
        self.landed("c9")
        if last is not None:
            last()
        self.landed("a7")
        self.landed("b7")
        keep.wait()
        for at, (name, direction, same, dz, half) in enumerate(self.MOVES):
            other = self.slot(self.block(*self.came(at), 1 - self.core), half)
            pltpu.make_async_copy(other, other, self.side_recv.at[at]).wait()
        other = self.slot(self.block(True, 0, 1 - self.core), None)
        pltpu.make_async_copy(other, other, self.side_recv.at[self.COUNT]).wait()

    def came(self, at):
        _, direction, same, dz, _ = self.MOVES[at]
        if direction == "y":
            return not same, dz
        return same, dz + (-1 if direction == "up" else 1)

    def close(self):
        for at, (name, direction, same, dz, half) in enumerate(self.MOVES):
            self.copy(name).wait_send()
            mine = self.slot(self.block(*self.came(at)), half)
            pltpu.make_async_copy(mine, mine, self.side_send.at[at]).wait()
        self.side_own().wait_send()


def mixer_kernel(
    ids, shard, table, gain, se, mr, weight_hbm, out,
    w, weight, tail_all, part, ids_all, sf, gf, query, mixf, mixed, send_buf, recv_buf, own_part, base, xs, xn,
    rim_send, rim_recv, far_send, far_recv,
    send, recv, side_send, side_recv, a2a_send, a2a_recv, x_send, x_recv,
    rs_send, rs_recv, ag_send, ag_recv, relay_send, relay_recv, halo_send, halo_recv, local,
):
    section = lax.axis_index("section")
    tensor = lax.axis_index("tensor")
    seq = lax.axis_index("seq")
    y, z, core = place()
    depth = shard.shape[1]
    vocab, width = table.shape
    wide = part.shape[1]
    count = width // wide
    share = 3 * wide
    half = vocab // 2
    ways = w.shape[0]
    micro = gf.shape[0]
    tiles = gf.shape[1]
    length = gf.shape[2] // 2
    taps = mr.shape[0]
    short_taps = se.shape[1]
    lane = 128
    block = 512
    broad = 512
    pitch = length + 8
    chunks = ((0, 64), (64, pitch - 64), (pitch, 80), (pitch + 80, pitch - 80))
    fine = tuple((at, *chunk) for at, chunk in enumerate(chunks))
    coarse = ((0, 0, pitch),) + tuple((at - 1, *chunks[at]) for at in (2, 3))
    ahead = (tensor + 1 + core * (ways - 2)) % ways
    behind = (tensor + ways - 1 - core * (ways - 2)) % ways
    far = (tensor + 2) % ways
    barrier = pltpu.get_barrier_semaphore()

    def greet(**axes):
        pl.semaphore_signal(barrier, inc=1, device_id=axes, device_id_type=MESH)

    def remote(src, dst, send_sem, recv_sem, **axes):
        return pltpu.make_async_remote_copy(
            src_ref=src, dst_ref=dst, send_sem=send_sem, recv_sem=recv_sem,
            device_id=axes, device_id_type=MESH,
        )

    def arrival(ref, sem):
        pltpu.make_async_copy(ref, ref, sem).wait()

    def lanes(tile):
        return pl.ds(pl.multiple_of(tile * lane, lane), lane)

    def short(tile, stream, start, rows):
        total = jnp.zeros((rows, lane), jnp.float32)
        for tap in range(short_taps):
            total += se[stream, tap, :, lanes(tile)] * sf[
                stream, tile, start - tap : start - tap + rows, :
            ]
        return total

    def gate(mb, tile, start, rows, at):
        values = short(tile, 1, start, rows) * short(tile, 2, start, rows)
        gf[mb, tile, at : at + rows, :] = values.astype(jnp.bfloat16).astype(jnp.float32)

    def medium(mb, begin, rows):
        def one_tile(tile, carry):
            total = jnp.zeros((rows, lane), jnp.float32)
            first = length + begin - taps
            window = gf[mb, tile, first : first + rows + taps, :]
            for shift in range(8):
                part_sum = jnp.zeros((rows + 8, lane), jnp.float32)
                for step in range(taps // 8):
                    tap = 8 * step + shift
                    at = taps - 8 - 8 * step
                    part_sum += mr[tap : tap + 1, lanes(tile)] * window[at : at + rows + 8]
                total += part_sum[8 - shift : 8 - shift + rows]
            to = mb * pitch + begin
            mixf[to : to + rows, lanes(tile)] = query[mb, tile, begin : begin + rows] * total
            return carry

        lax.fori_loop(0, tiles, one_tile, 0)

    def partial_to(chunk, owner, finish):
        index, first, rows = chunk
        window = slice(first, first + rows)

        def one_block(at, carry):
            inner = pl.ds(pl.multiple_of(at * broad, broad), broad)
            outer = pl.ds(pl.multiple_of(owner * width + at * broad, broad), broad)
            term = jnp.dot(mixed[window], weight[:, outer], preferred_element_type=jnp.float32)
            finish(window, inner, term)
            return carry

        lax.fori_loop(0, width // broad, one_block, 0)

    def hop(chunk, at, to):
        index, first, rows = chunk
        window = slice(first, first + rows)
        return remote(
            send_buf.at[at, window], recv_buf.at[at, window],
            rs_send.at[index * 3 + at], rs_recv.at[index * 3 + at], tensor=to,
        )

    def fill(at):
        def finish(window, inner, term):
            send_buf[at, window, inner] = term.astype(jnp.bfloat16)

        return finish

    def reduce_start(chunk):
        index, first, rows = chunk
        window = slice(first, first + rows)
        mixed[window] = mixf[window].astype(jnp.bfloat16)
        partial_to(chunk, far, fill(0))
        hop(chunk, 0, ahead).start()
        partial_to(chunk, behind, fill(2))
        hop(chunk, 2, behind).start()

        def onward(window, inner, term):
            mixf[window, inner] = term

        def keep(window, inner, term):
            own_part[window, inner] = term

        partial_to(chunk, ahead, onward)
        partial_to(chunk, tensor, keep)

    def reduce_middle(chunk):
        index, first, rows = chunk
        hop(chunk, 0, ahead).wait_recv()
        lines = 16

        def join(at, carry):
            window = pl.ds(pl.multiple_of(first + at * lines, lines), lines)
            both = mixf[window] + recv_buf[0, window].astype(jnp.float32)
            send_buf[1, window] = both.astype(jnp.bfloat16)
            return carry

        lax.fori_loop(0, rows // lines, join, 0)
        hop(chunk, 1, ahead).start()

    def reduce_end(chunk):
        index, first, rows = chunk
        hop(chunk, 2, behind).wait_recv()
        hop(chunk, 1, ahead).wait_recv()
        lines = 16

        def add(at, carry):
            window = pl.ds(pl.multiple_of(first + at * lines, lines), lines)
            total = own_part[window] + recv_buf[1, window].astype(jnp.float32)
            total += recv_buf[2, window].astype(jnp.float32)
            out[window] = (base[window] + total).astype(jnp.bfloat16)
            return carry

        lax.fori_loop(0, rows // lines, add, 0)

    def reduce_close(pieces):
        for chunk in pieces:
            hop(chunk, 0, ahead).wait_send()
            hop(chunk, 1, ahead).wait_send()
            hop(chunk, 2, behind).wait_send()

    def relay(chunk):
        first, rows = chunks[chunk]
        window = slice(first, first + rows)
        return remote(
            out.at[window], xs.at[tensor, window],
            relay_send.at[chunk], relay_recv.at[chunk], section=1,
        )

    load_weight = pltpu.make_async_copy(weight_hbm, weight, local.at[2])

    @pl.when(section == 0)
    def _():
        greet(tensor=ahead)
        greet(tensor=behind)

        def greet_seq(step, carry):
            greet(seq=(seq + step) % count)
            return carry

        load_shard = pltpu.make_async_copy(shard, xn.at[0:3, 0:depth], local.at[0])
        load_shard.start()
        lax.fori_loop(1, count, greet_seq, 0)
        load_shard.wait()
        tail = w.at[3, :, :, vocab : vocab + depth]
        for stream in range(3):
            w[3, stream, :, vocab : vocab + depth] = xn[stream, 0:depth].T
        for mb in range(micro):
            for begin, rows in ((0, lane), (lane, length - lane)):
                line = ids[mb : mb + 1, begin : begin + rows]
                ids_all[mb, length + begin : length + begin + rows] = jnp.broadcast_to(
                    line, (lane, rows)
                ).T
        pl.semaphore_wait(barrier, count + 2)
        load_weight.start()

        ids_on = remote(
            ids_all.at[:, length : 2 * length], ids_all.at[:, 0:length], halo_send.at[0], halo_recv.at[0],
            seq=(seq + 1) % count,
        )

        @pl.when(seq < count - 1)
        def _():
            ids_on.start()

        @pl.when(seq == 0)
        def _():
            ids_all[:, 0:length] = jnp.full((micro, length, lane), -1, jnp.int32)

        rows = pl.ds(pl.multiple_of(core * half, half), half)

        def table_of(owner):
            return w.at[1 + owner // 2, owner % 2, 0:vocab]

        def along(at, src, owner, to):
            return remote(src, table_of(owner).at[rows], x_send.at[at], x_recv.at[at], tensor=to)

        def across(at, owner):
            piece = table_of(owner).at[rows]
            return remote(
                piece, piece, x_send.at[at], x_recv.at[at], seq=seq_of(y, z, 1 - core)
            )

        mine = table.at[rows]
        along(0, mine, tensor, ahead).start()
        along(1, mine, tensor, behind).start()
        keep = pltpu.make_async_copy(table, table_of(tensor), local.at[0])
        keep.start()

        def spread(step):
            to = (seq + step) % count
            return remote(
                tail.at[:, pl.ds(pl.multiple_of(to * wide, wide), wide)],
                tail_all.at[:, :, pl.ds(pl.multiple_of(seq * depth, depth), depth)],
                a2a_send.at[step], a2a_recv.at[step], seq=to,
            )

        def spread_start(step, carry):
            spread(step).start()
            return carry

        lax.fori_loop(1, count, spread_start, 0)
        keep_tail = pltpu.make_async_copy(
            tail.at[:, pl.ds(pl.multiple_of(seq * wide, wide), wide)],
            tail_all.at[:, :, pl.ds(pl.multiple_of(seq * depth, depth), depth)],
            local.at[1],
        )
        keep_tail.start()

        along(0, mine, tensor, ahead).wait_recv()
        along(2, table_of(behind).at[rows], behind, ahead).start()
        across(3, behind).start()
        along(1, mine, tensor, behind).wait_recv()
        across(4, ahead).start()
        got = table_of(far).at[rows]
        arrival(got, x_recv.at[2])
        across(5, far).start()
        keep.wait()
        for at, owner in ((3, behind), (4, ahead), (5, far)):
            across(at, owner).wait_recv()
        along(0, mine, tensor, ahead).wait_send()
        along(1, mine, tensor, behind).wait_send()
        arrival(got, x_send.at[2])
        for at, owner in ((3, behind), (4, ahead), (5, far)):
            across(at, owner).wait_send()

        lines = 32

        def normalise(at, carry):
            window = pl.ds(pl.multiple_of(at * lines, lines), lines)
            total = jnp.zeros((lines, 1), jnp.float32)
            for way in range(ways):
                values = w[1 + way // 2, way % 2, window].astype(jnp.float32)
                total += jnp.sum(values * values, axis=1, keepdims=True)
            scale = lax.rsqrt(total / (ways * width) + EPS)
            for way in range(ways):
                values = w[1 + way // 2, way % 2, window].astype(jnp.float32)
                values = values * scale * gain[:, way * width : (way + 1) * width]
                w[1 + way // 2, way % 2, window] = values.astype(jnp.bfloat16)
            return carry

        lax.fori_loop(0, vocab // lines, normalise, 0)

        def spread_wait(step, carry):
            spread(step).wait_send()
            arrival(tail_all.at[:, :, pl.ds(0, depth)], a2a_recv.at[step])
            return carry

        lax.fori_loop(1, count, spread_wait, 0)
        keep_tail.wait()
        total = jnp.zeros((share, vocab), jnp.float32)
        for way in range(ways):
            total += lax.dot_general(
                tail_all[:, :, way * width : (way + 1) * width].reshape(share, width),
                w[1 + way // 2, way % 2, 0:vocab],
                (((1,), (1,)), ((), ())),
                preferred_element_type=jnp.float32,
            )
        for stream in range(3):
            part[stream] = total[stream * wide : (stream + 1) * wide].astype(jnp.bfloat16)

        def slot(owner, part_of):
            at, some = owner * wide, wide
            if part_of is not None:
                some = wide // 2
                at = at + part_of * some
            return w.at[0, :, pl.ds(pl.multiple_of(at, some), some), 0:vocab]

        spread_table = Gather(slot, part, send, recv, side_send, side_recv)
        spread_table.run(local.at[0])
        load_weight.wait()

        @pl.when(seq > 0)
        def _():
            ids_on.wait_recv()

        onehot = w.at[3, 0, 0 : 2 * length, 0:vocab]

        def streams(mb):
            for part_at in range(vocab // lane):
                number = lax.broadcasted_iota(jnp.int32, (2 * length, lane), 1) + part_at * lane
                hit = jnp.where(ids_all[mb] == number, 1.0, 0.0).astype(jnp.bfloat16)
                w[3, 0, 0 : 2 * length, part_at * lane : (part_at + 1) * lane] = hit

            def one_block(at, carry):
                stream, inner = at // (width // block), at % (width // block)
                columns = pl.ds(pl.multiple_of(inner * block, block), block)
                values = lax.dot_general(
                    onehot[...],
                    w[0, stream, columns, 0:vocab],
                    (((1,), (1,)), ((), ())),
                    preferred_element_type=jnp.float32,
                ).astype(jnp.bfloat16).astype(jnp.float32)
                for side in range(block // lane):
                    sf[stream, inner * (block // lane) + side, 8 : 8 + 2 * length, :] = values[
                        :, side * lane : (side + 1) * lane
                    ]
                return carry

            lax.fori_loop(0, 3 * width // block, one_block, 0)

        def shorts_of(mb):
            def own_rows(at, carry):
                columns = pl.ds(pl.multiple_of(at * block, block), block)
                values = jnp.dot(
                    onehot[...], table[:, columns], preferred_element_type=jnp.float32
                )
                base[mb * pitch : mb * pitch + length, columns] = values[length : 2 * length]
                return carry

            lax.fori_loop(0, width // block, own_rows, 0)

            def one_tile(tile, carry):
                query[mb, tile] = short(tile, 0, 8 + length, length)
                gate(mb, tile, 8, length, 0)
                gate(mb, tile, 8 + length, length, length)
                return carry

            lax.fori_loop(0, tiles, one_tile, 0)

        sf[:, :, 0:8, :] = jnp.zeros((3, tiles, 8, lane), jnp.float32)
        def pass_on(chunk):
            reduce_end(fine[chunk])
            relay(chunk).start()

        streams(0)
        shorts_of(0)
        medium(0, 0, 64)
        reduce_start(fine[0])
        medium(0, 64, length - 64)
        reduce_start(fine[1])
        reduce_middle(fine[0])
        streams(1)
        reduce_middle(fine[1])
        pass_on(0)
        shorts_of(1)
        pass_on(1)
        medium(1, 0, 80)
        reduce_start(fine[2])
        medium(1, 80, length - 80)
        reduce_middle(fine[2])
        reduce_start(fine[3])
        reduce_middle(fine[3])
        pass_on(2)
        pass_on(3)
        reduce_close(fine)
        spread_table.close()
        for chunk in range(len(chunks)):
            relay(chunk).wait_send()

        @pl.when(seq < count - 1)
        def _():
            ids_on.wait_send()

    @pl.when(section == 1)
    def _():
        greet(seq=seq_of(y, (z + 1) % RING, core))
        greet(seq=seq_of(y, (z + RING - 1) % RING, core))
        greet(seq=seq_of(1 - y, z, core))
        greet(seq=seq_of(y, z, 1 - core))
        greet(tensor=ahead)
        greet(tensor=behind)
        greet(section=0)

        @pl.when(seq > 0)
        def _():
            greet(seq=(seq + count - 1) % count)

        @pl.when(seq < count - 1)
        def _():
            pl.semaphore_wait(barrier, 7)

        @pl.when(seq == count - 1)
        def _():
            pl.semaphore_wait(barrier, 6)

        load_weight.start()
        per = width // depth

        def slot(owner, part_of):
            at, some = (owner % per) * depth, depth
            if part_of is not None:
                some = depth // 2
                at = at + part_of * some
            return w.at[owner // per, :, pl.ds(pl.multiple_of(at, some), some)]

        def share_out(chunk, at, owner, to):
            first, rows = chunks[chunk]
            piece = xs.at[owner, first : first + rows]
            return remote(
                piece, piece, ag_send.at[chunk * 3 + at], ag_recv.at[chunk * 3 + at], tensor=to
            )

        def gather_start(chunk):
            first, rows = chunks[chunk]
            arrival(xs.at[tensor, first : first + rows], relay_recv.at[chunk])
            share_out(chunk, 0, tensor, ahead).start()
            share_out(chunk, 1, tensor, behind).start()

        def gather_middle(chunk):
            first, rows = chunks[chunk]
            arrival(xs.at[behind, first : first + rows], ag_recv.at[chunk * 3])
            share_out(chunk, 2, behind, ahead).start()

        def gather_end(chunk):
            first, rows = chunks[chunk]
            arrival(xs.at[ahead, first : first + rows], ag_recv.at[chunk * 3 + 1])
            arrival(xs.at[far, first : first + rows], ag_recv.at[chunk * 3 + 2])

        def gather_close():
            for chunk in range(len(chunks)):
                share_out(chunk, 0, tensor, ahead).wait_send()
                share_out(chunk, 1, tensor, behind).wait_send()
                share_out(chunk, 2, behind, ahead).wait_send()

        def project(group, begin, end):
            first, rows = group * pitch, pitch
            lines = 16

            def normalise(at, carry):
                window = pl.ds(pl.multiple_of(first + at * lines, lines), lines)
                total = jnp.zeros((lines, 1), jnp.float32)
                for way in range(ways):
                    values = xs[way, window].astype(jnp.float32)
                    total += jnp.sum(values * values, axis=1, keepdims=True)
                scale = lax.rsqrt(total / (ways * width) + EPS)
                for way in range(ways):
                    values = xs[way, window].astype(jnp.float32)
                    values = values * scale * gain[:, way * width : (way + 1) * width]
                    xn[way, window] = values.astype(jnp.bfloat16)
                base[window] = xs[tensor, window].astype(jnp.float32)
                return carry

            if begin > 0:
                lax.fori_loop(0, rows // lines, normalise, 0)

            def one_block(at, carry):
                stream, inner = at // (width // block), at % (width // block)
                columns = pl.ds(pl.multiple_of(inner * block, block), block)
                total = jnp.zeros((rows, block), jnp.float32)
                for way in range(ways):
                    total += jnp.dot(
                        xn[way, first : first + rows],
                        w[way, stream, :, columns],
                        preferred_element_type=jnp.float32,
                    )
                total = total.astype(jnp.bfloat16).astype(jnp.float32)
                for side in range(block // lane):
                    tile = inner * (block // lane) + side
                    piece = total[:, side * lane : (side + 1) * lane]
                    sf[stream, tile, first + 8 : first + 8 + length, :] = piece[0:length]
                return carry

            lax.fori_loop(begin, end, one_block, 0)

        third = width // block

        def rim(mb):
            return remote(
                rim_send.at[mb], rim_recv.at[mb], halo_send.at[mb], halo_recv.at[mb],
                seq=(seq + 1) % count,
            )

        def gated_rim(mb):
            return remote(
                far_send.at[mb], far_recv.at[mb], halo_send.at[micro + mb], halo_recv.at[micro + mb],
                seq=(seq + 1) % count,
            )

        def rim_start(mb):
            last = (mb + 1) * pitch
            rim_send[mb] = sf[:, :, last - 16 : last, :].astype(jnp.bfloat16)

            @pl.when(seq < count - 1)
            def _():
                rim(mb).start()

        def shorts(mb):
            first = mb * pitch

            def one_gate(tile, carry):
                gate(mb, tile, first + 16, length - 8, length + 8)
                far_send[mb, tile] = gf[mb, tile, 2 * length - taps : 2 * length, :].astype(
                    jnp.bfloat16
                )
                return carry

            lax.fori_loop(0, tiles, one_gate, 0)

            @pl.when(seq < count - 1)
            def _():
                gated_rim(mb).start()

        def shorts_end(mb):
            first = mb * pitch

            @pl.when(seq > 0)
            def _():
                rim(mb).wait_recv()
                sf[:, :, first : first + 8, :] = rim_recv[mb].astype(jnp.float32)[:, :, 8:16]

            @pl.when(seq == 0)
            def _():
                sf[:, :, first : first + 8, :] = jnp.zeros((3, tiles, 8, lane), jnp.float32)

            def one_tile(tile, carry):
                gate(mb, tile, first + 8, 8, length)
                query[mb, tile] = short(tile, 0, first + 8, length)
                return carry

            lax.fori_loop(0, tiles, one_tile, 0)

        def gated_end(mb):
            @pl.when(seq > 0)
            def _():
                gated_rim(mb).wait_recv()

                def one_tile(tile, carry):
                    gf[mb, tile, length - taps : length, :] = far_recv[mb, tile].astype(
                        jnp.float32
                    )
                    return carry

                lax.fori_loop(0, tiles, one_tile, 0)

            @pl.when(seq == 0)
            def _():
                gf[mb, :, 0:length, :] = jnp.zeros((tiles, length, lane), jnp.float32)

        def early():
            gather_start(0)
            gather_middle(0)
            gather_start(1)

        def later():
            gather_middle(1)

        spread_weight = Gather(slot, shard, send, recv, side_send, side_recv)
        spread_weight.run(local.at[0], early, later)
        load_weight.wait()
        gather_end(0)
        gather_end(1)
        project(0, third, 3 * third)
        shorts(0)
        project(0, 0, third)
        rim_start(0)
        gather_start(2)
        shorts_end(0)
        gather_middle(2)
        gather_start(3)
        spread_weight.close()
        gated_end(0)
        medium(0, 0, 64)
        gather_middle(3)
        medium(0, 64, length - 64)
        reduce_start(coarse[0])
        gather_end(2)
        gather_end(3)
        project(1, third, 3 * third)
        shorts(1)
        project(1, 0, third)
        rim_start(1)
        reduce_middle(coarse[0])
        shorts_end(1)
        gated_end(1)
        medium(1, 0, 80)
        reduce_start(coarse[1])
        medium(1, 80, length - 80)
        reduce_middle(coarse[1])
        reduce_start(coarse[2])
        reduce_middle(coarse[2])
        gather_close()
        reduce_end(coarse[0])
        reduce_end(coarse[1])
        reduce_end(coarse[2])
        reduce_close(coarse)

        @pl.when(seq < count - 1)
        def _():
            for mb in range(micro):
                rim(mb).wait_send()
                gated_rim(mb).wait_send()


def body(token_ids, embed_table, norm_gain, in_weight, se_filter, mr_filter, out_weight):
    micro, length = token_ids.shape
    vocab, width = embed_table.shape
    full = norm_gain.shape[1]
    count = lax.axis_size("seq")
    ways = full // width
    lane = 128
    tiles = width // lane
    rows = micro * (length + 8)
    taps = mr_filter.shape[1]
    depth = in_weight.shape[1]
    wide = width // count
    shard = in_weight[0].transpose(1, 0, 2)
    moves = Gather.COUNT
    bf16, f32 = jnp.bfloat16, jnp.float32
    scratch, dma = pltpu.VMEM, pltpu.SemaphoreType.DMA
    result = pl.pallas_call(
        mixer_kernel,
        out_shape=jax.ShapeDtypeStruct((rows, width), bf16),
        in_specs=[VMEM, HBM, VMEM, VMEM, VMEM, VMEM, HBM],
        out_specs=VMEM,
        scratch_shapes=[
            scratch((ways, 3, width, width), bf16),
            scratch((width, full), bf16),
            scratch((3, wide, full), bf16),
            scratch((3, wide, vocab), bf16),
            scratch((micro, 2 * length, lane), jnp.int32),
            scratch((3, tiles, 2 * length + 16, lane), f32),
            scratch((micro, tiles, 2 * length, lane), f32),
            scratch((micro, tiles, length, lane), f32),
            scratch((rows, width), f32),
            scratch((rows, width), bf16),
            scratch((3, rows, width), bf16),
            scratch((3, rows, width), bf16),
            scratch((rows, width), f32),
            scratch((rows, width), f32),
            scratch((ways, rows, width), bf16),
            scratch((ways, rows, width), bf16),
            scratch((micro, 3, tiles, 16, lane), bf16),
            scratch((micro, 3, tiles, 16, lane), bf16),
            scratch((micro, tiles, taps, lane), bf16),
            scratch((micro, tiles, taps, lane), bf16),
            dma((moves,)),
            dma((moves,)),
            dma((moves + 1,)),
            dma((moves + 1,)),
            dma((count,)),
            dma((count,)),
            dma((6,)),
            dma((6,)),
            dma((12,)),
            dma((12,)),
            dma((12,)),
            dma((12,)),
            dma((4,)),
            dma((4,)),
            dma((2 * micro,)),
            dma((2 * micro,)),
            dma((3,)),
        ],
        compiler_params=pltpu.CompilerParams(
            collective_id=0, has_side_effects=True, vmem_limit_bytes=60 << 20
        ),
        name="mixer",
    )(token_ids, shard, embed_table, norm_gain, se_filter[0][:, :, None], mr_filter[0], out_weight[0])
    return result.reshape(1, micro, length + 8, width)[:, :, :length]


def solution(mesh):
    in_specs = (
        P(None, "seq"),
        P(None, "tensor"),
        P("section", None),
        P("section", "seq", None, "tensor"),
        P("section", None, None, "tensor"),
        P("section", None, "tensor"),
        P("section", "tensor", None),
    )
    out_specs = P("section", None, "seq", "tensor")
    return jax.shard_map(body, mesh=mesh, in_specs=in_specs, out_specs=out_specs, check_vma=False)
```
